128 devices in a mesh: cp: 64 (over z, x, y), dp: 2 (over core).
Axes of the slice: x: 4, y: 4, z: 4, core: 2. Of those that a mesh axis runs over, the one named last changes fastest.
Arguments:
- frame_rows: bfloat16 [192, 256, 8, 512], P('dp', 'cp'), parts along dimension 0, may hold values from -6 to 6
- frame_counts: int32 [32], P('dp'), parts along dimension 0, may hold values from 1 to 6, 64 in all
- conv_weight: bfloat16 [3, 3, 512, 512], replicated, may hold values from -0.09375 to 0.09375
- norm_gain: float32 [512], replicated, may hold values from 0.25 to 1.75
- latent_proj: bfloat16 [512, 16], replicated, may hold values from -0.25 to 0.25
- patch_weight: bfloat16 [64, 3072], replicated, may hold values from -0.75 to 0.75
- frame_embed: bfloat16 [6, 3072], replicated, may hold values from -5 to 5
- query_gain: float32 [3072], replicated, may hold values from 0.25 to 1.75
- query_weight: bfloat16 [3072, 3072], P(None, 'cp'), may hold values from -0.109375 to 0.109375
Outputs:
- queries: bfloat16 [24, 65536, 128], P(None, ('dp', 'cp')), parts along dimension 1
The draws below stay inside these ranges and needn't reach their ends.
There are 2 independent parts, one for each index of `dp`. The reference program is written for one: setup_inputs(seed, part) draws one part's arguments, and reference() takes and returns one part's arrays. A program takes and returns all parts, laid end to end along the dimension named above; an argument that names none is the same for every part. Nothing has to cross between parts.
Inputs may be any that keep to these rules, and one draw needn't show every extreme that they name: `frame_counts`: the counts sum to 64 and some clip has exactly 6 frames.
All inputs are finite; a program needn't handle non-finite values.
Results may differ from the reference program's by a relative error of at most 0.0061.
Values may be sent and summed in bfloat16 or wider, within the bound.
No kernel may reach another device: no remote copies, remote signals or barrier semaphores. Data moves between devices by JAX's collectives and lax.ppermute only.
A program may use at most 192 MiB of HBM per device.

```python
import math
import jax
import jax.numpy as jnp
import numpy as np
from jax import lax

C = 512
LAT = 16
HID = 3072
HEAD_DIM = 128
WIDTH = 8
MAXF = 6
ROWS = 256
HEADS = 24
TOK_DEV = 512
FRAMES = 64
CLIPS = 16
SLOTS = 96
SEQ = 32768


def level_of(stream_key, dims, cuts, smallest, top_value):
    def one(dim, shards_of):
        heights = jax.random.uniform(jax.random.fold_in(jax.random.fold_in(stream_key, 6), dim), (shards_of,), jnp.float32, smallest / len(cuts), top_value / len(cuts))
        return jnp.repeat(jnp.exp(heights), dims[dim] // shards_of).reshape((-1,) + (1,) * (len(dims) - dim - 1))

    loudness = one(*cuts[0])
    for cut in cuts[1:]:
        loudness = loudness * one(*cut)
    return loudness


def length_profile(number_of, total, most, lean):
    portions = [(1 << 20) // math.isqrt(grade ** lean) + 1 for grade in range(2, number_of + 1)]
    rest, holding = total - most - (number_of - 1), [1] * (number_of - 1)
    while rest > 0:
        free = [i for i in range(number_of - 1) if holding[i] < most]
        pool, budget = sum([portions[i] for i in free]), rest
        for i in free:
            more = min(most - holding[i], max(1, budget * portions[i] // pool), rest)
            holding[i] = holding[i] + more
            rest = rest - more
    return np.array([most] + holding)


def uneven(key, amount, total, limit, lean):
    if amount == 2:
        one = jax.random.randint(key, (), max(1, total - limit), min(limit, total - 1) + 1)
        return jnp.stack([one, total - one])
    sizes = jnp.asarray(length_profile(amount, total, limit, lean), jnp.int32)
    pairs = (amount - 1) // 2
    donor, taker = sizes[1:1 + 2 * pairs:2], sizes[2:2 + 2 * pairs:2]
    room = jnp.minimum(donor - 1, limit - taker)
    shifted = jax.random.randint(jax.random.fold_in(key, 1), (pairs,), 0, 1 << 20) % (room + 1)
    sizes = sizes.at[1:1 + 2 * pairs:2].set(donor - shifted).at[2:2 + 2 * pairs:2].set(taker + shifted)
    return sizes[jax.random.permutation(jax.random.fold_in(key, 2), amount)]


def normal_values(own_key, dims, deviation, reach, split=(), kind=jnp.bfloat16):
    array = jax.random.normal(own_key, dims, jnp.float32) * deviation
    if len(split) > 0:
        array = level_of(own_key, dims, split, -0.22, 0.18) * array
    return jnp.clip(array, min=-reach, max=reach).astype(kind)


def setup_inputs(seed: int = 0, part: int = 0) -> dict:
    key_of = jax.random.split(jax.random.key(seed), 10)
    part_splits = jax.random.split(jax.random.fold_in(key_of[9], part), 10)
    frame_rows = normal_values(part_splits[0], (SLOTS, ROWS, WIDTH, C), 1.0, 6.0, ((1, 64),))
    frame_counts = uneven(part_splits[1], CLIPS, FRAMES, MAXF, 2).astype(jnp.int32)
    conv_weight = normal_values(key_of[2], (3, 3, C, C), (9 * C) ** -0.5, 0.09375)
    norm_gain = jnp.clip(1.0 + 0.15 * jax.random.normal(key_of[3], (C,), jnp.float32), 0.25, 1.75)
    latent_proj = normal_values(key_of[4], (C, LAT), C ** -0.5, 0.25)
    patch_weight = normal_values(key_of[5], (4 * LAT, HID), (4 * LAT) ** -0.5, 0.75)
    frame_embed = normal_values(key_of[6], (MAXF, HID), 1.0, 5.0)
    query_gain = jnp.clip(1.0 + 0.15 * jax.random.normal(key_of[7], (HID,), jnp.float32), 0.25, 1.75)
    query_weight = normal_values(key_of[8], (HID, HID), HID ** -0.5, 0.109375, ((1, 64),))
    return dict(frame_rows=frame_rows, frame_counts=frame_counts, conv_weight=conv_weight, norm_gain=norm_gain, latent_proj=latent_proj, patch_weight=patch_weight, frame_embed=frame_embed, query_gain=query_gain, query_weight=query_weight)


EPSILON = 1e-06

def rms_scale(values, gain):
    return values * lax.rsqrt(lax.optimization_barrier(jnp.mean(values * values, axis=-1, keepdims=True)) + EPSILON) * gain

def reference(frame_rows, frame_counts, conv_weight, norm_gain, latent_proj, patch_weight, frame_embed, query_gain, query_weight):
    counts = frame_counts.astype(jnp.int32)
    clip_ends = jnp.cumsum(counts).astype(jnp.int32)
    clip_starts = clip_ends - counts
    packed_index = jnp.arange(FRAMES, dtype=jnp.int32)
    clip_index = lax.optimization_barrier(jnp.sum((clip_ends[None, :] <= packed_index[:, None]).astype(jnp.int32), axis=1))
    selector = clip_index[:, None] == jnp.arange(CLIPS, dtype=jnp.int32)[None, :]
    first_frame = lax.optimization_barrier(jnp.sum(jnp.where(selector, clip_starts[None, :], 0), axis=1)).astype(jnp.int32)
    frame_offset = (packed_index - first_frame).astype(jnp.int32)
    slot_index = (clip_index * MAXF + frame_offset).astype(jnp.int32)

    def encode_frame(slot_number):
        zero_index = jnp.zeros((), jnp.int32)
        single_frame = lax.dynamic_slice(frame_rows, (slot_number.astype(jnp.int32), zero_index, zero_index, zero_index), (1, ROWS, WIDTH, C))[0]
        summed = lax.conv_general_dilated(single_frame[None], conv_weight, (1, 1), ((1, 1), (1, 1)), dimension_numbers=('NHWC', 'HWIO', 'NHWC'), preferred_element_type=jnp.float32)[0]
        residual = single_frame.astype(jnp.float32) + jax.nn.silu(summed)
        normed = rms_scale(residual, norm_gain.astype(jnp.float32)).astype(jnp.bfloat16)
        latent = jnp.dot(normed.reshape(-1, C), latent_proj, preferred_element_type=jnp.float32).astype(jnp.bfloat16)
        tokens = latent.reshape(ROWS // 2, 2, WIDTH // 2, 2, LAT).transpose(0, 2, 1, 3, 4).reshape(TOK_DEV, 4 * LAT)
        return jnp.dot(tokens, patch_weight, preferred_element_type=jnp.float32).astype(jnp.bfloat16)
    embedded = lax.map(encode_frame, slot_index)
    picker = frame_offset[:, None] == jnp.arange(MAXF, dtype=jnp.int32)[None, :]
    position = lax.optimization_barrier(jnp.sum(jnp.where(picker[:, :, None], frame_embed.astype(jnp.float32)[None, :, :], 0.0), axis=1))
    with_position = embedded.astype(jnp.float32) + position[:, None, :]
    normalized = rms_scale(with_position, query_gain.astype(jnp.float32)).astype(jnp.bfloat16).reshape(SEQ, HID)
    projected = jnp.dot(normalized, query_weight, preferred_element_type=jnp.float32).astype(jnp.bfloat16)
    return projected.reshape(SEQ, HEADS, HEAD_DIM).transpose(1, 0, 2)
```

```python
import jax
import jax.numpy as jnp
from jax import lax
from jax.sharding import PartitionSpec as P

LAT = 16
HID = 3072
HEAD_DIM = 128
MAXF = 6
EPSILON = 1e-06
BF = jnp.bfloat16
F32 = jnp.float32


def split(value):
    high = lax.reduce_precision(value, 8, 7)
    return high.astype(BF), (value - high).astype(BF)


def local(
    frame_rows,
    frame_counts,
    conv_weight,
    norm_gain,
    latent_proj,
    patch_weight,
    frame_embed,
    query_gain,
    query_weight,
):
    devices = lax.axis_size("cp")
    own_index = lax.axis_index("cp")
    clip_count = frame_counts.shape[0]
    clip_ends = jnp.cumsum(frame_counts)
    clip_starts = clip_ends - frame_counts
    packed_index = jnp.arange(devices, dtype=jnp.int32)
    clip_index = jnp.sum((clip_ends[None, :] <= packed_index[:, None]).astype(jnp.int32), axis=1)
    selector = clip_index[:, None] == jnp.arange(clip_count, dtype=jnp.int32)[None, :]
    first_frame = jnp.sum(jnp.where(selector, clip_starts[None, :], 0), axis=1)
    frame_offset = packed_index - first_frame
    slot_index = clip_index * MAXF + frame_offset

    table = jnp.concatenate([patch_weight, frame_embed], axis=0).astype(F32) * query_gain[None, :]
    high, low = split(table)
    dims = (((0,), (1,)), ((), ()))
    folded = lax.dot_general(query_weight, high, dims, preferred_element_type=F32)
    folded = folded + lax.dot_general(query_weight, low, dims, preferred_element_type=F32)
    folded = lax.all_gather(folded.astype(BF), "cp", axis=0, tiled=True)

    frames = jnp.take(frame_rows, slot_index, axis=0)
    up = [(i, i + 1) for i in range(devices - 1)]
    down = [(j, i) for i, j in up]
    before = lax.ppermute(frames[:, 3:4], "cp", up)
    after = lax.ppermute(frames[:, 0:1], "cp", down)
    padded = jnp.concatenate([before, frames, after], axis=1)
    summed = lax.conv_general_dilated(
        padded, conv_weight, (1, 1), ((0, 0), (1, 1)),
        dimension_numbers=("NHWC", "HWIO", "NHWC"), preferred_element_type=F32,
    )
    residual = frames.astype(F32) + jax.nn.silu(summed)
    normed = residual * lax.rsqrt(jnp.mean(residual * residual, axis=-1, keepdims=True) + EPSILON) * norm_gain
    latent = jnp.einsum(
        "sijc,cl->sijl", normed.astype(BF), latent_proj, preferred_element_type=F32
    ).astype(BF)
    tokens = (
        latent.reshape(devices, 2, 2, 4, 2, LAT)
        .transpose(0, 1, 3, 2, 4, 5)
        .reshape(devices, 4, 128)
    )
    arrived = lax.all_to_all(tokens, "cp", split_axis=0, concat_axis=0, tiled=True)
    tokens = arrived.reshape(-1, 4 * LAT)

    own_offset = jnp.sum(jnp.where(packed_index == own_index, frame_offset, 0))
    picker = jnp.arange(MAXF, dtype=jnp.int32) == own_offset
    position = jnp.sum(jnp.where(picker[:, None], frame_embed.astype(F32), 0.0), axis=0)
    embedded = jnp.dot(tokens, patch_weight, preferred_element_type=F32) + position[None, :]
    scale = lax.rsqrt(jnp.mean(embedded * embedded, axis=-1, keepdims=True) + EPSILON)
    extra = jnp.broadcast_to(picker.astype(BF)[None, :], (tokens.shape[0], MAXF))
    full = jnp.concatenate([tokens, extra], axis=1)
    by_head = folded.reshape(HID // HEAD_DIM, HEAD_DIM, -1)
    projected = lax.dot_general(by_head, full, (((2,), (1,)), ((), ())), preferred_element_type=F32)
    projected = projected.transpose(0, 2, 1) * scale[None]
    return projected.astype(BF)


def solution(mesh):
    return jax.shard_map(
        local,
        mesh=mesh,
        in_specs=(P("dp", "cp", None, None), P("dp"), P(), P(), P(), P(), P(), P(), P(None, "cp")),
        out_specs=P(None, ("dp", "cp"), None),
        check_vma=False,
    )
```

```python
import functools

import jax
import jax.numpy as jnp
import numpy as np
from jax import lax
from jax.experimental import pallas as pl
from jax.experimental.pallas import tpu as pltpu
from jax.sharding import PartitionSpec as P

LAT = 16
HID = 3072
HEAD_DIM = 128
HEADS = HID // HEAD_DIM
MAXF = 6
C = 512
WIDTH = 8
STRIP = 4
FRAMES = 64
CLIPS = 16
PART = HID // FRAMES
TOKENS = 512
LANES = 128
MESSAGE = 32
EPSILON = 1e-06
BF = jnp.bfloat16
F32 = jnp.float32
VMEM = pl.BlockSpec(memory_space=pltpu.VMEM)
SMEM = pl.BlockSpec(memory_space=pltpu.SMEM)
ANY = pl.BlockSpec(memory_space=pl.ANY)
MIB = 1 << 20


def nt(left, right):
    return lax.dot_general(left, right, (((1,), (1,)), ((), ())), preferred_element_type=F32)


def dot(left, right):
    return jnp.dot(left, right, preferred_element_type=F32)


def split(value):
    high = value.astype(BF)
    return high, (value - high.astype(F32)).astype(BF)


def each_clip(counts, body):
    def step(clip, start):
        body(clip, start, counts[clip])
        return start + counts[clip]

    lax.fori_loop(0, CLIPS, step, 0)


def edges_kernel(counts, frames, first, last, sems):
    def clip(index, start, count):
        for row, target, sem in ((0, first, 0), (STRIP - 1, last, 1)):
            pltpu.make_async_copy(
                frames.at[pl.ds(index * MAXF, count), row], target.at[pl.ds(start, count)], sems.at[sem]
            ).start()

    each_clip(counts, clip)
    pltpu.make_async_copy(first, first, sems.at[0]).wait()
    pltpu.make_async_copy(last, last, sems.at[1]).wait()


def edges(counts, frames):
    shape = jax.ShapeDtypeStruct((FRAMES, WIDTH, C), BF)
    return pl.pallas_call(
        edges_kernel,
        out_shape=(shape, shape),
        in_specs=[SMEM, ANY],
        out_specs=(ANY, ANY),
        scratch_shapes=[pltpu.SemaphoreType.DMA((2,))],
        cost_estimate=pl.CostEstimate(flops=0, bytes_accessed=2 * MIB, transcendentals=0),
        name="edges",
    )(counts, frames)


def fold_kernel(weight, patch, embed, gain, folded, placed, padded):
    scale = gain[...]
    padded[...] = jnp.zeros_like(padded)
    padded[64 : 64 + PART, :] = weight[...]
    high, low = split(patch[...].astype(F32) * scale)
    both = nt(weight[...], jnp.concatenate([high, high], axis=0)) + nt(
        weight[...], jnp.concatenate([low, low], axis=0)
    )
    lane = lax.broadcasted_iota(jnp.int32, (PART // 2, LANES), 1)
    folded[...] = jnp.where(lane < 64, both[: PART // 2], both[PART // 2 :])
    high, low = split(embed[...].astype(F32) * scale)
    placed[...] = nt(high, padded[...]) + nt(low, padded[...])


def fold(weight, patch, embed, gain):
    return pl.pallas_call(
        fold_kernel,
        out_shape=(
            jax.ShapeDtypeStruct((PART // 2, LANES), F32),
            jax.ShapeDtypeStruct((MAXF, LANES), F32),
        ),
        in_specs=[VMEM] * 4,
        out_specs=(VMEM, VMEM),
        scratch_shapes=[pltpu.VMEM((LANES, HID), BF)],
        compiler_params=pltpu.CompilerParams(vmem_limit_bytes=16 * MIB),
        cost_estimate=pl.CostEstimate(flops=400_000_000, bytes_accessed=MIB, transcendentals=0),
        name="fold",
    )(weight, patch, embed, gain)


def latent_of(summed, frame, gain, proj):
    residual = frame.astype(F32) + 0.5 * summed * (1.0 + jnp.tanh(0.5 * summed))
    mean = jnp.mean(residual * residual, axis=-1, keepdims=True)
    normed = (residual * lax.rsqrt(mean + EPSILON) * gain).astype(BF)
    return nt(normed, proj)


def in_patch(latent, row):
    lane = lax.broadcasted_iota(jnp.int32, (FRAMES, LANES), 1) // LAT
    tokens = []
    for patch in range(WIDTH // 2):
        total = jnp.zeros((FRAMES, LANES), F32)
        for side in range(2):
            column = 2 * patch + side
            block = latent[column * FRAMES : (column + 1) * FRAMES]
            total = total + jnp.where(lane == (row % 2) * 2 + side, block, 0.0)
        tokens.append(total)
    return tokens


def spread_proj(proj, copies):
    copies[...] = jnp.zeros_like(copies)
    for copy in range(4):
        copies[copy * LAT : (copy + 1) * LAT, :] = proj[...]


def by_column(row, wide, cols, lane):
    row = row.astype(F32).reshape(FRAMES * WIDTH, C)
    for piece in range(C // LANES):
        wide[piece] = row[:, piece * LANES : (piece + 1) * LANES]
    for column in range(WIDTH):
        blocks = [wide[piece, pl.ds(column, FRAMES, stride=WIDTH), :] for piece in range(C // LANES)]
        block = jnp.concatenate(blocks, axis=1).astype(BF)
        cols[column * FRAMES : (column + 1) * FRAMES, lane : lane + C] = block


def inner_kernel(
    counts, frames, weight, gain, proj, sums, own, tokens, stage, wide, cols, taps, total, copies, frame_sem, tap_sems
):
    def clip(index, start, count):
        pltpu.make_async_copy(
            frames.at[pl.ds(index * MAXF, count)], stage.at[pl.ds(start, count)], frame_sem
        ).start()

    each_clip(counts, clip)
    order = (1, 0, 2)
    loads = {}
    for side in order:
        for row in range(3):
            loads[side, row] = pltpu.make_async_copy(
                weight.at[row, side], taps.at[side, pl.ds(row * C, C)], tap_sems.at[side, row]
            )
            loads[side, row].start()
    spread_proj(proj, copies)
    pltpu.make_async_copy(stage, stage, frame_sem).wait()
    for row in range(STRIP):
        by_column(stage[:, row], wide, cols, row * C)
    for place, row in enumerate((0, STRIP - 1)):
        own[place] = cols[:, row * C : (row + 1) * C]
    count = FRAMES * WIDTH
    for side in order:
        for row in range(3):
            loads[side, row].wait()
        begin, end = max(0, side - 1) * FRAMES, count - max(0, 1 - side) * FRAMES
        shift = (1 - side) * FRAMES
        for row in range(STRIP):
            low, high = max(row - 1, 0), min(row + 2, STRIP)
            skip = low - (row - 1)
            part = dot(
                cols[begin:end, low * C : high * C],
                taps[side, skip * C : (skip + high - low) * C, :],
            )
            if side == 1:
                total[row] = part
            else:
                total[row, begin + shift : end + shift, :] += part
    sums[0] = total[0]
    sums[1] = total[STRIP - 1]
    for row in (1, 2):
        latent = latent_of(total[row], cols[:, row * C : (row + 1) * C], gain[...], copies[...])
        for patch, value in enumerate(in_patch(latent, row)):
            tokens[(row // 2) * 4 + patch] = value


def inner(counts, frames, weight, gain, proj):
    return pl.pallas_call(
        inner_kernel,
        out_shape=(
            jax.ShapeDtypeStruct((2, FRAMES * WIDTH, C), F32),
            jax.ShapeDtypeStruct((2, FRAMES * WIDTH, C), BF),
            jax.ShapeDtypeStruct((8, FRAMES, LANES), F32),
        ),
        in_specs=[SMEM, ANY, ANY, VMEM, VMEM],
        out_specs=(VMEM, VMEM, VMEM),
        scratch_shapes=[
            pltpu.VMEM((FRAMES, STRIP, WIDTH, C), BF),
            pltpu.VMEM((C // LANES, FRAMES * WIDTH, LANES), F32),
            pltpu.VMEM((FRAMES * WIDTH, STRIP * C), BF),
            pltpu.VMEM((3, 3 * C, C), BF),
            pltpu.VMEM((STRIP, FRAMES * WIDTH, C), F32),
            pltpu.VMEM((LANES, C), BF),
            pltpu.SemaphoreType.DMA,
            pltpu.SemaphoreType.DMA((3, 3)),
        ],
        compiler_params=pltpu.CompilerParams(vmem_limit_bytes=40 * MIB),
        cost_estimate=pl.CostEstimate(flops=8_000_000_000, bytes_accessed=9 * MIB, transcendentals=MIB // 2),
        name="inner",
    )(counts, frames, weight, gain, proj)


def outer_kernel(
    counts, before, after, weight, sums, own, tokens, gain, proj, folded, placed, message, wide, cols, total, copies, flat
):
    spread_proj(proj, copies)
    count = FRAMES * WIDTH
    parts = [tokens[index] for index in range(8)]
    for place, (halo, tap, row) in enumerate(((before, 0, 0), (after, 2, STRIP - 1))):
        by_column(halo[...], wide, cols, 0)
        total[...] = sums[place]
        for side in range(3):
            begin, end = max(0, side - 1) * FRAMES, count - max(0, 1 - side) * FRAMES
            shift = (1 - side) * FRAMES
            total[begin + shift : end + shift, :] += dot(cols[begin:end], weight[tap, side])
        latent = latent_of(total[...], own[place], gain[...], copies[...])
        for patch, value in enumerate(in_patch(latent, row)):
            parts[(row // 2) * 4 + patch] += value
    frame = lax.broadcasted_iota(jnp.int32, (FRAMES, 1), 0)
    begin = jnp.zeros((FRAMES, 1), jnp.int32)
    start = 0
    for clip in range(CLIPS):
        begin = jnp.where(frame >= start, start, begin)
        start = start + counts[clip]
    position = jnp.zeros((FRAMES, LANES), F32)
    for offset in range(MAXF):
        position = position + jnp.where(frame - begin == offset, placed[offset : offset + 1, :], 0.0)
    high, low = split(position)
    parts[0] = parts[0] + high.astype(F32)
    parts[1] = parts[1] + low.astype(F32)
    for index in range(8):
        flat[pl.ds(index, FRAMES, stride=8), :] = parts[index]
    rest = jnp.broadcast_to(folded[...][None], (FRAMES, PART // 2, LANES))
    message[...] = jnp.concatenate([flat[...].reshape(FRAMES, 8, LANES), rest], axis=1).astype(BF)


def outer(counts, before, after, weight, sums, own, tokens, gain, proj, folded, placed):
    return pl.pallas_call(
        outer_kernel,
        out_shape=jax.ShapeDtypeStruct((FRAMES, MESSAGE, LANES), BF),
        in_specs=[SMEM] + [VMEM] * 10,
        out_specs=VMEM,
        scratch_shapes=[
            pltpu.VMEM((C // LANES, FRAMES * WIDTH, LANES), F32),
            pltpu.VMEM((FRAMES * WIDTH, C), BF),
            pltpu.VMEM((FRAMES * WIDTH, C), F32),
            pltpu.VMEM((LANES, C), BF),
            pltpu.VMEM((TOKENS, LANES), F32),
        ],
        compiler_params=pltpu.CompilerParams(vmem_limit_bytes=32 * MIB),
        cost_estimate=pl.CostEstimate(flops=1_700_000_000, bytes_accessed=7 * MIB, transcendentals=MIB // 2),
        name="outer",
    )(counts, before, after, weight, sums, own, tokens, gain, proj, folded, placed)


BLOCK = 4


def project_kernel(counts, index, arrived, patch, embed, spread, out, flat, query, scale, columns, shift):
    @pl.when(pl.program_id(0) == 0)
    def _():
        got = arrived[...].astype(F32)
        flat[...] = got[:, 0:8].reshape(TOKENS, LANES)
        lane = lax.broadcasted_iota(jnp.int32, (TOKENS, LANES), 1)
        token = jnp.where(lane < 64, flat[...], 0.0)
        query[...] = (token + pltpu.roll(token, 64, 1)).astype(BF)
        rest = got[:, 8:MESSAGE]
        lane = lax.broadcasted_iota(jnp.int32, rest.shape, 2)
        low, high = jnp.where(lane < 64, rest, 0.0), jnp.where(lane < 64, 0.0, rest)
        columns[...] = jnp.concatenate([low, high], axis=1).reshape(HID, LANES).astype(BF)
        lane = lax.broadcasted_iota(jnp.int32, (FRAMES, HID), 1)
        line = lax.broadcasted_iota(jnp.int32, (FRAMES, HID), 0) * PART
        sums = jnp.zeros((FRAMES, HID), F32)
        for row in range(2):
            sums = sums + dot(flat[pl.ds(row, FRAMES, stride=8), :].astype(BF), spread[...])
        shift[...] = jnp.sum(
            jnp.where((lane >= line) & (lane < line + PART), sums, 0.0), axis=0, keepdims=True
        )

        def clip(at, carry):
            start, begin = carry
            begin = jnp.where(start <= index[0], start, begin)
            return start + counts[at], begin

        _, begin = lax.fori_loop(0, CLIPS, clip, (0, 0))
        line = lax.broadcasted_iota(jnp.int32, (MAXF, HID), 0)
        position = jnp.sum(
            jnp.where(line == index[0] - begin, embed[...].astype(F32), 0.0), axis=0, keepdims=True
        )
        squares = jnp.zeros((TOKENS, LANES), F32)
        for block in range(HID // C):
            part = slice(block * C, (block + 1) * C)
            value = dot(query[:, 0:64], patch[:, part]) + position[:, part]
            value = value * value
            for piece in range(C // LANES):
                squares = squares + value[:, piece * LANES : (piece + 1) * LANES]
        mean = jnp.sum(squares, axis=-1, keepdims=True) * (1.0 / HID)
        scale[...] = jnp.broadcast_to(lax.rsqrt(mean + EPSILON), (TOKENS, LANES))

    step = pl.program_id(0)
    for head in range(BLOCK):
        at = pl.multiple_of((step * BLOCK + head) * HEAD_DIM, HEAD_DIM)
        value = nt(query[...], columns[pl.ds(at, HEAD_DIM), :]) + shift[:, pl.ds(at, HEAD_DIM)]
        out[head] = (value * scale[...]).astype(BF)


def project(counts, index, arrived, patch, embed, spread):
    def whole(*shape):
        return pl.BlockSpec(shape, lambda step: (0,) * len(shape))

    return pl.pallas_call(
        project_kernel,
        out_shape=jax.ShapeDtypeStruct((HEADS, TOKENS, HEAD_DIM), BF),
        grid=(HEADS // BLOCK,),
        in_specs=[
            SMEM,
            SMEM,
            whole(FRAMES, MESSAGE, LANES),
            whole(64, HID),
            whole(MAXF, HID),
            whole(LANES, HID),
        ],
        out_specs=pl.BlockSpec((BLOCK, TOKENS, HEAD_DIM), lambda step: (step, 0, 0)),
        scratch_shapes=[
            pltpu.VMEM((TOKENS, LANES), F32),
            pltpu.VMEM((TOKENS, LANES), BF),
            pltpu.VMEM((TOKENS, LANES), F32),
            pltpu.VMEM((HID, LANES), BF),
            pltpu.VMEM((1, HID), F32),
        ],
        compiler_params=pltpu.CompilerParams(vmem_limit_bytes=32 * MIB),
        cost_estimate=pl.CostEstimate(flops=800_000_000, bytes_accessed=5 * MIB, transcendentals=0),
        name="project",
    )(counts, index, arrived, patch, embed, spread)


def spread_table():
    table = np.zeros((LANES, HID), np.float32)
    for column in range(HID):
        table[64 + column % PART, column] = 1.0
    return table


def local(
    frame_rows,
    frame_counts,
    conv_weight,
    norm_gain,
    latent_proj,
    patch_weight,
    frame_embed,
    query_gain,
    query_weight,
):
    devices = lax.axis_size("cp")
    up = [(i, i + 1) for i in range(devices - 1)]
    down = [(j, i) for i, j in up]
    first, last = edges(frame_counts, frame_rows)
    before = lax.ppermute(last, "cp", up)
    after = lax.ppermute(first, "cp", down)
    gain = norm_gain[None, :]
    folded, placed = fold(query_weight.T, patch_weight, frame_embed, query_gain[None, :])
    sums, own, tokens = inner(frame_counts, frame_rows, conv_weight, gain, latent_proj.T)
    message = outer(
        frame_counts, before, after, conv_weight, sums, own, tokens, gain, latent_proj.T, folded, placed
    )
    arrived = lax.all_to_all(message, "cp", split_axis=0, concat_axis=0, tiled=True)
    index = lax.axis_index("cp").astype(jnp.int32)[None]
    spread = jnp.asarray(spread_table(), BF)
    return project(frame_counts, index, arrived, patch_weight, frame_embed, spread)


def solution(mesh):
    return jax.shard_map(
        local,
        mesh=mesh,
        in_specs=(P("dp", "cp", None, None), P("dp"), P(), P(), P(), P(), P(), P(), P(None, "cp")),
        out_specs=P(None, ("dp", "cp"), None),
        check_vma=False,
    )
```

```python
import functools

import jax
import jax.numpy as jnp
import numpy as np
from jax import lax
from jax.experimental import pallas as pl
from jax.experimental.pallas import tpu as pltpu
from jax.sharding import PartitionSpec as P

LAT = 16
HID = 3072
HEAD_DIM = 128
HEADS = HID // HEAD_DIM
MAXF = 6
C = 512
WIDTH = 8
STRIP = 4
FRAMES = 64
CLIPS = 16
PART = HID // FRAMES
TOKENS = 512
LANES = 128
MESSAGE = 32
EPSILON = 1e-06
BF = jnp.bfloat16
F32 = jnp.float32
VMEM = pl.BlockSpec(memory_space=pltpu.VMEM)
SMEM = pl.BlockSpec(memory_space=pltpu.SMEM)
HBM = pl.BlockSpec(memory_space=pltpu.HBM)
MIB = 1 << 20


def in_hbm(value):
    return pltpu.with_memory_space_constraint(value, pltpu.HBM)


def nt(left, right):
    return lax.dot_general(left, right, (((1,), (1,)), ((), ())), preferred_element_type=F32)


def dot(left, right):
    return jnp.dot(left, right, preferred_element_type=F32)


def split(value):
    high = value.astype(BF)
    return high, (value - high.astype(F32)).astype(BF)


def each_clip(counts, body):
    def step(clip, start):
        body(clip, start, counts[clip])
        return start + counts[clip]

    lax.fori_loop(0, CLIPS, step, 0)


def edges_kernel(counts, index, frames, odd_pair, even_pair, sems):
    low = (index[0] % 2) * (STRIP - 1)

    def clip(at, start, count):
        for row, target, sem in ((low, odd_pair, 0), (STRIP - 1 - low, even_pair, 1)):
            pltpu.make_async_copy(
                frames.at[pl.ds(at * MAXF, count), row], target.at[pl.ds(start, count)], sems.at[sem]
            ).start()

    each_clip(counts, clip)
    pltpu.make_async_copy(odd_pair, odd_pair, sems.at[0]).wait()
    pltpu.make_async_copy(even_pair, even_pair, sems.at[1]).wait()


def edges(counts, index, frames):
    shape = jax.ShapeDtypeStruct((FRAMES, WIDTH, C), BF)
    return pl.pallas_call(
        edges_kernel,
        out_shape=(shape, shape),
        in_specs=[SMEM, SMEM, HBM],
        out_specs=(VMEM, VMEM),
        scratch_shapes=[pltpu.SemaphoreType.DMA((2,))],
        cost_estimate=pl.CostEstimate(flops=0, bytes_accessed=2 * MIB, transcendentals=0),
        name="edges",
    )(counts, index, in_hbm(frames))


def latent_of(summed, frame, gain, proj):
    residual = frame.astype(F32) + 0.5 * summed * (1.0 + jnp.tanh(0.5 * summed))
    mean = jnp.mean(residual * residual, axis=-1, keepdims=True)
    normed = (residual * lax.rsqrt(mean + EPSILON) * gain).astype(BF)
    return nt(normed, proj)


def in_patch(latent, row):
    lane = lax.broadcasted_iota(jnp.int32, (FRAMES, LANES), 1) // LAT
    tokens = []
    for patch in range(WIDTH // 2):
        total = jnp.zeros((FRAMES, LANES), F32)
        for side in range(2):
            column = 2 * patch + side
            block = latent[column * FRAMES : (column + 1) * FRAMES]
            total = total + jnp.where(lane == (row % 2) * 2 + side, block, 0.0)
        tokens.append(total)
    return tokens


def spread_proj(proj, copies):
    copies[...] = jnp.zeros_like(copies)
    for copy in range(4):
        copies[copy * LAT : (copy + 1) * LAT, :] = proj[...]


def by_column(row, wide, cols, lane):
    row = row.astype(F32).reshape(FRAMES * WIDTH, C)
    for piece in range(C // LANES):
        wide[piece] = row[:, piece * LANES : (piece + 1) * LANES]
    for column in range(WIDTH):
        blocks = [wide[piece, pl.ds(column, FRAMES, stride=WIDTH), :] for piece in range(C // LANES)]
        block = jnp.concatenate(blocks, axis=1).astype(BF)
        cols[column * FRAMES : (column + 1) * FRAMES, lane : lane + C] = block


def fold(weight, table, scale, padded, folded, placed, gram):
    padded[...] = jnp.zeros_like(padded)
    padded[64 : 64 + PART, :] = weight[...]
    high, low = split(table[...].astype(F32) * scale)
    both = nt(weight[...], jnp.concatenate([high[:64], high[:64]], axis=0))
    both = both + nt(weight[...], jnp.concatenate([low[:64], low[:64]], axis=0))
    lane = lax.broadcasted_iota(jnp.int32, (PART // 2, LANES), 1)
    folded[...] = jnp.where(lane < 64, both[: PART // 2], both[PART // 2 :])
    placed[...] = nt(high[64:], padded[...]) + nt(low[64:], padded[...])
    gram[...] = nt(table[...], table[...])


def inner_kernel(
    counts,
    frames,
    weight,
    gain,
    proj,
    columns,
    patch,
    embed,
    scale,
    sums,
    own,
    tokens,
    taps,
    copies,
    norm,
    folded,
    placed,
    gram,
    stage,
    wide,
    cols,
    total,
    projs,
    held,
    table,
    embeds,
    gains,
    padded,
    sems,
    tap_sems,
):
    small = [
        pltpu.make_async_copy(source, target, sems.at[place])
        for place, (source, target) in enumerate(
            (
                (columns, held),
                (patch, table.at[pl.ds(0, 64)]),
                (embed, embeds),
                (scale, gains),
                (proj, projs),
                (gain, norm),
            )
        )
    ]
    for copy in small:
        copy.start()

    def clip(index, start, count):
        pltpu.make_async_copy(
            frames.at[pl.ds(index * MAXF, count)], stage.at[pl.ds(start, count)], sems.at[6]
        ).start()

    each_clip(counts, clip)
    order = (1, 0, 2)
    loads = {}
    for side in order:
        for row in range(3):
            loads[side, row] = pltpu.make_async_copy(
                weight.at[row, side], taps.at[side, pl.ds(row * C, C)], tap_sems.at[side, row]
            )
            loads[side, row].start()
    for copy in small:
        copy.wait()
    spread_proj(projs, copies)
    table[64:80, :] = jnp.concatenate(
        [embeds[...].astype(F32), jnp.zeros((16 - MAXF, HID), F32)], axis=0
    ).astype(BF)
    fold(held, table, gains[...], padded, folded, placed, gram)
    pltpu.make_async_copy(stage, stage, sems.at[6]).wait()
    for row in range(STRIP):
        by_column(stage[:, row], wide.at[row], cols, row * C)
    for place, row in enumerate((0, STRIP - 1)):
        own[place] = cols[:, row * C : (row + 1) * C]
    count = FRAMES * WIDTH
    for side in order:
        for row in range(3):
            loads[side, row].wait()
        begin, end = max(0, side - 1) * FRAMES, count - max(0, 1 - side) * FRAMES
        shift = (1 - side) * FRAMES
        for row in range(STRIP):
            low, high = max(row - 1, 0), min(row + 2, STRIP)
            skip = low - (row - 1)
            part = dot(
                cols[begin:end, low * C : high * C],
                taps[side, skip * C : (skip + high - low) * C, :],
            )
            if side == 1:
                total[row] = part
            else:
                total[row, begin + shift : end + shift, :] += part
    sums[0] = total[0]
    sums[1] = total[STRIP - 1]
    for row in (1, 2):
        latent = latent_of(total[row], cols[:, row * C : (row + 1) * C], norm[...], copies[...])
        for patch_index, value in enumerate(in_patch(latent, row)):
            tokens[(row // 2) * 4 + patch_index] = value


def inner(counts, frames, weight, gain, proj, columns, patch, embed, scale):
    return pl.pallas_call(
        inner_kernel,
        out_shape=(
            jax.ShapeDtypeStruct((2, FRAMES * WIDTH, C), F32),
            jax.ShapeDtypeStruct((2, FRAMES * WIDTH, C), BF),
            jax.ShapeDtypeStruct((8, FRAMES, LANES), F32),
            jax.ShapeDtypeStruct((3, 3 * C, C), BF),
            jax.ShapeDtypeStruct((LANES, C), BF),
            jax.ShapeDtypeStruct((1, C), F32),
            jax.ShapeDtypeStruct((PART // 2, LANES), F32),
            jax.ShapeDtypeStruct((16, LANES), F32),
            jax.ShapeDtypeStruct((80, 80), F32),
        ),
        in_specs=[SMEM] + [HBM] * 8,
        out_specs=(VMEM,) * 9,
        scratch_shapes=[
            pltpu.VMEM((FRAMES, STRIP, WIDTH, C), BF),
            pltpu.VMEM((STRIP, C // LANES, FRAMES * WIDTH, LANES), F32),
            pltpu.VMEM((FRAMES * WIDTH, STRIP * C), BF),
            pltpu.VMEM((STRIP, FRAMES * WIDTH, C), F32),
            pltpu.VMEM((LAT, C), BF),
            pltpu.VMEM((PART, HID), BF),
            pltpu.VMEM((80, HID), BF),
            pltpu.VMEM((MAXF, HID), BF),
            pltpu.VMEM((1, HID), F32),
            pltpu.VMEM((LANES, HID), BF),
            pltpu.SemaphoreType.DMA((7,)),
            pltpu.SemaphoreType.DMA((3, 3)),
        ],
        compiler_params=pltpu.CompilerParams(vmem_limit_bytes=36 * MIB),
        cost_estimate=pl.CostEstimate(flops=8_000_000_000, bytes_accessed=9 * MIB, transcendentals=MIB // 2),
        name="inner",
    )(counts, *map(in_hbm, (frames, weight, gain, proj, columns, patch, embed, scale)))


def outer_kernel(
    counts, index, odd_pair, even_pair, taps, sums, own, tokens, copies, gain, folded, placed, message, wide, cols, total, flat
):
    count = FRAMES * WIDTH
    parts = [tokens[index] for index in range(8)]
    odd = index[0] % 2 == 1
    for place, (tap, row) in enumerate(((0, 0), (2, STRIP - 1))):
        ours, other = (even_pair, odd_pair) if place == 0 else (odd_pair, even_pair)
        by_column(jnp.where(odd, ours[...], other[...]), wide, cols, 0)
        total[...] = sums[place]
        for side in range(3):
            begin, end = max(0, side - 1) * FRAMES, count - max(0, 1 - side) * FRAMES
            shift = (1 - side) * FRAMES
            total[begin + shift : end + shift, :] += dot(cols[begin:end], taps[side, tap * C : (tap + 1) * C, :])
        latent = latent_of(total[...], own[place], gain[...], copies[...])
        for patch, value in enumerate(in_patch(latent, row)):
            parts[(row // 2) * 4 + patch] += value
    frame = lax.broadcasted_iota(jnp.int32, (FRAMES, 1), 0)
    begin = jnp.zeros((FRAMES, 1), jnp.int32)
    start = 0
    for clip in range(CLIPS):
        begin = jnp.where(frame >= start, start, begin)
        start = start + counts[clip]
    position = jnp.zeros((FRAMES, LANES), F32)
    for offset in range(MAXF):
        position = position + jnp.where(frame - begin == offset, placed[offset : offset + 1, :], 0.0)
    high, low = split(position)
    parts[0] = parts[0] + high.astype(F32)
    parts[1] = parts[1] + low.astype(F32)
    for index in range(8):
        flat[pl.ds(index, FRAMES, stride=8), :] = parts[index]
    rest = jnp.broadcast_to(folded[...][None], (FRAMES, PART // 2, LANES))
    message[...] = jnp.concatenate([flat[...].reshape(FRAMES, 8, LANES), rest], axis=1).astype(BF)


def outer(counts, index, odd_pair, even_pair, taps, sums, own, tokens, copies, gain, folded, placed):
    return pl.pallas_call(
        outer_kernel,
        out_shape=jax.ShapeDtypeStruct((FRAMES, MESSAGE, LANES), BF),
        in_specs=[SMEM, SMEM] + [VMEM] * 10,
        out_specs=VMEM,
        scratch_shapes=[
            pltpu.VMEM((C // LANES, FRAMES * WIDTH, LANES), F32),
            pltpu.VMEM((FRAMES * WIDTH, C), BF),
            pltpu.VMEM((FRAMES * WIDTH, C), F32),
            pltpu.VMEM((TOKENS, LANES), F32),
        ],
        compiler_params=pltpu.CompilerParams(vmem_limit_bytes=32 * MIB),
        cost_estimate=pl.CostEstimate(flops=1_700_000_000, bytes_accessed=7 * MIB, transcendentals=MIB // 2),
        name="outer",
    )(counts, index, odd_pair, even_pair, taps, sums, own, tokens, copies, gain, folded, placed)


BLOCK = 4


def project_kernel(counts, index, arrived, gram, spread, out, flat, query, scale, columns, shift):
    @pl.when(pl.program_id(0) == 0)
    def _():
        got = arrived[...].astype(F32)
        flat[...] = got[:, 0:8].reshape(TOKENS, LANES)
        lane = lax.broadcasted_iota(jnp.int32, (TOKENS, LANES), 1)
        token = jnp.where(lane < 64, flat[...], 0.0)
        query[...] = (token + pltpu.roll(token, 64, 1)).astype(BF)
        rest = got[:, 8:MESSAGE]
        lane = lax.broadcasted_iota(jnp.int32, rest.shape, 2)
        low, high = jnp.where(lane < 64, rest, 0.0), jnp.where(lane < 64, 0.0, rest)
        columns[...] = jnp.concatenate([low, high], axis=1).reshape(HID, LANES).astype(BF)
        lane = lax.broadcasted_iota(jnp.int32, (FRAMES, HID), 1)
        line = lax.broadcasted_iota(jnp.int32, (FRAMES, HID), 0) * PART
        sums = jnp.zeros((FRAMES, HID), F32)
        for row in range(2):
            piece = pltpu.roll(flat[pl.ds(row, FRAMES, stride=8), :], 64, 1)
            sums = sums + dot(piece[:, 0:64].astype(BF), spread[...])
        shift[...] = jnp.sum(
            jnp.where((lane >= line) & (lane < line + PART), sums, 0.0), axis=0, keepdims=True
        )

        def clip(at, carry):
            start, begin = carry
            begin = jnp.where(start <= index[0], start, begin)
            return start + counts[at], begin

        _, begin = lax.fori_loop(0, CLIPS, clip, (0, 0))
        matrix = gram[...]
        line = lax.broadcasted_iota(jnp.int32, (16, 80), 0)
        position = jnp.sum(jnp.where(line == index[0] - begin, matrix[64:], 0.0), axis=0, keepdims=True)
        lane = lax.broadcasted_iota(jnp.int32, (1, 80), 1)
        square = jnp.sum(jnp.where(lane == 64 + index[0] - begin, position, 0.0), axis=1, keepdims=True)
        token = token[:, 0:64]
        total = jnp.zeros((TOKENS, 64), F32) + 2.0 * position[:, 0:64]
        matrix = matrix[:64, :64]
        for _ in range(3):
            piece = matrix.astype(BF)
            total = total + dot(token.astype(BF), piece)
            matrix = matrix - piece.astype(F32)
        total = jnp.sum(total * token, axis=-1, keepdims=True) + square
        mean = jnp.maximum(total, 0.0) * (1.0 / HID)
        scale[...] = jnp.broadcast_to(lax.rsqrt(mean + EPSILON), (TOKENS, LANES))

    step = pl.program_id(0)
    for head in range(BLOCK):
        at = pl.multiple_of((step * BLOCK + head) * HEAD_DIM, HEAD_DIM)
        value = nt(query[...], columns[pl.ds(at, HEAD_DIM), :]) + shift[:, pl.ds(at, HEAD_DIM)]
        out[head] = (value * scale[...]).astype(BF)


def project(counts, index, arrived, gram, spread):
    return pl.pallas_call(
        project_kernel,
        out_shape=jax.ShapeDtypeStruct((HEADS, TOKENS, HEAD_DIM), BF),
        grid=(HEADS // BLOCK,),
        in_specs=[SMEM, SMEM, VMEM, VMEM, VMEM],
        out_specs=pl.BlockSpec((BLOCK, TOKENS, HEAD_DIM), lambda step: (step, 0, 0)),
        scratch_shapes=[
            pltpu.VMEM((TOKENS, LANES), F32),
            pltpu.VMEM((TOKENS, LANES), BF),
            pltpu.VMEM((TOKENS, LANES), F32),
            pltpu.VMEM((HID, LANES), BF),
            pltpu.VMEM((1, HID), F32),
        ],
        compiler_params=pltpu.CompilerParams(vmem_limit_bytes=24 * MIB),
        cost_estimate=pl.CostEstimate(flops=800_000_000, bytes_accessed=5 * MIB, transcendentals=0),
        name="project",
    )(counts, index, arrived, gram, spread)


def spread_table():
    table = np.zeros((64, HID), np.float32)
    table[np.arange(HID) % PART, np.arange(HID)] = 1.0
    return table


def local(
    frame_rows,
    frame_counts,
    conv_weight,
    norm_gain,
    latent_proj,
    patch_weight,
    frame_embed,
    query_gain,
    query_weight,
):
    devices = lax.axis_size("cp")
    index = lax.axis_index("cp").astype(jnp.int32)[None]
    odd_pair, even_pair = edges(frame_counts, index, frame_rows)
    pairs = [[(i, i + 1) for i in range(begin, devices - 1, 2)] for begin in (1, 0)]
    swaps = [pair + [(j, i) for i, j in pair] for pair in pairs]
    odd_pair = lax.ppermute(odd_pair, "cp", swaps[0])
    even_pair = lax.ppermute(even_pair, "cp", swaps[1])
    sums, own, tokens, taps, copies, gain, folded, placed, gram = inner(
        frame_counts,
        frame_rows,
        conv_weight,
        norm_gain[None, :],
        latent_proj.T,
        query_weight.T,
        patch_weight,
        frame_embed,
        query_gain[None, :],
    )
    message = outer(frame_counts, index, odd_pair, even_pair, taps, sums, own, tokens, copies, gain, folded, placed)
    arrived = lax.all_to_all(message, "cp", split_axis=0, concat_axis=0, tiled=True)
    return project(frame_counts, index, arrived, gram, jnp.asarray(spread_table(), BF))


def solution(mesh):
    return jax.shard_map(
        local,
        mesh=mesh,
        in_specs=(P("dp", "cp", None, None), P("dp"), P(), P(), P(), P(), P(), P(), P(None, "cp")),
        out_specs=P(None, ("dp", "cp"), None),
        check_vma=False,
    )
```

```python
import functools

import jax
import jax.numpy as jnp
import numpy as np
from jax import lax
from jax.experimental import pallas as pl
from jax.experimental.pallas import tpu as pltpu
from jax.sharding import PartitionSpec as P

LAT = 16
HID = 3072
HEAD_DIM = 128
HEADS = HID // HEAD_DIM
MAXF = 6
C = 512
WIDTH = 8
STRIP = 4
FRAMES = 64
CLIPS = 16
PART = HID // FRAMES
TOKENS = 512
LANES = 128
MESSAGE = 32
EPSILON = 1e-06
BF = jnp.bfloat16
F32 = jnp.float32
VMEM = pl.BlockSpec(memory_space=pltpu.VMEM)
SMEM = pl.BlockSpec(memory_space=pltpu.SMEM)
HBM = pl.BlockSpec(memory_space=pltpu.HBM)
MIB = 1 << 20


def in_hbm(value):
    return pltpu.with_memory_space_constraint(value, pltpu.HBM)


def nt(left, right):
    return lax.dot_general(left, right, (((1,), (1,)), ((), ())), preferred_element_type=F32)


def dot(left, right):
    return jnp.dot(left, right, preferred_element_type=F32)


def split(value):
    high = value.astype(BF)
    return high, (value - high.astype(F32)).astype(BF)


def each_clip(counts, body):
    def step(clip, start):
        body(clip, start, counts[clip])
        return start + counts[clip]

    lax.fori_loop(0, CLIPS, step, 0)


def is_odd():
    return lax.rem(lax.axis_index("cp"), 2)


def fetch_kernel(counts, frames, odd_rows, even_rows, stage, sem):
    def clip(at, start, count):
        pltpu.make_async_copy(
            frames.at[pl.ds(at * MAXF, count)], stage.at[pl.ds(start, count)], sem
        ).start()

    each_clip(counts, clip)
    pltpu.make_async_copy(stage, stage, sem).wait()
    row = is_odd() * (STRIP - 1)
    odd_rows[...] = stage[:, row]
    even_rows[...] = stage[:, STRIP - 1 - row]


def fetch(counts, frames):
    return pl.pallas_call(
        fetch_kernel,
        out_shape=(
            pltpu.VMEM((FRAMES, WIDTH, C), BF),
            pltpu.VMEM((FRAMES, WIDTH, C), BF),
            pltpu.VMEM((FRAMES, STRIP, WIDTH, C), BF),
        ),
        in_specs=[SMEM, HBM],
        out_specs=(VMEM,) * 3,
        scratch_shapes=[pltpu.SemaphoreType.DMA],
        cost_estimate=pl.CostEstimate(flops=0, bytes_accessed=4 * MIB, transcendentals=0),
        name="fetch",
    )(in_hbm(counts), in_hbm(frames))


def latent_of(summed, frame, gain, proj):
    residual = frame.astype(F32) + 0.5 * summed * (1.0 + jnp.tanh(0.5 * summed))
    mean = jnp.mean(residual * residual, axis=-1, keepdims=True)
    normed = (residual * lax.rsqrt(mean + EPSILON) * gain).astype(BF)
    return nt(normed, proj)


def in_patch(latent, below):
    lane = lax.broadcasted_iota(jnp.int32, (FRAMES, LANES), 1) // LAT
    tokens = []
    for patch in range(WIDTH // 2):
        total = jnp.zeros((FRAMES, LANES), F32)
        for side in range(2):
            column = 2 * patch + side
            block = latent[column * FRAMES : (column + 1) * FRAMES]
            total = total + jnp.where(lane == below * 2 + side, block, 0.0)
        tokens.append(total)
    return tokens


def spread_proj(proj, copies):
    copies[...] = jnp.zeros_like(copies)
    for copy in range(4):
        copies[copy * LAT : (copy + 1) * LAT, :] = proj[...]


def by_column(row, wide, cols, lane):
    row = row.astype(F32).reshape(FRAMES * WIDTH, C)
    for piece in range(C // LANES):
        wide[piece] = row[:, piece * LANES : (piece + 1) * LANES]
    for column in range(WIDTH):
        blocks = [wide[piece, pl.ds(column, FRAMES, stride=WIDTH), :] for piece in range(C // LANES)]
        block = jnp.concatenate(blocks, axis=1).astype(BF)
        cols[column * FRAMES : (column + 1) * FRAMES, lane : lane + C] = block


def fold(weight, table, scale, padded, folded, placed, gram):
    padded[...] = jnp.zeros_like(padded)
    padded[64 : 64 + PART, :] = weight[...]
    high, low = split(table[...].astype(F32) * scale)
    both = nt(weight[...], jnp.concatenate([high[:64], high[:64]], axis=0))
    both = both + nt(weight[...], jnp.concatenate([low[:64], low[:64]], axis=0))
    lane = lax.broadcasted_iota(jnp.int32, (PART // 2, LANES), 1)
    folded[...] = jnp.where(lane < 64, both[: PART // 2], both[PART // 2 :])
    placed[...] = nt(high[64:], padded[...]) + nt(low[64:], padded[...])
    gram[...] = nt(table[...], table[...])


def inner_kernel(
    stage,
    weight,
    columns,
    patch,
    embed,
    scale,
    proj,
    gain,
    sums,
    own,
    tokens,
    taps,
    copies,
    norm,
    folded,
    placed,
    gram,
    wide,
    cols,
    total,
    held,
    table,
    embeds,
    scales,
    projs,
    padded,
    small_sems,
    sems,
):
    small = [
        pltpu.make_async_copy(source, target, small_sems.at[place])
        for place, (source, target) in enumerate(
            (
                (columns, held),
                (patch, table.at[pl.ds(0, 64)]),
                (embed, embeds),
                (scale, scales),
                (proj, projs),
                (gain, norm),
            )
        )
    ]
    for copy in small:
        copy.start()
    order = (1, 0, 2)
    loads = {}
    for side in order:
        for row in range(3):
            loads[side, row] = pltpu.make_async_copy(
                weight.at[row, side], taps.at[side, pl.ds(row * C, C)], sems.at[side, row]
            )
            loads[side, row].start()
    for row in range(2):
        by_column(stage[:, row], wide.at[row], cols, row * C)
    for copy in small:
        copy.wait()
    table[64:80, :] = jnp.concatenate(
        [embeds[...].astype(F32), jnp.zeros((16 - MAXF, HID), F32)], axis=0
    ).astype(BF)
    fold(held, table, scales[...], padded, folded, placed, gram)
    spread_proj(projs, copies)
    count = FRAMES * WIDTH
    ready = 2
    for side in order:
        begin, end = max(0, side - 1) * FRAMES, count - max(0, 1 - side) * FRAMES
        shift = (1 - side) * FRAMES
        for row in range(STRIP):
            low, high = max(row - 1, 0), min(row + 2, STRIP)
            while ready < high:
                by_column(stage[:, ready], wide.at[ready], cols, ready * C)
                ready += 1
            if row == 0:
                for tap in range(3):
                    loads[side, tap].wait()
            skip = low - (row - 1)
            part = dot(
                cols[begin:end, low * C : high * C],
                taps[side, skip * C : (skip + high - low) * C, :],
            )
            target = sums.at[row // 2] if row in (0, STRIP - 1) else total.at[row - 1]
            if side == 1:
                target[...] = part
            else:
                target[begin + shift : end + shift, :] += part
    for place, row in enumerate((0, STRIP - 1)):
        own[place] = cols[:, row * C : (row + 1) * C]
    for row in (1, 2):
        latent = latent_of(total[row - 1], cols[:, row * C : (row + 1) * C], norm[...], copies[...])
        for patch_index, value in enumerate(in_patch(latent, row % 2)):
            tokens[(row // 2) * 4 + patch_index] = value


def inner(stage, *operands):
    return pl.pallas_call(
        inner_kernel,
        out_shape=(
            jax.ShapeDtypeStruct((2, FRAMES * WIDTH, C), F32),
            jax.ShapeDtypeStruct((2, FRAMES * WIDTH, C), BF),
            jax.ShapeDtypeStruct((8, FRAMES, LANES), F32),
            jax.ShapeDtypeStruct((3, 3 * C, C), BF),
            jax.ShapeDtypeStruct((LANES, C), BF),
            jax.ShapeDtypeStruct((1, C), F32),
            jax.ShapeDtypeStruct((PART // 2, LANES), F32),
            jax.ShapeDtypeStruct((16, LANES), F32),
            jax.ShapeDtypeStruct((80, 80), F32),
        ),
        in_specs=[VMEM] + [HBM] * 7,
        out_specs=(VMEM,) * 9,
        scratch_shapes=[
            pltpu.VMEM((STRIP, C // LANES, FRAMES * WIDTH, LANES), F32),
            pltpu.VMEM((FRAMES * WIDTH, STRIP * C), BF),
            pltpu.VMEM((2, FRAMES * WIDTH, C), F32),
            pltpu.VMEM((PART, HID), BF),
            pltpu.VMEM((80, HID), BF),
            pltpu.VMEM((MAXF, HID), BF),
            pltpu.VMEM((1, HID), F32),
            pltpu.VMEM((LAT, C), BF),
            pltpu.VMEM((LANES, HID), BF),
            pltpu.SemaphoreType.DMA((6,)),
            pltpu.SemaphoreType.DMA((3, 3)),
        ],
        compiler_params=pltpu.CompilerParams(vmem_limit_bytes=32 * MIB),
        cost_estimate=pl.CostEstimate(flops=8_000_000_000, bytes_accessed=9 * MIB, transcendentals=MIB // 2),
        name="inner",
    )(stage, *map(in_hbm, operands))


def edge_row(place, halo, taps, sums, own, copies, gain, wide, cols, total):
    count = FRAMES * WIDTH
    tap = pl.multiple_of(place * 2 * C, C)
    by_column(halo[...], wide, cols, 0)
    total[...] = sums[place]
    for side in (1, 0, 2):
        begin, end = max(0, side - 1) * FRAMES, count - max(0, 1 - side) * FRAMES
        shift = (1 - side) * FRAMES
        total[begin + shift : end + shift, :] += dot(cols[begin:end], taps[side, pl.ds(tap, C), :])
    latent = latent_of(total[...], own[place], gain[...], copies[...])
    return in_patch(latent, place)


def outer_scratch():
    return [
        pltpu.VMEM((C // LANES, FRAMES * WIDTH, LANES), F32),
        pltpu.VMEM((FRAMES * WIDTH, C), BF),
        pltpu.VMEM((FRAMES * WIDTH, C), F32),
    ]


def outer_even_kernel(listed, halo, taps, sums, own, tokens, copies, gain, placed, parts, *scratch):
    *scratch, counts, sem = scratch
    load = pltpu.make_async_copy(listed, counts, sem)
    load.start()
    place = 1 - is_odd()
    for patch, value in enumerate(edge_row(place, halo, taps, sums, own, copies, gain, *scratch)):
        parts[patch] = tokens[place * 4 + patch] + value
    load.wait()
    frame = lax.broadcasted_iota(jnp.int32, (FRAMES, 1), 0)
    begin = jnp.zeros((FRAMES, 1), jnp.int32)
    start = 0
    for clip in range(CLIPS):
        begin = jnp.where(frame >= start, start, begin)
        start = start + counts[clip]
    position = jnp.zeros((FRAMES, LANES), F32)
    for offset in range(MAXF):
        position = position + jnp.where(frame - begin == offset, placed[offset : offset + 1, :], 0.0)
    high, low = split(position)
    parts[4] = high.astype(F32)
    parts[5] = low.astype(F32)


def outer_even(counts, halo, taps, sums, own, tokens, copies, gain, placed):
    return pl.pallas_call(
        outer_even_kernel,
        out_shape=jax.ShapeDtypeStruct((6, FRAMES, LANES), F32),
        in_specs=[HBM] + [VMEM] * 8,
        out_specs=VMEM,
        scratch_shapes=outer_scratch() + [pltpu.SMEM((CLIPS,), jnp.int32), pltpu.SemaphoreType.DMA],
        compiler_params=pltpu.CompilerParams(vmem_limit_bytes=24 * MIB),
        cost_estimate=pl.CostEstimate(flops=800_000_000, bytes_accessed=4 * MIB, transcendentals=MIB // 4),
        name="outer_even",
    )(in_hbm(counts), halo, taps, sums, own, tokens, copies, gain, placed)


def outer_odd_kernel(halo, taps, sums, own, tokens, copies, gain, parts, folded, message, *scratch):
    *scratch, flat = scratch
    place = is_odd()
    mine = edge_row(place, halo, taps, sums, own, copies, gain, *scratch)
    for patch in range(4):
        mine[patch] = mine[patch] + tokens[place * 4 + patch]
    for index in range(8):
        value = jnp.where(place == index // 4, mine[index % 4], parts[index % 4])
        if index < 2:
            value = value + parts[4 + index]
        flat[pl.ds(index, FRAMES, stride=8), :] = value
    rest = jnp.broadcast_to(folded[...][None], (FRAMES, PART // 2, LANES))
    message[...] = jnp.concatenate([flat[...].reshape(FRAMES, 8, LANES), rest], axis=1).astype(BF)


def outer_odd(halo, taps, sums, own, tokens, copies, gain, parts, folded):
    return pl.pallas_call(
        outer_odd_kernel,
        out_shape=jax.ShapeDtypeStruct((FRAMES, MESSAGE, LANES), BF),
        in_specs=[VMEM] * 9,
        out_specs=VMEM,
        scratch_shapes=outer_scratch() + [pltpu.VMEM((TOKENS, LANES), F32)],
        compiler_params=pltpu.CompilerParams(vmem_limit_bytes=24 * MIB),
        cost_estimate=pl.CostEstimate(flops=800_000_000, bytes_accessed=4 * MIB, transcendentals=MIB // 4),
        name="outer_odd",
    )(halo, taps, sums, own, tokens, copies, gain, parts, folded)


GROUP = 3


def project_kernel(listed, arrived, gram, spread, out, flat, columns, shift, held, counts, load_sem, sems):
    load = pltpu.make_async_copy(listed, counts, load_sem)
    load.start()
    got = arrived[...].astype(F32)
    flat[...] = got[:, 0:8].reshape(TOKENS, LANES)
    lane = lax.broadcasted_iota(jnp.int32, (TOKENS, LANES), 1)
    token = jnp.where(lane < 64, flat[...], 0.0)
    query = (token + pltpu.roll(token, 64, 1)).astype(BF)
    rest = got[:, 8:MESSAGE]
    lane = lax.broadcasted_iota(jnp.int32, rest.shape, 2)
    low, high = jnp.where(lane < 64, rest, 0.0), jnp.where(lane < 64, 0.0, rest)
    columns[...] = jnp.concatenate([low, high], axis=1).reshape(HID, LANES).astype(BF)
    lane = lax.broadcasted_iota(jnp.int32, (FRAMES, LANES), 1)
    piece = jnp.where(
        lane < 64, pltpu.roll(flat[pl.ds(0, FRAMES, stride=8), :], 64, 1), flat[pl.ds(1, FRAMES, stride=8), :]
    )
    laid = dot(piece.astype(BF), spread[...])
    lane = lax.broadcasted_iota(jnp.int32, (8, 8 * PART), 1)
    line = lax.broadcasted_iota(jnp.int32, (8, 8 * PART), 0) * PART
    mask = (lane >= line) & (lane < line + PART)
    for block in range(8):
        shift[:, block * 8 * PART : (block + 1) * 8 * PART] = jnp.sum(
            jnp.where(mask, laid[block * 8 : (block + 1) * 8], 0.0), axis=0, keepdims=True
        )
    own = lax.axis_index("cp")
    load.wait()

    def clip(at, carry):
        start, begin = carry
        begin = jnp.where(start <= own, start, begin)
        return start + counts[at], begin

    _, begin = lax.fori_loop(0, CLIPS, clip, (0, 0))
    matrix = gram[...]
    line = lax.broadcasted_iota(jnp.int32, (16, 80), 0)
    position = jnp.sum(jnp.where(line == own - begin, matrix[64:], 0.0), axis=0, keepdims=True)
    lane = lax.broadcasted_iota(jnp.int32, (1, 80), 1)
    square = jnp.sum(jnp.where(lane == 64 + own - begin, position, 0.0), axis=1, keepdims=True)
    token = token[:, 0:64]
    total = jnp.zeros((TOKENS, 64), F32) + 2.0 * position[:, 0:64]
    matrix = matrix[:64, :64]
    for _ in range(3):
        part = matrix.astype(BF)
        total = total + dot(token.astype(BF), part)
        matrix = matrix - part.astype(F32)
    total = jnp.sum(total * token, axis=-1, keepdims=True) + square
    scale = lax.rsqrt(jnp.maximum(total, 0.0) * (1.0 / HID) + EPSILON)
    copies = []
    for group in range(HEADS // GROUP):
        at = slice(group * GROUP * HEAD_DIM, (group + 1) * GROUP * HEAD_DIM)
        value = ((nt(query, columns[at, :]) + shift[:, at]) * scale).astype(BF)
        for head in range(GROUP):
            held[group * GROUP + head] = value[:, head * HEAD_DIM : (head + 1) * HEAD_DIM]
        heads = pl.ds(group * GROUP, GROUP)
        copies.append(pltpu.make_async_copy(held.at[heads], out.at[heads], sems.at[group]))
        copies[-1].start()
    for copy in copies:
        copy.wait()


def project(counts, arrived, gram, spread):
    return pl.pallas_call(
        project_kernel,
        out_shape=jax.ShapeDtypeStruct((HEADS, TOKENS, HEAD_DIM), BF),
        in_specs=[HBM, VMEM, VMEM, VMEM],
        out_specs=HBM,
        scratch_shapes=[
            pltpu.VMEM((TOKENS, LANES), F32),
            pltpu.VMEM((HID, LANES), BF),
            pltpu.VMEM((1, HID), F32),
            pltpu.VMEM((HEADS, TOKENS, HEAD_DIM), BF),
            pltpu.SMEM((CLIPS,), jnp.int32),
            pltpu.SemaphoreType.DMA,
            pltpu.SemaphoreType.DMA((HEADS // GROUP,)),
        ],
        compiler_params=pltpu.CompilerParams(vmem_limit_bytes=24 * MIB),
        cost_estimate=pl.CostEstimate(flops=800_000_000, bytes_accessed=5 * MIB, transcendentals=0),
        name="project",
    )(in_hbm(counts), arrived, gram, spread)


def spread_table():
    table = np.zeros((LANES, 8 * PART), np.float32)
    lane = np.arange(8 * PART)
    table[lane % PART, lane] = 1.0
    table[64 + lane % PART, lane] = 1.0
    return table


def local(
    frame_rows,
    frame_counts,
    conv_weight,
    norm_gain,
    latent_proj,
    patch_weight,
    frame_embed,
    query_gain,
    query_weight,
):
    devices = lax.axis_size("cp")
    pairs = [[(i, i + 1) for i in range(begin, devices - 1, 2)] for begin in (1, 0)]
    swaps = [pair + [(j, i) for i, j in pair] for pair in pairs]
    odd_rows, even_rows, stage = fetch(frame_counts, frame_rows)
    odd_pair = lax.ppermute(odd_rows, "cp", swaps[0])
    even_pair = lax.ppermute(even_rows, "cp", swaps[1])
    sums, own, tokens, taps, copies, gain, folded, placed, gram = inner(
        stage,
        conv_weight,
        query_weight.T,
        patch_weight,
        frame_embed,
        query_gain[None, :],
        latent_proj.T,
        norm_gain[None, :],
    )
    parts = outer_even(frame_counts, even_pair, taps, sums, own, tokens, copies, gain, placed)
    message = outer_odd(odd_pair, taps, sums, own, tokens, copies, gain, parts, folded)
    arrived = lax.all_to_all(message, "cp", split_axis=0, concat_axis=0, tiled=True)
    return project(frame_counts, arrived, gram, jnp.asarray(spread_table(), BF))


def solution(mesh):
    return jax.shard_map(
        local,
        mesh=mesh,
        in_specs=(P("dp", "cp", None, None), P("dp"), P(), P(), P(), P(), P(), P(), P(None, "cp")),
        out_specs=P(None, ("dp", "cp"), None),
        check_vma=False,
    )
```

```python
import functools

import jax
import jax.numpy as jnp
import numpy as np
from jax import lax
from jax.experimental import pallas as pl
from jax.experimental.pallas import tpu as pltpu
from jax.sharding import PartitionSpec as P

LAT = 16
HID = 3072
HEAD_DIM = 128
HEADS = HID // HEAD_DIM
MAXF = 6
C = 512
WIDTH = 8
STRIP = 4
FRAMES = 64
CLIPS = 16
PART = HID // FRAMES
TOKENS = 512
LANES = 128
MESSAGE = 32
EPSILON = 1e-06
BF = jnp.bfloat16
F32 = jnp.float32
VMEM = pl.BlockSpec(memory_space=pltpu.VMEM)
SMEM = pl.BlockSpec(memory_space=pltpu.SMEM)
HBM = pl.BlockSpec(memory_space=pltpu.HBM)
MIB = 1 << 20


def in_hbm(value):
    return pltpu.with_memory_space_constraint(value, pltpu.HBM)


def nt(left, right):
    return lax.dot_general(left, right, (((1,), (1,)), ((), ())), preferred_element_type=F32)


def dot(left, right):
    return jnp.dot(left, right, preferred_element_type=F32)


def split(value):
    high = value.astype(BF)
    return high, (value - high.astype(F32)).astype(BF)


def each_clip(counts, body):
    def step(clip, start):
        body(clip, start, counts[clip])
        return start + counts[clip]

    lax.fori_loop(0, CLIPS, step, 0)


def is_odd():
    return lax.rem(lax.axis_index("cp"), 2)


def fetch_kernel(counts, frames, odd_rows, even_rows, stage, sem):
    def clip(at, start, count):
        pltpu.make_async_copy(
            frames.at[pl.ds(at * MAXF, count)], stage.at[pl.ds(start, count)], sem
        ).start()

    each_clip(counts, clip)
    pltpu.make_async_copy(stage, stage, sem).wait()
    row = is_odd() * (STRIP - 1)
    odd_rows[...] = stage[:, row]
    even_rows[...] = stage[:, STRIP - 1 - row]


def fetch(counts, frames):
    return pl.pallas_call(
        fetch_kernel,
        out_shape=(
            pltpu.VMEM((FRAMES, WIDTH, C), BF),
            pltpu.VMEM((FRAMES, WIDTH, C), BF),
            pltpu.VMEM((FRAMES, STRIP, WIDTH, C), BF),
        ),
        in_specs=[SMEM, HBM],
        out_specs=(VMEM,) * 3,
        scratch_shapes=[pltpu.SemaphoreType.DMA],
        cost_estimate=pl.CostEstimate(flops=0, bytes_accessed=4 * MIB, transcendentals=0),
        name="fetch",
    )(in_hbm(counts), in_hbm(frames))


def latent_of(summed, frame, gain, proj):
    residual = frame.astype(F32) + 0.5 * summed * (1.0 + jnp.tanh(0.5 * summed))
    mean = jnp.mean(residual * residual, axis=-1, keepdims=True)
    normed = (residual * lax.rsqrt(mean + EPSILON) * gain).astype(BF)
    return nt(normed, proj)


def in_patch(latent, below):
    lane = lax.broadcasted_iota(jnp.int32, (FRAMES, LANES), 1) // LAT
    tokens = []
    for patch in range(WIDTH // 2):
        total = jnp.zeros((FRAMES, LANES), F32)
        for side in range(2):
            column = 2 * patch + side
            block = latent[column * FRAMES : (column + 1) * FRAMES]
            total = total + jnp.where(lane == below * 2 + side, block, 0.0)
        tokens.append(total)
    return tokens


def spread_proj(proj, copies):
    copies[...] = jnp.zeros_like(copies)
    for copy in range(4):
        copies[copy * LAT : (copy + 1) * LAT, :] = proj[...]


def by_column(row, wide, cols, lane):
    row = row.astype(F32).reshape(FRAMES * WIDTH, C)
    for piece in range(C // LANES):
        wide[piece] = row[:, piece * LANES : (piece + 1) * LANES]
    for column in range(WIDTH):
        blocks = [wide[piece, pl.ds(column, FRAMES, stride=WIDTH), :] for piece in range(C // LANES)]
        block = jnp.concatenate(blocks, axis=1).astype(BF)
        cols[column * FRAMES : (column + 1) * FRAMES, lane : lane + C] = block


def inner_kernel(
    stage,
    weight,
    proj,
    gain,
    sums,
    own,
    tokens,
    taps,
    copies,
    norm,
    wide,
    cols,
    total,
    projs,
    small_sems,
    sems,
):
    small = [
        pltpu.make_async_copy(source, target, small_sems.at[place])
        for place, (source, target) in enumerate(((proj, projs), (gain, norm)))
    ]
    order = (1, 0, 2)
    loads = {}
    for side in order:
        for row in (1, 2, 0):
            loads[side, row] = pltpu.make_async_copy(
                weight.at[row, side], taps.at[side, pl.ds(row * C, C)], sems.at[side, row]
            )
            loads[side, row].start()
    for copy in small:
        copy.start()
    for row in range(STRIP):
        by_column(stage[:, row], wide.at[row], cols, row * C)
    for place, row in enumerate((0, STRIP - 1)):
        own[place] = cols[:, row * C : (row + 1) * C]
    count = FRAMES * WIDTH
    for side in order:
        begin, end = max(0, side - 1) * FRAMES, count - max(0, 1 - side) * FRAMES
        shift = (1 - side) * FRAMES
        for row in range(STRIP):
            low, high = max(row - 1, 0), min(row + 2, STRIP)
            for tap in ((1, 2), (0,), (), ())[row]:
                loads[side, tap].wait()
            skip = low - (row - 1)
            part = dot(
                cols[begin:end, low * C : high * C],
                taps[side, skip * C : (skip + high - low) * C, :],
            )
            target = sums.at[row // 2] if row in (0, STRIP - 1) else total.at[row - 1]
            if side == 1:
                target[...] = part
            else:
                target[begin + shift : end + shift, :] += part
    for copy in small:
        copy.wait()
    spread_proj(projs, copies)
    for row in (1, 2):
        latent = latent_of(total[row - 1], cols[:, row * C : (row + 1) * C], norm[...], copies[...])
        for patch_index, value in enumerate(in_patch(latent, row % 2)):
            tokens[(row // 2) * 4 + patch_index] = value


def inner(stage, *operands):
    return pl.pallas_call(
        inner_kernel,
        out_shape=(
            jax.ShapeDtypeStruct((2, FRAMES * WIDTH, C), F32),
            jax.ShapeDtypeStruct((2, FRAMES * WIDTH, C), BF),
            jax.ShapeDtypeStruct((8, FRAMES, LANES), F32),
            jax.ShapeDtypeStruct((3, 3 * C, C), BF),
            jax.ShapeDtypeStruct((LANES, C), BF),
            jax.ShapeDtypeStruct((1, C), F32),
        ),
        in_specs=[VMEM] + [HBM] * 3,
        out_specs=(VMEM,) * 6,
        scratch_shapes=[
            pltpu.VMEM((STRIP, C // LANES, FRAMES * WIDTH, LANES), F32),
            pltpu.VMEM((FRAMES * WIDTH, STRIP * C), BF),
            pltpu.VMEM((2, FRAMES * WIDTH, C), F32),
            pltpu.VMEM((LAT, C), BF),
            pltpu.SemaphoreType.DMA((2,)),
            pltpu.SemaphoreType.DMA((3, 3)),
        ],
        compiler_params=pltpu.CompilerParams(vmem_limit_bytes=32 * MIB),
        cost_estimate=pl.CostEstimate(flops=8_000_000_000, bytes_accessed=9 * MIB, transcendentals=MIB // 2),
        name="inner",
    )(stage, *map(in_hbm, operands))


def edge_row(place, halo, taps, sums, own, copies, gain, wide, cols, total):
    count = FRAMES * WIDTH
    tap = pl.multiple_of(place * 2 * C, C)
    by_column(halo[...], wide, cols, 0)
    total[...] = sums[place]
    for side in (1, 0, 2):
        begin, end = max(0, side - 1) * FRAMES, count - max(0, 1 - side) * FRAMES
        shift = (1 - side) * FRAMES
        total[begin + shift : end + shift, :] += dot(cols[begin:end], taps[side, pl.ds(tap, C), :])
    latent = latent_of(total[...], own[place], gain[...], copies[...])
    return in_patch(latent, place)


def outer_scratch():
    return [
        pltpu.VMEM((C // LANES, FRAMES * WIDTH, LANES), F32),
        pltpu.VMEM((FRAMES * WIDTH, C), BF),
        pltpu.VMEM((FRAMES * WIDTH, C), F32),
    ]


def outer_even_kernel(listed, halo, taps, sums, own, tokens, copies, gain, placed, parts, *scratch):
    *scratch, counts, sem = scratch
    load = pltpu.make_async_copy(listed, counts, sem)
    load.start()
    place = 1 - is_odd()
    for patch, value in enumerate(edge_row(place, halo, taps, sums, own, copies, gain, *scratch)):
        parts[patch] = tokens[place * 4 + patch] + value
    load.wait()
    frame = lax.broadcasted_iota(jnp.int32, (FRAMES, 1), 0)
    begin = jnp.zeros((FRAMES, 1), jnp.int32)
    start = 0
    for clip in range(CLIPS):
        begin = jnp.where(frame >= start, start, begin)
        start = start + counts[clip]
    position = jnp.zeros((FRAMES, LANES), F32)
    for offset in range(MAXF):
        position = position + jnp.where(frame - begin == offset, placed[offset : offset + 1, :], 0.0)
    high, low = split(position)
    parts[4] = high.astype(F32)
    parts[5] = low.astype(F32)


def outer_even(counts, halo, taps, sums, own, tokens, copies, gain, placed):
    return pl.pallas_call(
        outer_even_kernel,
        out_shape=jax.ShapeDtypeStruct((6, FRAMES, LANES), F32),
        in_specs=[HBM] + [VMEM] * 8,
        out_specs=VMEM,
        scratch_shapes=outer_scratch() + [pltpu.SMEM((CLIPS,), jnp.int32), pltpu.SemaphoreType.DMA],
        compiler_params=pltpu.CompilerParams(vmem_limit_bytes=24 * MIB),
        cost_estimate=pl.CostEstimate(flops=800_000_000, bytes_accessed=4 * MIB, transcendentals=MIB // 4),
        name="outer_even",
    )(in_hbm(counts), halo, taps, sums, own, tokens, copies, gain, placed)


def outer_odd_kernel(halo, taps, sums, own, tokens, copies, gain, parts, folded, message, *scratch):
    *scratch, flat = scratch
    place = is_odd()
    mine = edge_row(place, halo, taps, sums, own, copies, gain, *scratch)
    for patch in range(4):
        mine[patch] = mine[patch] + tokens[place * 4 + patch]
    for index in range(8):
        value = jnp.where(place == index // 4, mine[index % 4], parts[index % 4])
        if index < 2:
            value = value + parts[4 + index]
        flat[pl.ds(index, FRAMES, stride=8), :] = value
    rest = jnp.broadcast_to(folded[...][None], (FRAMES, PART // 2, LANES))
    message[...] = jnp.concatenate([flat[...].reshape(FRAMES, 8, LANES), rest], axis=1).astype(BF)


def outer_odd(halo, taps, sums, own, tokens, copies, gain, parts, folded):
    return pl.pallas_call(
        outer_odd_kernel,
        out_shape=jax.ShapeDtypeStruct((FRAMES, MESSAGE, LANES), BF),
        in_specs=[VMEM] * 9,
        out_specs=VMEM,
        scratch_shapes=outer_scratch() + [pltpu.VMEM((TOKENS, LANES), F32)],
        compiler_params=pltpu.CompilerParams(vmem_limit_bytes=24 * MIB),
        cost_estimate=pl.CostEstimate(flops=800_000_000, bytes_accessed=4 * MIB, transcendentals=MIB // 4),
        name="outer_odd",
    )(halo, taps, sums, own, tokens, copies, gain, parts, folded)


def fold_kernel(after, counts, columns, patch, embed, scale, folded, placed, gram, added, table, rows):
    del after
    table[0:64, :] = patch[...]
    table[64:80, :] = jnp.concatenate(
        [embed[...].astype(F32), jnp.zeros((16 - MAXF, HID), F32)], axis=0
    ).astype(BF)
    high, low = split(table[...].astype(F32) * scale[...])
    rows[0:64, :] = high[:64]
    rows[64:128, :] = low[:64]
    rows[128:144, :] = high[64:]
    rows[144:160, :] = low[64:]
    product = nt(rows[...], columns[...])
    product = jnp.concatenate([product, jnp.zeros((160, LANES - PART), F32)], axis=1)
    both = (product[:64] + product[64:128]).T
    both = jnp.concatenate([both, both], axis=1)
    lane = lax.broadcasted_iota(jnp.int32, (PART // 2, LANES), 1)
    folded[...] = jnp.where(lane < 64, both[: PART // 2], both[PART // 2 : PART])
    placed[...] = pltpu.roll(product[128:144] + product[144:160], 64, 1)
    product = nt(table[...], table[...])
    matrix = product[:64, :64]
    for part in range(3):
        piece = matrix.astype(BF)
        gram[part] = piece
        matrix = matrix - piece.astype(F32)
    own = lax.axis_index("cp")

    def clip(at, carry):
        start, begin = carry
        begin = jnp.where(start <= own, start, begin)
        return start + counts[at], begin

    _, begin = lax.fori_loop(0, CLIPS, clip, (0, 0))
    line = lax.broadcasted_iota(jnp.int32, (16, 80), 0)
    position = jnp.sum(jnp.where(line == own - begin, product[64:], 0.0), axis=0, keepdims=True)
    lane = lax.broadcasted_iota(jnp.int32, (1, 80), 1)
    square = jnp.sum(jnp.where(lane == 64 + own - begin, position, 0.0), axis=1, keepdims=True)
    added[0:1, :] = 2.0 * position[:, :64]
    added[1:2, :] = jnp.broadcast_to(square, (1, 64))


def fold(after, counts, columns, patch, embed, scale):
    return pl.pallas_call(
        fold_kernel,
        out_shape=(
            jax.ShapeDtypeStruct((PART // 2, LANES), F32),
            jax.ShapeDtypeStruct((16, LANES), F32),
            jax.ShapeDtypeStruct((3, 64, 64), BF),
            jax.ShapeDtypeStruct((2, 64), F32),
        ),
        in_specs=[VMEM, SMEM] + [VMEM] * 4,
        out_specs=(VMEM,) * 4,
        scratch_shapes=[pltpu.VMEM((80, HID), BF), pltpu.VMEM((160, HID), BF)],
        compiler_params=pltpu.CompilerParams(vmem_limit_bytes=8 * MIB),
        cost_estimate=pl.CostEstimate(flops=1_000_000_000, bytes_accessed=MIB, transcendentals=0),
        name="fold",
    )(after, counts, columns, patch, embed, scale)


GROUP = 3


def project_kernel(arrived, gram, added, spread, out, flat, columns, shift, held, sems):
    got = arrived[...].astype(F32)
    flat[...] = got[:, 0:8].reshape(TOKENS, LANES)
    lane = lax.broadcasted_iota(jnp.int32, (TOKENS, LANES), 1)
    token = jnp.where(lane < 64, flat[...], 0.0)
    query = (token + pltpu.roll(token, 64, 1)).astype(BF)
    rest = got[:, 8:MESSAGE]
    lane = lax.broadcasted_iota(jnp.int32, rest.shape, 2)
    low, high = jnp.where(lane < 64, rest, 0.0), jnp.where(lane < 64, 0.0, rest)
    columns[...] = jnp.concatenate([low, high], axis=1).reshape(HID, LANES).astype(BF)
    lane = lax.broadcasted_iota(jnp.int32, (FRAMES, LANES), 1)
    piece = jnp.where(
        lane < 64, pltpu.roll(flat[pl.ds(0, FRAMES, stride=8), :], 64, 1), flat[pl.ds(1, FRAMES, stride=8), :]
    )
    laid = dot(piece.astype(BF), spread[...])
    lane = lax.broadcasted_iota(jnp.int32, (8, 8 * PART), 1)
    line = lax.broadcasted_iota(jnp.int32, (8, 8 * PART), 0) * PART
    mask = (lane >= line) & (lane < line + PART)
    for block in range(8):
        shift[:, block * 8 * PART : (block + 1) * 8 * PART] = jnp.sum(
            jnp.where(mask, laid[block * 8 : (block + 1) * 8], 0.0), axis=0, keepdims=True
        )
    token = token[:, 0:64]
    total = jnp.zeros((TOKENS, 64), F32) + added[0:1, :]
    for part in range(3):
        total = total + dot(token.astype(BF), gram[part])
    total = jnp.sum(total * token, axis=-1, keepdims=True) + added[1:2, 0:1]
    scale = lax.rsqrt(jnp.maximum(total, 0.0) * (1.0 / HID) + EPSILON)
    copies = []
    for group in range(HEADS // GROUP):
        at = slice(group * GROUP * HEAD_DIM, (group + 1) * GROUP * HEAD_DIM)
        value = ((nt(query, columns[at, :]) + shift[:, at]) * scale).astype(BF)
        for head in range(GROUP):
            held[group * GROUP + head] = value[:, head * HEAD_DIM : (head + 1) * HEAD_DIM]
        heads = pl.ds(group * GROUP, GROUP)
        copies.append(pltpu.make_async_copy(held.at[heads], out.at[heads], sems.at[group]))
        copies[-1].start()
    for copy in copies:
        copy.wait()


def project(arrived, gram, added, spread):
    return pl.pallas_call(
        project_kernel,
        out_shape=jax.ShapeDtypeStruct((HEADS, TOKENS, HEAD_DIM), BF),
        in_specs=[VMEM] * 4,
        out_specs=HBM,
        scratch_shapes=[
            pltpu.VMEM((TOKENS, LANES), F32),
            pltpu.VMEM((HID, LANES), BF),
            pltpu.VMEM((1, HID), F32),
            pltpu.VMEM((HEADS, TOKENS, HEAD_DIM), BF),
            pltpu.SemaphoreType.DMA((HEADS // GROUP,)),
        ],
        compiler_params=pltpu.CompilerParams(vmem_limit_bytes=24 * MIB),
        cost_estimate=pl.CostEstimate(flops=800_000_000, bytes_accessed=5 * MIB, transcendentals=0),
        name="project",
    )(arrived, gram, added, spread)


def spread_table():
    table = np.zeros((LANES, 8 * PART), np.float32)
    lane = np.arange(8 * PART)
    table[lane % PART, lane] = 1.0
    table[64 + lane % PART, lane] = 1.0
    return table


def local(
    frame_rows,
    frame_counts,
    conv_weight,
    norm_gain,
    latent_proj,
    patch_weight,
    frame_embed,
    query_gain,
    query_weight,
):
    devices = lax.axis_size("cp")
    pairs = [[(i, i + 1) for i in range(begin, devices - 1, 2)] for begin in (1, 0)]
    swaps = [pair + [(j, i) for i, j in pair] for pair in pairs]
    odd_rows, even_rows, stage = fetch(frame_counts, frame_rows)
    even_pair = lax.ppermute(even_rows, "cp", swaps[1])
    odd_pair = lax.ppermute(odd_rows, "cp", swaps[0])
    sums, own, tokens, taps, copies, gain = inner(
        stage, conv_weight, latent_proj.T, norm_gain[None, :]
    )
    folded, placed, gram, added = fold(
        gain, frame_counts, query_weight.T, patch_weight, frame_embed, query_gain[None, :]
    )
    parts = outer_even(frame_counts, even_pair, taps, sums, own, tokens, copies, gain, placed)
    message = outer_odd(odd_pair, taps, sums, own, tokens, copies, gain, parts, folded)
    arrived = lax.all_to_all(message, "cp", split_axis=0, concat_axis=0, tiled=True)
    return project(arrived, gram, added, jnp.asarray(spread_table(), BF))


def solution(mesh):
    return jax.shard_map(
        local,
        mesh=mesh,
        in_specs=(P("dp", "cp", None, None), P("dp"), P(), P(), P(), P(), P(), P(), P(None, "cp")),
        out_specs=P(None, ("dp", "cp"), None),
        check_vma=False,
    )
```

```python
import functools

import jax
import jax.numpy as jnp
import numpy as np
from jax import lax
from jax.experimental import pallas as pl
from jax.experimental.pallas import tpu as pltpu
from jax.sharding import PartitionSpec as P

LAT = 16
HID = 3072
HEAD_DIM = 128
HEADS = HID // HEAD_DIM
MAXF = 6
C = 512
WIDTH = 8
STRIP = 4
FRAMES = 64
CLIPS = 16
PART = HID // FRAMES
TOKENS = 512
LANES = 128
MESSAGE = 32
EPSILON = 1e-06
BF = jnp.bfloat16
F32 = jnp.float32
VMEM = pl.BlockSpec(memory_space=pltpu.VMEM)
SMEM = pl.BlockSpec(memory_space=pltpu.SMEM)
HBM = pl.BlockSpec(memory_space=pltpu.HBM)
MIB = 1 << 20


def in_hbm(value):
    return pltpu.with_memory_space_constraint(value, pltpu.HBM)


def nt(left, right):
    return lax.dot_general(left, right, (((1,), (1,)), ((), ())), preferred_element_type=F32)


def dot(left, right):
    return jnp.dot(left, right, preferred_element_type=F32)


def split(value):
    high = value.astype(BF)
    return high, (value - high.astype(F32)).astype(BF)


def each_clip(counts, body):
    start = 0
    for clip in range(CLIPS):
        body(clip, start, counts[clip])
        start = start + counts[clip]


def is_odd():
    return lax.rem(lax.axis_index("cp"), 2)


def fetch_kernel(counts, frames, odd_rows, even_rows, stage, sem):
    def clip(at, start, count):
        pltpu.make_async_copy(
            frames.at[pl.ds(at * MAXF, count)], stage.at[pl.ds(start, count)], sem
        ).start()

    each_clip(counts, clip)
    pltpu.make_async_copy(stage, stage, sem).wait()
    row = is_odd() * (STRIP - 1)
    odd_rows[...] = stage[:, row]
    even_rows[...] = stage[:, STRIP - 1 - row]


def fetch(counts, frames):
    return pl.pallas_call(
        fetch_kernel,
        out_shape=(
            pltpu.VMEM((FRAMES, WIDTH, C), BF),
            pltpu.VMEM((FRAMES, WIDTH, C), BF),
            pltpu.VMEM((FRAMES, STRIP, WIDTH, C), BF),
        ),
        in_specs=[SMEM, HBM],
        out_specs=(VMEM,) * 3,
        scratch_shapes=[pltpu.SemaphoreType.DMA],
        cost_estimate=pl.CostEstimate(flops=0, bytes_accessed=4 * MIB, transcendentals=0),
        name="fetch",
    )(in_hbm(counts), in_hbm(frames))


def latent_of(summed, frame, gain, proj):
    residual = frame.astype(F32) + 0.5 * summed * (1.0 + jnp.tanh(0.5 * summed))
    mean = jnp.mean(residual * residual, axis=-1, keepdims=True)
    normed = (residual * lax.rsqrt(mean + EPSILON) * gain).astype(BF)
    return dot(normed, proj)


def in_patch(latent, below):
    lane = lax.broadcasted_iota(jnp.int32, (FRAMES, LANES), 1) // LAT
    tokens = []
    for patch in range(WIDTH // 2):
        total = jnp.zeros((FRAMES, LANES), F32)
        for side in range(2):
            column = 2 * patch + side
            block = latent[column * FRAMES : (column + 1) * FRAMES]
            total = total + jnp.where(lane == below * 2 + side, block, 0.0)
        tokens.append(total)
    return tokens


def spread_proj(proj, copies):
    four = jnp.concatenate([proj[...].astype(F32)] * 4 + [jnp.zeros((LANES - 4 * LAT, C), F32)], axis=0)
    copies[...] = four.T.astype(BF)


def by_column(row, wide, cols, lane):
    row = row.astype(F32).reshape(FRAMES * WIDTH, C)
    for piece in range(C // LANES):
        wide[piece] = row[:, piece * LANES : (piece + 1) * LANES]
    for column in range(WIDTH):
        blocks = [wide[piece, pl.ds(column, FRAMES, stride=WIDTH), :] for piece in range(C // LANES)]
        block = jnp.concatenate(blocks, axis=1).astype(BF)
        cols[column * FRAMES : (column + 1) * FRAMES, lane : lane + C] = block


def inner_kernel(
    stage,
    weight,
    proj,
    gain,
    sums,
    own,
    tokens,
    taps,
    copies,
    norm,
    wide,
    cols,
    total,
    projs,
    small_sems,
    sems,
):
    small = [
        pltpu.make_async_copy(source, target, small_sems.at[place])
        for place, (source, target) in enumerate(((proj, projs), (gain, norm)))
    ]
    order = (1, 0, 2)
    loads = {}
    for side in order:
        for row in (1, 2, 0):
            loads[side, row] = pltpu.make_async_copy(
                weight.at[row, side], taps.at[side, pl.ds(row * C, C)], sems.at[side, row]
            )
            loads[side, row].start()
    for copy in small:
        copy.start()
    for row in range(STRIP):
        by_column(stage[:, row], wide.at[row], cols, row * C)
    for place, row in enumerate((0, STRIP - 1)):
        own[place] = cols[:, row * C : (row + 1) * C]
    count = FRAMES * WIDTH
    for side in order:
        begin, end = max(0, side - 1) * FRAMES, count - max(0, 1 - side) * FRAMES
        shift = (1 - side) * FRAMES
        for row in range(STRIP):
            low, high = max(row - 1, 0), min(row + 2, STRIP)
            for tap in ((1, 2), (0,), (), ())[row]:
                loads[side, tap].wait()
            skip = low - (row - 1)
            part = dot(
                cols[begin:end, low * C : high * C],
                taps[side, skip * C : (skip + high - low) * C, :],
            )
            target = sums.at[row // 2] if row in (0, STRIP - 1) else total.at[row - 1]
            if side == 1:
                target[...] = part
            else:
                target[begin + shift : end + shift, :] += part
    for copy in small:
        copy.wait()
    spread_proj(projs, copies)
    for row in (1, 2):
        latent = latent_of(total[row - 1], cols[:, row * C : (row + 1) * C], norm[...], copies[...])
        for patch_index, value in enumerate(in_patch(latent, row % 2)):
            tokens[(row // 2) * 4 + patch_index] = value


def inner(stage, *operands):
    return pl.pallas_call(
        inner_kernel,
        out_shape=(
            jax.ShapeDtypeStruct((2, FRAMES * WIDTH, C), F32),
            jax.ShapeDtypeStruct((2, FRAMES * WIDTH, C), BF),
            jax.ShapeDtypeStruct((8, FRAMES, LANES), F32),
            jax.ShapeDtypeStruct((3, 3 * C, C), BF),
            jax.ShapeDtypeStruct((C, LANES), BF),
            jax.ShapeDtypeStruct((1, C), F32),
        ),
        in_specs=[VMEM] + [HBM] * 3,
        out_specs=(VMEM,) * 6,
        scratch_shapes=[
            pltpu.VMEM((STRIP, C // LANES, FRAMES * WIDTH, LANES), F32),
            pltpu.VMEM((FRAMES * WIDTH, STRIP * C), BF),
            pltpu.VMEM((2, FRAMES * WIDTH, C), F32),
            pltpu.VMEM((LAT, C), BF),
            pltpu.SemaphoreType.DMA((2,)),
            pltpu.SemaphoreType.DMA((3, 3)),
        ],
        compiler_params=pltpu.CompilerParams(vmem_limit_bytes=32 * MIB),
        cost_estimate=pl.CostEstimate(flops=8_000_000_000, bytes_accessed=9 * MIB, transcendentals=MIB // 2),
        name="inner",
    )(stage, *map(in_hbm, operands))


def edge_row(place, halo, taps, sums, own, copies, gain, wide, cols, total):
    count = FRAMES * WIDTH
    tap = pl.multiple_of(place * 2 * C, C)
    by_column(halo[...], wide, cols, 0)
    total[...] = sums[place]
    for side in (1, 0, 2):
        begin, end = max(0, side - 1) * FRAMES, count - max(0, 1 - side) * FRAMES
        shift = (1 - side) * FRAMES
        total[begin + shift : end + shift, :] += dot(cols[begin:end], taps[side, pl.ds(tap, C), :])
    latent = latent_of(total[...], own[place], gain[...], copies[...])
    return in_patch(latent, place)


def outer_scratch():
    return [
        pltpu.VMEM((C // LANES, FRAMES * WIDTH, LANES), F32),
        pltpu.VMEM((FRAMES * WIDTH, C), BF),
        pltpu.VMEM((FRAMES * WIDTH, C), F32),
    ]


def outer_even_kernel(listed, halo, taps, sums, own, tokens, copies, gain, placed, parts, *scratch):
    *scratch, counts, sem = scratch
    load = pltpu.make_async_copy(listed, counts, sem)
    load.start()
    place = 1 - is_odd()
    for patch, value in enumerate(edge_row(place, halo, taps, sums, own, copies, gain, *scratch)):
        parts[patch] = tokens[place * 4 + patch] + value
    load.wait()
    frame = lax.broadcasted_iota(jnp.int32, (FRAMES, 1), 0)
    begin = jnp.zeros((FRAMES, 1), jnp.int32)
    start = 0
    for clip in range(CLIPS):
        begin = jnp.where(frame >= start, start, begin)
        start = start + counts[clip]
    position = jnp.zeros((FRAMES, LANES), F32)
    for offset in range(MAXF):
        position = position + jnp.where(frame - begin == offset, placed[offset : offset + 1, :], 0.0)
    high, low = split(position)
    parts[4] = high.astype(F32)
    parts[5] = low.astype(F32)


def outer_even(counts, halo, taps, sums, own, tokens, copies, gain, placed):
    return pl.pallas_call(
        outer_even_kernel,
        out_shape=jax.ShapeDtypeStruct((6, FRAMES, LANES), F32),
        in_specs=[HBM] + [VMEM] * 8,
        out_specs=VMEM,
        scratch_shapes=outer_scratch() + [pltpu.SMEM((CLIPS,), jnp.int32), pltpu.SemaphoreType.DMA],
        compiler_params=pltpu.CompilerParams(vmem_limit_bytes=24 * MIB),
        cost_estimate=pl.CostEstimate(flops=800_000_000, bytes_accessed=4 * MIB, transcendentals=MIB // 4),
        name="outer_even",
    )(in_hbm(counts), halo, taps, sums, own, tokens, copies, gain, placed)


def outer_odd_kernel(halo, taps, sums, own, tokens, copies, gain, parts, folded, message, *scratch):
    *scratch, flat = scratch
    place = is_odd()
    mine = edge_row(place, halo, taps, sums, own, copies, gain, *scratch)
    for patch in range(4):
        mine[patch] = mine[patch] + tokens[place * 4 + patch]
    for index in range(8):
        value = jnp.where(place == index // 4, mine[index % 4], parts[index % 4])
        if index < 2:
            value = value + parts[4 + index]
        flat[pl.ds(index, FRAMES, stride=8), :] = value
    rest = jnp.broadcast_to(folded[...][None], (FRAMES, PART // 2, LANES))
    message[...] = jnp.concatenate([flat[...].reshape(FRAMES, 8, LANES), rest], axis=1).astype(BF)


def outer_odd(halo, taps, sums, own, tokens, copies, gain, parts, folded):
    return pl.pallas_call(
        outer_odd_kernel,
        out_shape=jax.ShapeDtypeStruct((FRAMES, MESSAGE, LANES), BF),
        in_specs=[VMEM] * 9,
        out_specs=VMEM,
        scratch_shapes=outer_scratch() + [pltpu.VMEM((TOKENS, LANES), F32)],
        compiler_params=pltpu.CompilerParams(vmem_limit_bytes=24 * MIB),
        cost_estimate=pl.CostEstimate(flops=800_000_000, bytes_accessed=4 * MIB, transcendentals=MIB // 4),
        name="outer_odd",
    )(halo, taps, sums, own, tokens, copies, gain, parts, folded)


def fold_kernel(after, listed, columns, patch, embed, scale, folded, placed, gram, added, table, rows, counts, sem):
    del after
    load = pltpu.make_async_copy(listed, counts, sem)
    load.start()
    table[0:64, :] = patch[...]
    table[64:80, :] = jnp.concatenate(
        [embed[...].astype(F32), jnp.zeros((16 - MAXF, HID), F32)], axis=0
    ).astype(BF)
    high, low = split(table[...].astype(F32) * scale[...])
    rows[0:64, :] = high[:64]
    rows[64:128, :] = low[:64]
    rows[128:144, :] = high[64:]
    rows[144:160, :] = low[64:]
    product = nt(rows[...], columns[...])
    product = jnp.concatenate([product, jnp.zeros((160, LANES - PART), F32)], axis=1)
    both = (product[:64] + product[64:128]).T
    both = jnp.concatenate([both, both], axis=1)
    lane = lax.broadcasted_iota(jnp.int32, (PART // 2, LANES), 1)
    folded[...] = jnp.where(lane < 64, both[: PART // 2], both[PART // 2 : PART])
    placed[...] = pltpu.roll(product[128:144] + product[144:160], 64, 1)
    product = nt(table[...], table[...])
    matrix = product[:64, :64]
    pieces = []
    for _ in range(3):
        pieces.append(matrix.astype(BF).astype(F32))
        matrix = matrix - pieces[-1]
    pieces = jnp.concatenate([*pieces, jnp.zeros((64, 64), F32)], axis=1)
    gram[...] = jnp.concatenate([pieces, jnp.zeros((64, 256), F32)], axis=0).astype(BF)
    own = lax.axis_index("cp")
    load.wait()
    start, begin = 0, 0
    for clip in range(CLIPS):
        begin = jnp.where(start <= own, start, begin)
        start = start + counts[clip]
    line = lax.broadcasted_iota(jnp.int32, (16, 80), 0)
    position = jnp.sum(jnp.where(line == own - begin, product[64:], 0.0), axis=0, keepdims=True)
    lane = lax.broadcasted_iota(jnp.int32, (1, 80), 1)
    square = jnp.sum(jnp.where(lane == 64 + own - begin, position, 0.0), axis=1, keepdims=True)
    added[0:1, :] = jnp.concatenate([2.0 * position[:, :64], jnp.zeros((1, 64), F32)], axis=1)
    added[1:2, :] = jnp.broadcast_to(square, (1, LANES))


def fold(after, counts, columns, patch, embed, scale):
    return pl.pallas_call(
        fold_kernel,
        out_shape=(
            jax.ShapeDtypeStruct((PART // 2, LANES), F32),
            jax.ShapeDtypeStruct((16, LANES), F32),
            jax.ShapeDtypeStruct((LANES, 256), BF),
            jax.ShapeDtypeStruct((2, LANES), F32),
        ),
        in_specs=[VMEM, HBM] + [VMEM] * 4,
        out_specs=(VMEM,) * 4,
        scratch_shapes=[
            pltpu.VMEM((80, HID), BF),
            pltpu.VMEM((160, HID), BF),
            pltpu.SMEM((CLIPS,), jnp.int32),
            pltpu.SemaphoreType.DMA,
        ],
        compiler_params=pltpu.CompilerParams(vmem_limit_bytes=8 * MIB),
        cost_estimate=pl.CostEstimate(flops=1_000_000_000, bytes_accessed=MIB, transcendentals=0),
        name="fold",
    )(after, in_hbm(counts), columns, patch, embed, scale)


GROUP = 4


def project_kernel(arrived, gram, added, spread, out, flat, columns, shift, held, sems):
    got = arrived[...].astype(F32)
    flat[...] = got[:, 0:8].reshape(TOKENS, LANES)
    lane = lax.broadcasted_iota(jnp.int32, (TOKENS, LANES), 1)
    token = jnp.where(lane < 64, flat[...], 0.0)
    token = token + pltpu.roll(token, 64, 1)
    query = token.astype(BF)
    product = dot(query, gram[...])
    total = (product[:, :LANES] + product[:, LANES:] + added[0:1, :]) * token
    total = jnp.sum(total, axis=-1, keepdims=True) + added[1:2, 0:1]
    scale = lax.rsqrt(jnp.maximum(total, 0.0) * (1.0 / HID) + EPSILON)
    rest = got[:, 8:MESSAGE]
    lane = lax.broadcasted_iota(jnp.int32, rest.shape, 2)
    low, high = jnp.where(lane < 64, rest, 0.0), jnp.where(lane < 64, 0.0, rest)
    columns[...] = jnp.concatenate([low, high], axis=1).reshape(HID, LANES).astype(BF)
    lane = lax.broadcasted_iota(jnp.int32, (FRAMES, LANES), 1)
    piece = jnp.where(
        lane < 64, pltpu.roll(flat[pl.ds(0, FRAMES, stride=8), :], 64, 1), flat[pl.ds(1, FRAMES, stride=8), :]
    )
    laid = dot(piece.astype(BF), spread[...])
    lane = lax.broadcasted_iota(jnp.int32, (8, 8 * PART), 1)
    line = lax.broadcasted_iota(jnp.int32, (8, 8 * PART), 0) * PART
    mask = (lane >= line) & (lane < line + PART)
    for block in range(8):
        shift[:, block * 8 * PART : (block + 1) * 8 * PART] = jnp.sum(
            jnp.where(mask, laid[block * 8 : (block + 1) * 8], 0.0), axis=0, keepdims=True
        )
    copies = []
    for group in range(HEADS // GROUP):
        at = slice(group * GROUP * HEAD_DIM, (group + 1) * GROUP * HEAD_DIM)
        value = ((nt(query, columns[at, :]) + shift[:, at]) * scale).astype(BF)
        for head in range(GROUP):
            held[group * GROUP + head] = value[:, head * HEAD_DIM : (head + 1) * HEAD_DIM]
        heads = pl.ds(group * GROUP, GROUP)
        copies.append(pltpu.make_async_copy(held.at[heads], out.at[heads], sems.at[group]))
        copies[-1].start()
    for copy in copies:
        copy.wait()


def project(arrived, gram, added, spread):
    return pl.pallas_call(
        project_kernel,
        out_shape=jax.ShapeDtypeStruct((HEADS, TOKENS, HEAD_DIM), BF),
        in_specs=[VMEM] * 4,
        out_specs=HBM,
        scratch_shapes=[
            pltpu.VMEM((TOKENS, LANES), F32),
            pltpu.VMEM((HID, LANES), BF),
            pltpu.VMEM((1, HID), F32),
            pltpu.VMEM((HEADS, TOKENS, HEAD_DIM), BF),
            pltpu.SemaphoreType.DMA((HEADS // GROUP,)),
        ],
        compiler_params=pltpu.CompilerParams(vmem_limit_bytes=24 * MIB),
        cost_estimate=pl.CostEstimate(flops=800_000_000, bytes_accessed=5 * MIB, transcendentals=0),
        name="project",
    )(arrived, gram, added, spread)


def spread_table():
    table = np.zeros((LANES, 8 * PART), np.float32)
    lane = np.arange(8 * PART)
    table[lane % PART, lane] = 1.0
    table[64 + lane % PART, lane] = 1.0
    return table


def local(
    frame_rows,
    frame_counts,
    conv_weight,
    norm_gain,
    latent_proj,
    patch_weight,
    frame_embed,
    query_gain,
    query_weight,
):
    devices = lax.axis_size("cp")
    pairs = [[(i, i + 1) for i in range(begin, devices - 1, 2)] for begin in (1, 0)]
    swaps = [pair + [(j, i) for i, j in pair] for pair in pairs]
    odd_rows, even_rows, stage = fetch(frame_counts, frame_rows)
    even_pair = lax.ppermute(even_rows, "cp", swaps[1])
    odd_pair = lax.ppermute(odd_rows, "cp", swaps[0])
    sums, own, tokens, taps, copies, gain = inner(
        stage, conv_weight, latent_proj.T, norm_gain[None, :]
    )
    folded, placed, gram, added = fold(
        gain, frame_counts, query_weight.T, patch_weight, frame_embed, query_gain[None, :]
    )
    parts = outer_even(frame_counts, even_pair, taps, sums, own, tokens, copies, gain, placed)
    message = outer_odd(odd_pair, taps, sums, own, tokens, copies, gain, parts, folded)
    arrived = lax.all_to_all(message, "cp", split_axis=0, concat_axis=0, tiled=True)
    return project(arrived, gram, added, jnp.asarray(spread_table(), BF))


def solution(mesh):
    return jax.shard_map(
        local,
        mesh=mesh,
        in_specs=(P("dp", "cp", None, None), P("dp"), P(), P(), P(), P(), P(), P(), P(None, "cp")),
        out_specs=P(None, ("dp", "cp"), None),
        check_vma=False,
    )
```

```python
import functools

import jax
import jax.numpy as jnp
import numpy as np
from jax import lax
from jax.experimental import pallas as pl
from jax.experimental.pallas import tpu as pltpu
from jax.sharding import PartitionSpec as P

LAT = 16
HID = 3072
HEAD_DIM = 128
HEADS = HID // HEAD_DIM
MAXF = 6
C = 512
WIDTH = 8
STRIP = 4
FRAMES = 64
CLIPS = 16
PART = HID // FRAMES
TOKENS = 512
SPARE = 64
LANES = 128
MESSAGE = 32
EPSILON = 1e-06
BF = jnp.bfloat16
F32 = jnp.float32
VMEM = pl.BlockSpec(memory_space=pltpu.VMEM)
SMEM = pl.BlockSpec(memory_space=pltpu.SMEM)
HBM = pl.BlockSpec(memory_space=pltpu.HBM)
MIB = 1 << 20


def in_hbm(value):
    return pltpu.with_memory_space_constraint(value, pltpu.HBM)


def nt(left, right):
    return lax.dot_general(left, right, (((1,), (1,)), ((), ())), preferred_element_type=F32)


def dot(left, right):
    return jnp.dot(left, right, preferred_element_type=F32)


def split(value):
    high = value.astype(BF)
    return high, (value - high.astype(F32)).astype(BF)


def each_clip(counts, body):
    start = 0
    for clip in range(CLIPS):
        body(clip, start, counts[clip])
        start = start + counts[clip]


def is_odd():
    return lax.rem(lax.axis_index("cp"), 2)


def fetch_kernel(counts, frames, odd_rows, even_rows, stage, sem):
    def clip(at, start, count):
        pltpu.make_async_copy(
            frames.at[pl.ds(at * MAXF, count)], stage.at[pl.ds(start, count)], sem
        ).start()

    each_clip(counts, clip)
    pltpu.make_async_copy(stage, stage, sem).wait()
    row = is_odd() * (STRIP - 1)
    odd_rows[...] = stage[:, row]
    even_rows[...] = stage[:, STRIP - 1 - row]


def fetch(counts, frames):
    return pl.pallas_call(
        fetch_kernel,
        out_shape=(
            pltpu.VMEM((FRAMES, WIDTH, C), BF),
            pltpu.VMEM((FRAMES, WIDTH, C), BF),
            pltpu.VMEM((FRAMES, STRIP, WIDTH, C), BF),
        ),
        in_specs=[SMEM, HBM],
        out_specs=(VMEM,) * 3,
        scratch_shapes=[pltpu.SemaphoreType.DMA],
        cost_estimate=pl.CostEstimate(flops=0, bytes_accessed=4 * MIB, transcendentals=0),
        name="fetch",
    )(in_hbm(counts), in_hbm(frames))


def latent_of(summed, frame, gain, proj):
    residual = frame.astype(F32) + 0.5 * summed * (1.0 + jnp.tanh(0.5 * summed))
    mean = jnp.mean(residual * residual, axis=-1, keepdims=True)
    normed = (residual * lax.rsqrt(mean + EPSILON) * gain).astype(BF)
    return dot(normed, proj)


def in_patch(latent, below):
    lane = lax.broadcasted_iota(jnp.int32, (FRAMES, LANES), 1) // LAT
    tokens = []
    for patch in range(WIDTH // 2):
        total = jnp.zeros((FRAMES, LANES), F32)
        for side in range(2):
            column = 2 * patch + side
            block = latent[column * FRAMES : (column + 1) * FRAMES]
            total = total + jnp.where(lane == below * 2 + side, block, 0.0)
        tokens.append(total)
    return tokens


def spread_proj(proj, copies):
    four = jnp.concatenate([proj[...].astype(F32)] * 4 + [jnp.zeros((LANES - 4 * LAT, C), F32)], axis=0)
    copies[...] = four.T.astype(BF)


def by_column(row, wide, cols, lane):
    row = row.astype(F32).reshape(FRAMES * WIDTH, C)
    for piece in range(C // LANES):
        wide[piece, 0 : FRAMES * WIDTH] = row[:, piece * LANES : (piece + 1) * LANES]
    for column in range(WIDTH):
        blocks = [wide[piece, pl.ds(column, FRAMES, stride=WIDTH), :] for piece in range(C // LANES)]
        block = jnp.concatenate(blocks, axis=1).astype(BF)
        cols[column * FRAMES : (column + 1) * FRAMES, lane : lane + C] = block


def inner_kernel(
    stage,
    weight,
    proj,
    gain,
    sums,
    own,
    tokens,
    taps,
    copies,
    norm,
    wide,
    cols,
    total,
    projs,
    small_sems,
    sems,
):
    small = [
        pltpu.make_async_copy(source, target, small_sems.at[place])
        for place, (source, target) in enumerate(((proj, projs), (gain, norm)))
    ]
    order = (1, 0, 2)
    loads = {}
    for side in order:
        for row in (1, 2, 0):
            loads[side, row] = pltpu.make_async_copy(
                weight.at[row, side], taps.at[side, pl.ds(row * C, C)], sems.at[side, row]
            )
            loads[side, row].start()
    for copy in small:
        copy.start()
    for row in range(STRIP):
        by_column(stage[:, row], wide.at[row], cols, row * C)
    for place, row in enumerate((0, STRIP - 1)):
        own[place] = cols[:, row * C : (row + 1) * C]
    count = FRAMES * WIDTH
    for side in order:
        begin, end = max(0, side - 1) * FRAMES, count - max(0, 1 - side) * FRAMES
        shift = (1 - side) * FRAMES
        for row in range(STRIP):
            low, high = max(row - 1, 0), min(row + 2, STRIP)
            for tap in ((1, 2), (0,), (), ())[row]:
                loads[side, tap].wait()
            skip = low - (row - 1)
            part = dot(
                cols[begin:end, low * C : high * C],
                taps[side, skip * C : (skip + high - low) * C, :],
            )
            target = sums.at[row // 2] if row in (0, STRIP - 1) else total.at[row - 1]
            if side == 1:
                target[...] = part
            else:
                target[begin + shift : end + shift, :] += part
    for copy in small:
        copy.wait()
    spread_proj(projs, copies)
    for row in (1, 2):
        latent = latent_of(total[row - 1], cols[:, row * C : (row + 1) * C], norm[...], copies[...])
        for patch_index, value in enumerate(in_patch(latent, row % 2)):
            tokens[(row // 2) * 4 + patch_index] = value


def inner(stage, *operands):
    return pl.pallas_call(
        inner_kernel,
        out_shape=(
            jax.ShapeDtypeStruct((2, FRAMES * WIDTH, C), F32),
            jax.ShapeDtypeStruct((2, FRAMES * WIDTH, C), BF),
            jax.ShapeDtypeStruct((8, FRAMES, LANES), F32),
            jax.ShapeDtypeStruct((3, 3 * C, C), BF),
            jax.ShapeDtypeStruct((C, LANES), BF),
            jax.ShapeDtypeStruct((1, C), F32),
        ),
        in_specs=[VMEM] + [HBM] * 3,
        out_specs=(VMEM,) * 6,
        scratch_shapes=[
            pltpu.VMEM((STRIP, C // LANES, FRAMES * WIDTH + SPARE, LANES), F32),
            pltpu.VMEM((FRAMES * WIDTH, STRIP * C), BF),
            pltpu.VMEM((2, FRAMES * WIDTH, C), F32),
            pltpu.VMEM((LAT, C), BF),
            pltpu.SemaphoreType.DMA((2,)),
            pltpu.SemaphoreType.DMA((3, 3)),
        ],
        compiler_params=pltpu.CompilerParams(vmem_limit_bytes=32 * MIB),
        cost_estimate=pl.CostEstimate(flops=8_000_000_000, bytes_accessed=9 * MIB, transcendentals=MIB // 2),
        name="inner",
    )(stage, *map(in_hbm, operands))


def edge_row(place, halo, taps, sums, own, copies, gain, wide, cols, total):
    count = FRAMES * WIDTH
    tap = pl.multiple_of(place * 2 * C, C)
    by_column(halo[...], wide, cols, 0)
    total[...] = sums[place]
    for side in (1, 0, 2):
        begin, end = max(0, side - 1) * FRAMES, count - max(0, 1 - side) * FRAMES
        shift = (1 - side) * FRAMES
        total[begin + shift : end + shift, :] += dot(cols[begin:end], taps[side, pl.ds(tap, C), :])
    latent = latent_of(total[...], own[place], gain[...], copies[...])
    return in_patch(latent, place)


def outer_scratch():
    return [
        pltpu.VMEM((C // LANES, FRAMES * WIDTH + SPARE, LANES), F32),
        pltpu.VMEM((FRAMES * WIDTH, C), BF),
        pltpu.VMEM((FRAMES * WIDTH, C), F32),
    ]


def outer_even_kernel(listed, halo, taps, sums, own, tokens, copies, gain, placed, parts, *scratch):
    *scratch, counts, sem = scratch
    load = pltpu.make_async_copy(listed, counts, sem)
    load.start()
    place = 1 - is_odd()
    for patch, value in enumerate(edge_row(place, halo, taps, sums, own, copies, gain, *scratch)):
        parts[patch] = tokens[place * 4 + patch] + value
    load.wait()
    frame = lax.broadcasted_iota(jnp.int32, (FRAMES, 1), 0)
    begin = jnp.zeros((FRAMES, 1), jnp.int32)
    start = 0
    for clip in range(CLIPS):
        begin = jnp.where(frame >= start, start, begin)
        start = start + counts[clip]
    position = jnp.zeros((FRAMES, LANES), F32)
    for offset in range(MAXF):
        position = position + jnp.where(frame - begin == offset, placed[offset : offset + 1, :], 0.0)
    high, low = split(position)
    parts[4] = high.astype(F32)
    parts[5] = low.astype(F32)


def outer_even(counts, halo, taps, sums, own, tokens, copies, gain, placed):
    return pl.pallas_call(
        outer_even_kernel,
        out_shape=jax.ShapeDtypeStruct((6, FRAMES, LANES), F32),
        in_specs=[HBM] + [VMEM] * 8,
        out_specs=VMEM,
        scratch_shapes=outer_scratch() + [pltpu.SMEM((CLIPS,), jnp.int32), pltpu.SemaphoreType.DMA],
        compiler_params=pltpu.CompilerParams(vmem_limit_bytes=24 * MIB),
        cost_estimate=pl.CostEstimate(flops=800_000_000, bytes_accessed=4 * MIB, transcendentals=MIB // 4),
        name="outer_even",
    )(in_hbm(counts), halo, taps, sums, own, tokens, copies, gain, placed)


def outer_odd_kernel(halo, taps, sums, own, tokens, copies, gain, parts, folded, message, *scratch):
    *scratch, flat = scratch
    place = is_odd()
    mine = edge_row(place, halo, taps, sums, own, copies, gain, *scratch)
    for patch in range(4):
        mine[patch] = mine[patch] + tokens[place * 4 + patch]
    for index in range(8):
        value = jnp.where(place == index // 4, mine[index % 4], parts[index % 4])
        if index < 2:
            value = value + parts[4 + index]
        flat[pl.ds(index, FRAMES, stride=8), :] = value
    rest = jnp.broadcast_to(folded[...][None], (FRAMES, PART // 2, LANES))
    message[...] = jnp.concatenate([flat[0:TOKENS].reshape(FRAMES, 8, LANES), rest], axis=1).astype(BF)


def outer_odd(halo, taps, sums, own, tokens, copies, gain, parts, folded):
    return pl.pallas_call(
        outer_odd_kernel,
        out_shape=jax.ShapeDtypeStruct((FRAMES, MESSAGE, LANES), BF),
        in_specs=[VMEM] * 9,
        out_specs=VMEM,
        scratch_shapes=outer_scratch() + [pltpu.VMEM((TOKENS + SPARE, LANES), F32)],
        compiler_params=pltpu.CompilerParams(vmem_limit_bytes=24 * MIB),
        cost_estimate=pl.CostEstimate(flops=800_000_000, bytes_accessed=4 * MIB, transcendentals=MIB // 4),
        name="outer_odd",
    )(halo, taps, sums, own, tokens, copies, gain, parts, folded)


def fold_kernel(after, listed, columns, patch, embed, scale, folded, placed, gram, added, table, rows, counts, sem):
    del after
    load = pltpu.make_async_copy(listed, counts, sem)
    load.start()
    table[0:64, :] = patch[...]
    table[64:80, :] = jnp.concatenate(
        [embed[...].astype(F32), jnp.zeros((16 - MAXF, HID), F32)], axis=0
    ).astype(BF)
    high, low = split(table[...].astype(F32) * scale[...])
    rows[0:64, :] = high[:64]
    rows[64:128, :] = low[:64]
    rows[128:144, :] = high[64:]
    rows[144:160, :] = low[64:]
    product = nt(rows[...], columns[...])
    product = jnp.concatenate([product, jnp.zeros((160, LANES - PART), F32)], axis=1)
    both = (product[:64] + product[64:128]).T
    both = jnp.concatenate([both, both], axis=1)
    lane = lax.broadcasted_iota(jnp.int32, (PART // 2, LANES), 1)
    folded[...] = jnp.where(lane < 64, both[: PART // 2], both[PART // 2 : PART])
    placed[...] = pltpu.roll(product[128:144] + product[144:160], 64, 1)
    product = nt(table[...], table[...])
    matrix = product[:64, :64]
    pieces = []
    for _ in range(3):
        pieces.append(matrix.astype(BF).astype(F32))
        matrix = matrix - pieces[-1]
    pieces = jnp.concatenate([*pieces, jnp.zeros((64, 64), F32)], axis=1)
    gram[...] = jnp.concatenate([pieces, jnp.zeros((64, 256), F32)], axis=0).astype(BF)
    own = lax.axis_index("cp")
    load.wait()
    start, begin = 0, 0
    for clip in range(CLIPS):
        begin = jnp.where(start <= own, start, begin)
        start = start + counts[clip]
    line = lax.broadcasted_iota(jnp.int32, (16, 80), 0)
    position = jnp.sum(jnp.where(line == own - begin, product[64:], 0.0), axis=0, keepdims=True)
    lane = lax.broadcasted_iota(jnp.int32, (1, 80), 1)
    square = jnp.sum(jnp.where(lane == 64 + own - begin, position, 0.0), axis=1, keepdims=True)
    added[0:1, :] = jnp.concatenate([2.0 * position[:, :64], jnp.zeros((1, 64), F32)], axis=1)
    added[1:2, :] = jnp.broadcast_to(square, (1, LANES))


def fold(after, counts, columns, patch, embed, scale):
    return pl.pallas_call(
        fold_kernel,
        out_shape=(
            jax.ShapeDtypeStruct((PART // 2, LANES), F32),
            jax.ShapeDtypeStruct((16, LANES), F32),
            jax.ShapeDtypeStruct((LANES, 256), BF),
            jax.ShapeDtypeStruct((2, LANES), F32),
        ),
        in_specs=[VMEM, HBM] + [VMEM] * 4,
        out_specs=(VMEM,) * 4,
        scratch_shapes=[
            pltpu.VMEM((80, HID), BF),
            pltpu.VMEM((160, HID), BF),
            pltpu.SMEM((CLIPS,), jnp.int32),
            pltpu.SemaphoreType.DMA,
        ],
        compiler_params=pltpu.CompilerParams(vmem_limit_bytes=8 * MIB),
        cost_estimate=pl.CostEstimate(flops=1_000_000_000, bytes_accessed=MIB, transcendentals=0),
        name="fold",
    )(after, in_hbm(counts), columns, patch, embed, scale)


GROUP = 4


def project_kernel(arrived, gram, added, spread, out, flat, columns, shift, held, sems):
    got = arrived[...].astype(F32)
    rows = got[:, 0:8].reshape(TOKENS, LANES)
    flat[0:TOKENS] = rows
    lane = lax.broadcasted_iota(jnp.int32, (TOKENS, LANES), 1)
    token = jnp.where(lane < 64, rows, 0.0)
    token = token + pltpu.roll(token, 64, 1)
    query = token.astype(BF)
    product = dot(query, gram[...])
    total = (product[:, :LANES] + product[:, LANES:] + added[0:1, :]) * token
    total = jnp.sum(total, axis=-1, keepdims=True) + added[1:2, 0:1]
    scale = lax.rsqrt(jnp.maximum(total, 0.0) * (1.0 / HID) + EPSILON)
    rest = got[:, 8:MESSAGE]
    lane = lax.broadcasted_iota(jnp.int32, rest.shape, 2)
    low, high = jnp.where(lane < 64, rest, 0.0), jnp.where(lane < 64, 0.0, rest)
    columns[...] = jnp.concatenate([low, high], axis=1).reshape(HID, LANES).astype(BF)
    lane = lax.broadcasted_iota(jnp.int32, (FRAMES, LANES), 1)
    piece = jnp.where(
        lane < 64, pltpu.roll(flat[pl.ds(0, FRAMES, stride=8), :], 64, 1), flat[pl.ds(1, FRAMES, stride=8), :]
    )
    laid = dot(piece.astype(BF), spread[...])
    lane = lax.broadcasted_iota(jnp.int32, (8, 8 * PART), 1)
    line = lax.broadcasted_iota(jnp.int32, (8, 8 * PART), 0) * PART
    mask = (lane >= line) & (lane < line + PART)
    for block in range(8):
        shift[:, block * 8 * PART : (block + 1) * 8 * PART] = jnp.sum(
            jnp.where(mask, laid[block * 8 : (block + 1) * 8], 0.0), axis=0, keepdims=True
        )
    copies = []
    for group in range(HEADS // GROUP):
        at = slice(group * GROUP * HEAD_DIM, (group + 1) * GROUP * HEAD_DIM)
        value = ((nt(query, columns[at, :]) + shift[:, at]) * scale).astype(BF)
        for head in range(GROUP):
            held[group * GROUP + head] = value[:, head * HEAD_DIM : (head + 1) * HEAD_DIM]
        heads = pl.ds(group * GROUP, GROUP)
        copies.append(pltpu.make_async_copy(held.at[heads], out.at[heads], sems.at[group]))
        copies[-1].start()
    for copy in copies:
        copy.wait()


def project(arrived, gram, added, spread):
    return pl.pallas_call(
        project_kernel,
        out_shape=jax.ShapeDtypeStruct((HEADS, TOKENS, HEAD_DIM), BF),
        in_specs=[VMEM] * 4,
        out_specs=HBM,
        scratch_shapes=[
            pltpu.VMEM((TOKENS + SPARE, LANES), F32),
            pltpu.VMEM((HID, LANES), BF),
            pltpu.VMEM((1, HID), F32),
            pltpu.VMEM((HEADS, TOKENS, HEAD_DIM), BF),
            pltpu.SemaphoreType.DMA((HEADS // GROUP,)),
        ],
        compiler_params=pltpu.CompilerParams(vmem_limit_bytes=24 * MIB),
        cost_estimate=pl.CostEstimate(flops=800_000_000, bytes_accessed=5 * MIB, transcendentals=0),
        name="project",
    )(arrived, gram, added, spread)


def spread_table():
    table = np.zeros((LANES, 8 * PART), np.float32)
    lane = np.arange(8 * PART)
    table[lane % PART, lane] = 1.0
    table[64 + lane % PART, lane] = 1.0
    return table


def local(
    frame_rows,
    frame_counts,
    conv_weight,
    norm_gain,
    latent_proj,
    patch_weight,
    frame_embed,
    query_gain,
    query_weight,
):
    devices = lax.axis_size("cp")
    pairs = [[(i, i + 1) for i in range(begin, devices - 1, 2)] for begin in (1, 0)]
    swaps = [pair + [(j, i) for i, j in pair] for pair in pairs]
    odd_rows, even_rows, stage = fetch(frame_counts, frame_rows)
    even_pair = lax.ppermute(even_rows, "cp", swaps[1])
    odd_pair = lax.ppermute(odd_rows, "cp", swaps[0])
    sums, own, tokens, taps, copies, gain = inner(
        stage, conv_weight, latent_proj.T, norm_gain[None, :]
    )
    folded, placed, gram, added = fold(
        gain, frame_counts, query_weight.T, patch_weight, frame_embed, query_gain[None, :]
    )
    parts = outer_even(frame_counts, even_pair, taps, sums, own, tokens, copies, gain, placed)
    message = outer_odd(odd_pair, taps, sums, own, tokens, copies, gain, parts, folded)
    arrived = lax.all_to_all(message, "cp", split_axis=0, concat_axis=0, tiled=True)
    return project(arrived, gram, added, jnp.asarray(spread_table(), BF))


def solution(mesh):
    return jax.shard_map(
        local,
        mesh=mesh,
        in_specs=(P("dp", "cp", None, None), P("dp"), P(), P(), P(), P(), P(), P(), P(None, "cp")),
        out_specs=P(None, ("dp", "cp"), None),
        check_vma=False,
    )
```

```python
import functools

import jax
import jax.numpy as jnp
import numpy as np
from jax import lax
from jax.experimental import pallas as pl
from jax.experimental.pallas import tpu as pltpu
from jax.sharding import PartitionSpec as P

LAT = 16
HID = 3072
HEAD_DIM = 128
HEADS = HID // HEAD_DIM
MAXF = 6
C = 512
WIDTH = 8
STRIP = 4
FRAMES = 64
CLIPS = 16
PART = HID // FRAMES
TOKENS = 512
SPARE = 64
LANES = 128
MESSAGE = 32
EPSILON = 1e-06
BF = jnp.bfloat16
F32 = jnp.float32
VMEM = pl.BlockSpec(memory_space=pltpu.VMEM)
SMEM = pl.BlockSpec(memory_space=pltpu.SMEM)
HBM = pl.BlockSpec(memory_space=pltpu.HBM)
MIB = 1 << 20


def in_hbm(value):
    return pltpu.with_memory_space_constraint(value, pltpu.HBM)


def nt(left, right):
    return lax.dot_general(left, right, (((1,), (1,)), ((), ())), preferred_element_type=F32)


def dot(left, right):
    return jnp.dot(left, right, preferred_element_type=F32)


def split(value):
    high = value.astype(BF)
    return high, (value - high.astype(F32)).astype(BF)


def each_clip(counts, body):
    start = 0
    for clip in range(CLIPS):
        body(clip, start, counts[clip])
        start = start + counts[clip]


def is_odd():
    return lax.rem(lax.axis_index("cp"), 2)


def fetch_kernel(counts, frames, odd_rows, even_rows, stage, sem):
    def clip(at, start, count):
        pltpu.make_async_copy(
            frames.at[pl.ds(at * MAXF, count)], stage.at[pl.ds(start, count)], sem
        ).start()

    each_clip(counts, clip)
    pltpu.make_async_copy(stage, stage, sem).wait()
    row = is_odd() * (STRIP - 1)
    odd_rows[...] = stage[:, row]
    even_rows[...] = stage[:, STRIP - 1 - row]


def fetch(counts, frames):
    return pl.pallas_call(
        fetch_kernel,
        out_shape=(
            pltpu.VMEM((FRAMES, WIDTH, C), BF),
            pltpu.VMEM((FRAMES, WIDTH, C), BF),
            pltpu.VMEM((FRAMES, STRIP, WIDTH, C), BF),
        ),
        in_specs=[SMEM, HBM],
        out_specs=(VMEM,) * 3,
        scratch_shapes=[pltpu.SemaphoreType.DMA],
        cost_estimate=pl.CostEstimate(flops=0, bytes_accessed=4 * MIB, transcendentals=0),
        name="fetch",
    )(in_hbm(counts), in_hbm(frames))


def latent_of(summed, frame, gain, proj):
    half = 0.5 * summed
    residual = frame.astype(F32) + (half + half * jnp.tanh(half))
    mean = jnp.mean(residual * residual, axis=-1, keepdims=True)
    return dot((residual * gain).astype(BF), proj) * lax.rsqrt(mean + EPSILON)


def in_patch(latent, below):
    lane = lax.broadcasted_iota(jnp.int32, (FRAMES, LANES), 1) // LAT
    tokens = []
    for patch in range(WIDTH // 2):
        total = jnp.zeros((FRAMES, LANES), F32)
        for side in range(2):
            column = 2 * patch + side
            block = latent[column * FRAMES : (column + 1) * FRAMES]
            total = total + jnp.where(lane == below * 2 + side, block, 0.0)
        tokens.append(total)
    return tokens


def spread_proj(proj, copies):
    four = jnp.concatenate([proj[...].astype(F32)] * 4 + [jnp.zeros((LANES - 4 * LAT, C), F32)], axis=0)
    copies[...] = four.T.astype(BF)


def by_column(row, wide, cols, lane):
    row = row.astype(F32).reshape(FRAMES * WIDTH, C)
    for piece in range(C // LANES):
        wide[piece, 0 : FRAMES * WIDTH] = row[:, piece * LANES : (piece + 1) * LANES]
    for column in range(WIDTH):
        blocks = [wide[piece, pl.ds(column, FRAMES, stride=WIDTH), :] for piece in range(C // LANES)]
        block = jnp.concatenate(blocks, axis=1).astype(BF)
        cols[column * FRAMES : (column + 1) * FRAMES, lane : lane + C] = block


def inner_kernel(
    stage,
    weight,
    proj,
    gain,
    sums,
    own,
    tokens,
    taps,
    copies,
    norm,
    wide,
    cols,
    total,
    projs,
    small_sems,
    sems,
):
    small = [
        pltpu.make_async_copy(source, target, small_sems.at[place])
        for place, (source, target) in enumerate(((proj, projs), (gain, norm)))
    ]
    order = (1, 0, 2)
    loads = {}
    for side in order:
        for row in (1, 2, 0):
            loads[side, row] = pltpu.make_async_copy(
                weight.at[row, side], taps.at[side, pl.ds(row * C, C)], sems.at[side, row]
            )
            loads[side, row].start()
    for copy in small:
        copy.start()
    for row in range(STRIP):
        by_column(stage[:, row], wide.at[row], cols, row * C)
    for place, row in enumerate((0, STRIP - 1)):
        own[place] = cols[:, row * C : (row + 1) * C]
    count = FRAMES * WIDTH
    for side in order:
        begin, end = max(0, side - 1) * FRAMES, count - max(0, 1 - side) * FRAMES
        shift = (1 - side) * FRAMES
        for row in range(STRIP):
            low, high = max(row - 1, 0), min(row + 2, STRIP)
            for tap in ((1, 2), (0,), (), ())[row]:
                loads[side, tap].wait()
            skip = low - (row - 1)
            part = dot(
                cols[begin:end, low * C : high * C],
                taps[side, skip * C : (skip + high - low) * C, :],
            )
            target = sums.at[row // 2] if row in (0, STRIP - 1) else total.at[row - 1]
            if side == 1:
                target[...] = part
            else:
                target[begin + shift : end + shift, :] += part
    for copy in small:
        copy.wait()
    spread_proj(projs, copies)
    for row in (1, 2):
        latent = latent_of(total[row - 1], cols[:, row * C : (row + 1) * C], norm[...], copies[...])
        for patch_index, value in enumerate(in_patch(latent, row % 2)):
            tokens[(row // 2) * 4 + patch_index] = value


def inner(stage, *operands):
    return pl.pallas_call(
        inner_kernel,
        out_shape=(
            jax.ShapeDtypeStruct((2, FRAMES * WIDTH, C), F32),
            jax.ShapeDtypeStruct((2, FRAMES * WIDTH, C), BF),
            jax.ShapeDtypeStruct((8, FRAMES, LANES), F32),
            jax.ShapeDtypeStruct((3, 3 * C, C), BF),
            jax.ShapeDtypeStruct((C, LANES), BF),
            jax.ShapeDtypeStruct((1, C), F32),
        ),
        in_specs=[VMEM] + [HBM] * 3,
        out_specs=(VMEM,) * 6,
        scratch_shapes=[
            pltpu.VMEM((STRIP, C // LANES, FRAMES * WIDTH + SPARE, LANES), F32),
            pltpu.VMEM((FRAMES * WIDTH, STRIP * C), BF),
            pltpu.VMEM((2, FRAMES * WIDTH, C), F32),
            pltpu.VMEM((LAT, C), BF),
            pltpu.SemaphoreType.DMA((2,)),
            pltpu.SemaphoreType.DMA((3, 3)),
        ],
        compiler_params=pltpu.CompilerParams(vmem_limit_bytes=32 * MIB),
        cost_estimate=pl.CostEstimate(flops=8_000_000_000, bytes_accessed=9 * MIB, transcendentals=MIB // 2),
        name="inner",
    )(stage, *map(in_hbm, operands))


def edge_row(place, halo, taps, sums, own, copies, gain, wide, cols, total):
    count = FRAMES * WIDTH
    tap = pl.multiple_of(place * 2 * C, C)
    by_column(halo[...], wide, cols, 0)
    total[...] = sums[place]
    for side in (0, 2, 1):
        begin, end = max(0, side - 1) * FRAMES, count - max(0, 1 - side) * FRAMES
        shift = (1 - side) * FRAMES
        total[begin + shift : end + shift, :] += dot(cols[begin:end], taps[side, pl.ds(tap, C), :])
    latent = latent_of(total[...], own[place], gain[...], copies[...])
    return in_patch(latent, place)


def outer_scratch():
    return [
        pltpu.VMEM((C // LANES, FRAMES * WIDTH + SPARE, LANES), F32),
        pltpu.VMEM((FRAMES * WIDTH, C), BF),
        pltpu.VMEM((FRAMES * WIDTH, C), F32),
    ]


def outer_even_kernel(listed, halo, taps, sums, own, tokens, copies, gain, placed, parts, *scratch):
    *scratch, counts, sem = scratch
    load = pltpu.make_async_copy(listed, counts, sem)
    load.start()
    place = 1 - is_odd()
    for patch, value in enumerate(edge_row(place, halo, taps, sums, own, copies, gain, *scratch)):
        parts[patch] = tokens[place * 4 + patch] + value
    load.wait()
    frame = lax.broadcasted_iota(jnp.int32, (FRAMES, 1), 0)
    begin = jnp.zeros((FRAMES, 1), jnp.int32)
    start = 0
    for clip in range(CLIPS):
        begin = jnp.where(frame >= start, start, begin)
        start = start + counts[clip]
    position = jnp.zeros((FRAMES, LANES), F32)
    for offset in range(MAXF):
        position = position + jnp.where(frame - begin == offset, placed[offset : offset + 1, :], 0.0)
    high, low = split(position)
    parts[4] = high.astype(F32)
    parts[5] = low.astype(F32)


def outer_even(counts, halo, taps, sums, own, tokens, copies, gain, placed):
    return pl.pallas_call(
        outer_even_kernel,
        out_shape=jax.ShapeDtypeStruct((6, FRAMES, LANES), F32),
        in_specs=[HBM] + [VMEM] * 8,
        out_specs=VMEM,
        scratch_shapes=outer_scratch() + [pltpu.SMEM((CLIPS,), jnp.int32), pltpu.SemaphoreType.DMA],
        compiler_params=pltpu.CompilerParams(vmem_limit_bytes=24 * MIB),
        cost_estimate=pl.CostEstimate(flops=800_000_000, bytes_accessed=4 * MIB, transcendentals=MIB // 4),
        name="outer_even",
    )(in_hbm(counts), halo, taps, sums, own, tokens, copies, gain, placed)


def outer_odd_kernel(halo, taps, sums, own, tokens, copies, gain, parts, folded, message, *scratch):
    *scratch, flat = scratch
    place = is_odd()
    mine = edge_row(place, halo, taps, sums, own, copies, gain, *scratch)
    for patch in range(4):
        mine[patch] = mine[patch] + tokens[place * 4 + patch]
    for index in range(8):
        value = jnp.where(place == index // 4, mine[index % 4], parts[index % 4])
        if index < 2:
            value = value + parts[4 + index]
        flat[pl.ds(index, FRAMES, stride=8), :] = value
    rest = jnp.broadcast_to(folded[...][None], (FRAMES, PART // 2, LANES))
    message[...] = jnp.concatenate([flat[0:TOKENS].reshape(FRAMES, 8, LANES), rest], axis=1).astype(BF)


def outer_odd(halo, taps, sums, own, tokens, copies, gain, parts, folded):
    return pl.pallas_call(
        outer_odd_kernel,
        out_shape=jax.ShapeDtypeStruct((FRAMES, MESSAGE, LANES), BF),
        in_specs=[VMEM] * 9,
        out_specs=VMEM,
        scratch_shapes=outer_scratch() + [pltpu.VMEM((TOKENS + SPARE, LANES), F32)],
        compiler_params=pltpu.CompilerParams(vmem_limit_bytes=24 * MIB),
        cost_estimate=pl.CostEstimate(flops=800_000_000, bytes_accessed=4 * MIB, transcendentals=MIB // 4),
        name="outer_odd",
    )(halo, taps, sums, own, tokens, copies, gain, parts, folded)


def fold_kernel(after, listed, columns, patch, embed, scale, folded, placed, gram, added, table, rows, counts, sem):
    del after
    load = pltpu.make_async_copy(listed, counts, sem)
    load.start()
    table[0:64, :] = patch[...]
    table[64:80, :] = jnp.concatenate(
        [embed[...].astype(F32), jnp.zeros((16 - MAXF, HID), F32)], axis=0
    ).astype(BF)
    high, low = split(table[...].astype(F32) * scale[...])
    rows[0:64, :] = high[:64]
    rows[64:128, :] = low[:64]
    rows[128:144, :] = high[64:]
    rows[144:160, :] = low[64:]
    product = nt(rows[...], columns[...])
    product = jnp.concatenate([product, jnp.zeros((160, LANES - PART), F32)], axis=1)
    both = (product[:64] + product[64:128]).T
    both = jnp.concatenate([both, both], axis=1)
    lane = lax.broadcasted_iota(jnp.int32, (PART // 2, LANES), 1)
    folded[...] = jnp.where(lane < 64, both[: PART // 2], both[PART // 2 : PART])
    placed[...] = pltpu.roll(product[128:144] + product[144:160], 64, 1)
    product = nt(table[...], table[...])
    matrix = product[:64, :64]
    pieces = []
    for _ in range(3):
        pieces.append(matrix.astype(BF).astype(F32))
        matrix = matrix - pieces[-1]
    pieces = jnp.concatenate([*pieces, jnp.zeros((64, 64), F32)], axis=1)
    gram[...] = jnp.concatenate([pieces, jnp.zeros((64, 256), F32)], axis=0).astype(BF)
    own = lax.axis_index("cp")
    load.wait()
    start, begin = 0, 0
    for clip in range(CLIPS):
        begin = jnp.where(start <= own, start, begin)
        start = start + counts[clip]
    line = lax.broadcasted_iota(jnp.int32, (16, 80), 0)
    position = jnp.sum(jnp.where(line == own - begin, product[64:], 0.0), axis=0, keepdims=True)
    lane = lax.broadcasted_iota(jnp.int32, (1, 80), 1)
    square = jnp.sum(jnp.where(lane == 64 + own - begin, position, 0.0), axis=1, keepdims=True)
    added[0:1, :] = jnp.concatenate([2.0 * position[:, :64], jnp.zeros((1, 64), F32)], axis=1)
    added[1:2, :] = jnp.broadcast_to(square, (1, LANES))


def fold(after, counts, columns, patch, embed, scale):
    return pl.pallas_call(
        fold_kernel,
        out_shape=(
            jax.ShapeDtypeStruct((PART // 2, LANES), F32),
            jax.ShapeDtypeStruct((16, LANES), F32),
            jax.ShapeDtypeStruct((LANES, 256), BF),
            jax.ShapeDtypeStruct((2, LANES), F32),
        ),
        in_specs=[VMEM, HBM] + [VMEM] * 4,
        out_specs=(VMEM,) * 4,
        scratch_shapes=[
            pltpu.VMEM((80, HID), BF),
            pltpu.VMEM((160, HID), BF),
            pltpu.SMEM((CLIPS,), jnp.int32),
            pltpu.SemaphoreType.DMA,
        ],
        compiler_params=pltpu.CompilerParams(vmem_limit_bytes=8 * MIB),
        cost_estimate=pl.CostEstimate(flops=1_000_000_000, bytes_accessed=MIB, transcendentals=0),
        name="fold",
    )(after, in_hbm(counts), columns, patch, embed, scale)


GROUP = 4


def project_kernel(arrived, gram, added, spread, out, flat, columns, shift, held, sems):
    got = arrived[...].astype(F32)
    rows = got[:, 0:8].reshape(TOKENS, LANES)
    flat[0:TOKENS] = rows
    lane = lax.broadcasted_iota(jnp.int32, (TOKENS, LANES), 1)
    token = jnp.where(lane < 64, rows, 0.0)
    token = token + pltpu.roll(token, 64, 1)
    query = token.astype(BF)
    product = dot(query, gram[...])
    total = (product[:, :LANES] + product[:, LANES:] + added[0:1, :]) * token
    total = jnp.sum(total, axis=-1, keepdims=True) + added[1:2, 0:1]
    scale = lax.rsqrt(jnp.maximum(total, 0.0) * (1.0 / HID) + EPSILON)
    rest = got[:, 8:MESSAGE]
    lane = lax.broadcasted_iota(jnp.int32, rest.shape, 2)
    low, high = jnp.where(lane < 64, rest, 0.0), jnp.where(lane < 64, 0.0, rest)
    columns[...] = jnp.concatenate([low, high], axis=1).reshape(HID, LANES).astype(BF)
    lane = lax.broadcasted_iota(jnp.int32, (FRAMES, LANES), 1)
    piece = jnp.where(
        lane < 64, pltpu.roll(flat[pl.ds(0, FRAMES, stride=8), :], 64, 1), flat[pl.ds(1, FRAMES, stride=8), :]
    )
    laid = dot(piece.astype(BF), spread[...])
    lane = lax.broadcasted_iota(jnp.int32, (8, 8 * PART), 1)
    line = lax.broadcasted_iota(jnp.int32, (8, 8 * PART), 0) * PART
    mask = (lane >= line) & (lane < line + PART)
    for block in range(8):
        shift[:, block * 8 * PART : (block + 1) * 8 * PART] = jnp.sum(
            jnp.where(mask, laid[block * 8 : (block + 1) * 8], 0.0), axis=0, keepdims=True
        )
    copies = []
    for group in range(HEADS // GROUP):
        at = slice(group * GROUP * HEAD_DIM, (group + 1) * GROUP * HEAD_DIM)
        value = ((nt(query, columns[at, :]) + shift[:, at]) * scale).astype(BF)
        for head in range(GROUP):
            held[group * GROUP + head] = value[:, head * HEAD_DIM : (head + 1) * HEAD_DIM]
        heads = pl.ds(group * GROUP, GROUP)
        copies.append(pltpu.make_async_copy(held.at[heads], out.at[heads], sems.at[group]))
        copies[-1].start()
    for copy in copies:
        copy.wait()


def project(arrived, gram, added, spread):
    return pl.pallas_call(
        project_kernel,
        out_shape=jax.ShapeDtypeStruct((HEADS, TOKENS, HEAD_DIM), BF),
        in_specs=[VMEM] * 4,
        out_specs=HBM,
        scratch_shapes=[
            pltpu.VMEM((TOKENS + SPARE, LANES), F32),
            pltpu.VMEM((HID, LANES), BF),
            pltpu.VMEM((1, HID), F32),
            pltpu.VMEM((HEADS, TOKENS, HEAD_DIM), BF),
            pltpu.SemaphoreType.DMA((HEADS // GROUP,)),
        ],
        compiler_params=pltpu.CompilerParams(vmem_limit_bytes=24 * MIB),
        cost_estimate=pl.CostEstimate(flops=800_000_000, bytes_accessed=5 * MIB, transcendentals=0),
        name="project",
    )(arrived, gram, added, spread)


def spread_table():
    table = np.zeros((LANES, 8 * PART), np.float32)
    lane = np.arange(8 * PART)
    table[lane % PART, lane] = 1.0
    table[64 + lane % PART, lane] = 1.0
    return table


def local(
    frame_rows,
    frame_counts,
    conv_weight,
    norm_gain,
    latent_proj,
    patch_weight,
    frame_embed,
    query_gain,
    query_weight,
):
    devices = lax.axis_size("cp")
    pairs = [[(i, i + 1) for i in range(begin, devices - 1, 2)] for begin in (1, 0)]
    swaps = [pair + [(j, i) for i, j in pair] for pair in pairs]
    odd_rows, even_rows, stage = fetch(frame_counts, frame_rows)
    even_pair = lax.ppermute(even_rows, "cp", swaps[1])
    odd_pair = lax.ppermute(odd_rows, "cp", swaps[0])
    sums, own, tokens, taps, copies, gain = inner(
        stage, conv_weight, latent_proj.T, norm_gain[None, :]
    )
    folded, placed, gram, added = fold(
        gain, frame_counts, query_weight.T, patch_weight, frame_embed, query_gain[None, :]
    )
    parts = outer_even(frame_counts, even_pair, taps, sums, own, tokens, copies, gain, placed)
    message = outer_odd(odd_pair, taps, sums, own, tokens, copies, gain, parts, folded)
    arrived = lax.all_to_all(message, "cp", split_axis=0, concat_axis=0, tiled=True)
    return project(arrived, gram, added, jnp.asarray(spread_table(), BF))


def solution(mesh):
    return jax.shard_map(
        local,
        mesh=mesh,
        in_specs=(P("dp", "cp", None, None), P("dp"), P(), P(), P(), P(), P(), P(), P(None, "cp")),
        out_specs=P(None, ("dp", "cp"), None),
        check_vma=False,
    )
```

```python
import functools

import jax
import jax.numpy as jnp
import numpy as np
from jax import lax
from jax.experimental import pallas as pl
from jax.experimental.pallas import tpu as pltpu
from jax.sharding import PartitionSpec as P

LAT = 16
HID = 3072
HEAD_DIM = 128
HEADS = HID // HEAD_DIM
MAXF = 6
C = 512
WIDTH = 8
STRIP = 4
FRAMES = 64
CLIPS = 16
PART = HID // FRAMES
TOKENS = 512
SPARE = 64
LANES = 128
MESSAGE = 32
EPSILON = 1e-06
BF = jnp.bfloat16
F32 = jnp.float32
VMEM = pl.BlockSpec(memory_space=pltpu.VMEM)
SMEM = pl.BlockSpec(memory_space=pltpu.SMEM)
HBM = pl.BlockSpec(memory_space=pltpu.HBM)
MIB = 1 << 20


def in_hbm(value):
    return pltpu.with_memory_space_constraint(value, pltpu.HBM)


def nt(left, right):
    return lax.dot_general(left, right, (((1,), (1,)), ((), ())), preferred_element_type=F32)


def dot(left, right):
    return jnp.dot(left, right, preferred_element_type=F32)


def split(value):
    high = value.astype(BF)
    return high, (value - high.astype(F32)).astype(BF)


def each_clip(counts, body):
    start = 0
    for clip in range(CLIPS):
        body(clip, start, counts[clip])
        start = start + counts[clip]


def is_odd():
    return lax.rem(lax.axis_index("cp"), 2)


def fetch_kernel(counts, frames, odd_rows, even_rows, stage, sem):
    def clip(at, start, count):
        pltpu.make_async_copy(
            frames.at[pl.ds(at * MAXF, count)], stage.at[pl.ds(start, count)], sem
        ).start()

    each_clip(counts, clip)
    pltpu.make_async_copy(stage, stage, sem).wait()
    row = is_odd() * (STRIP - 1)
    odd_rows[...] = stage[:, row]
    even_rows[...] = stage[:, STRIP - 1 - row]


def fetch(counts, frames):
    return pl.pallas_call(
        fetch_kernel,
        out_shape=(
            pltpu.VMEM((FRAMES, WIDTH, C), BF),
            pltpu.VMEM((FRAMES, WIDTH, C), BF),
            pltpu.VMEM((FRAMES, STRIP, WIDTH, C), BF),
        ),
        in_specs=[SMEM, HBM],
        out_specs=(VMEM,) * 3,
        scratch_shapes=[pltpu.SemaphoreType.DMA],
        cost_estimate=pl.CostEstimate(flops=0, bytes_accessed=4 * MIB, transcendentals=0),
        name="fetch",
    )(in_hbm(counts), in_hbm(frames))


def latent_of(summed, frame, gain, proj):
    half = 0.5 * summed
    residual = frame.astype(F32) + (half + half * jnp.tanh(half))
    mean = jnp.mean(residual * residual, axis=-1, keepdims=True)
    return dot((residual * gain).astype(BF), proj) * lax.rsqrt(mean + EPSILON)


def in_patch(latent, below):
    lane = lax.broadcasted_iota(jnp.int32, (FRAMES, LANES), 1) // LAT
    tokens = []
    for patch in range(WIDTH // 2):
        total = jnp.zeros((FRAMES, LANES), F32)
        for side in range(2):
            column = 2 * patch + side
            block = latent[column * FRAMES : (column + 1) * FRAMES]
            total = total + jnp.where(lane == below * 2 + side, block, 0.0)
        tokens.append(total)
    return tokens


def spread_proj(proj, copies):
    four = jnp.concatenate([proj[...].astype(F32)] * 4 + [jnp.zeros((LANES - 4 * LAT, C), F32)], axis=0)
    copies[...] = four.T.astype(BF)


def by_column(row, wide, cols, lane):
    row = row.astype(F32).reshape(FRAMES * WIDTH, C)
    for piece in range(C // LANES):
        wide[piece, 0 : FRAMES * WIDTH] = row[:, piece * LANES : (piece + 1) * LANES]
    for column in range(WIDTH):
        blocks = [wide[piece, pl.ds(column, FRAMES, stride=WIDTH), :] for piece in range(C // LANES)]
        block = jnp.concatenate(blocks, axis=1).astype(BF)
        cols[column * FRAMES : (column + 1) * FRAMES, lane : lane + C] = block


def inner_kernel(
    stage,
    weight,
    proj,
    gain,
    sums,
    own,
    tokens,
    taps,
    copies,
    norm,
    wide,
    cols,
    total,
    projs,
    small_sems,
    sems,
):
    small = [
        pltpu.make_async_copy(source, target, small_sems.at[place])
        for place, (source, target) in enumerate(((proj, projs), (gain, norm)))
    ]
    order = (1, 0, 2)
    loads = {}
    for side in order:
        for row in (1, 2, 0):
            loads[side, row] = pltpu.make_async_copy(
                weight.at[row, side], taps.at[side, pl.ds(row * C, C)], sems.at[side, row]
            )
            loads[side, row].start()
    for copy in small:
        copy.start()
    for row in range(STRIP):
        by_column(stage[:, row], wide.at[row], cols, row * C)
    for place, row in enumerate((0, STRIP - 1)):
        own[place] = cols[:, row * C : (row + 1) * C]
    count = FRAMES * WIDTH
    for side in order:
        begin, end = max(0, side - 1) * FRAMES, count - max(0, 1 - side) * FRAMES
        shift = (1 - side) * FRAMES
        for row in range(STRIP):
            low, high = max(row - 1, 0), min(row + 2, STRIP)
            for tap in ((1, 2), (0,), (), ())[row]:
                loads[side, tap].wait()
            skip = low - (row - 1)
            part = dot(
                cols[begin:end, low * C : high * C],
                taps[side, skip * C : (skip + high - low) * C, :],
            )
            target = sums.at[row // 2] if row in (0, STRIP - 1) else total.at[row - 1]
            if side == 1:
                target[...] = part
            else:
                target[begin + shift : end + shift, :] += part
    for copy in small:
        copy.wait()
    spread_proj(projs, copies)
    for row in (1, 2):
        latent = latent_of(total[row - 1], cols[:, row * C : (row + 1) * C], norm[...], copies[...])
        for patch_index, value in enumerate(in_patch(latent, row % 2)):
            tokens[(row // 2) * 4 + patch_index] = value


def inner(stage, *operands):
    return pl.pallas_call(
        inner_kernel,
        out_shape=(
            jax.ShapeDtypeStruct((2, FRAMES * WIDTH, C), F32),
            jax.ShapeDtypeStruct((2, FRAMES * WIDTH, C), BF),
            jax.ShapeDtypeStruct((8, FRAMES, LANES), F32),
            jax.ShapeDtypeStruct((3, 3 * C, C), BF),
            jax.ShapeDtypeStruct((C, LANES), BF),
            jax.ShapeDtypeStruct((1, C), F32),
        ),
        in_specs=[VMEM] + [HBM] * 3,
        out_specs=(VMEM,) * 6,
        scratch_shapes=[
            pltpu.VMEM((STRIP, C // LANES, FRAMES * WIDTH + SPARE, LANES), F32),
            pltpu.VMEM((FRAMES * WIDTH, STRIP * C), BF),
            pltpu.VMEM((2, FRAMES * WIDTH, C), F32),
            pltpu.VMEM((LAT, C), BF),
            pltpu.SemaphoreType.DMA((2,)),
            pltpu.SemaphoreType.DMA((3, 3)),
        ],
        compiler_params=pltpu.CompilerParams(vmem_limit_bytes=32 * MIB),
        cost_estimate=pl.CostEstimate(flops=8_000_000_000, bytes_accessed=9 * MIB, transcendentals=MIB // 2),
        name="inner",
    )(stage, *map(in_hbm, operands))


def edge_row(place, halo, taps, sums, own, copies, gain, wide, cols, total):
    count = FRAMES * WIDTH
    tap = pl.multiple_of(place * 2 * C, C)
    by_column(halo[...], wide, cols, 0)
    total[...] = sums[place]
    for side in (0, 2, 1):
        begin, end = max(0, side - 1) * FRAMES, count - max(0, 1 - side) * FRAMES
        shift = (1 - side) * FRAMES
        total[begin + shift : end + shift, :] += dot(cols[begin:end], taps[side, pl.ds(tap, C), :])
    latent = latent_of(total[...], own[place], gain[...], copies[...])
    return in_patch(latent, place)


def outer_scratch():
    return [
        pltpu.VMEM((C // LANES, FRAMES * WIDTH + SPARE, LANES), F32),
        pltpu.VMEM((FRAMES * WIDTH, C), BF),
        pltpu.VMEM((FRAMES * WIDTH, C), F32),
    ]


def outer_even_kernel(halo, taps, sums, own, tokens, copies, gain, parts, *scratch):
    place = 1 - is_odd()
    for patch, value in enumerate(edge_row(place, halo, taps, sums, own, copies, gain, *scratch)):
        parts[patch] = tokens[place * 4 + patch] + value


def outer_even(halo, taps, sums, own, tokens, copies, gain):
    return pl.pallas_call(
        outer_even_kernel,
        out_shape=jax.ShapeDtypeStruct((4, FRAMES, LANES), F32),
        in_specs=[VMEM] * 7,
        out_specs=VMEM,
        scratch_shapes=outer_scratch(),
        compiler_params=pltpu.CompilerParams(vmem_limit_bytes=24 * MIB),
        cost_estimate=pl.CostEstimate(flops=800_000_000, bytes_accessed=4 * MIB, transcendentals=MIB // 4),
        name="outer_even",
    )(halo, taps, sums, own, tokens, copies, gain)


def outer_odd_kernel(halo, taps, sums, own, tokens, copies, gain, parts, placed, folded, message, *scratch):
    *scratch, flat = scratch
    place = is_odd()
    mine = edge_row(place, halo, taps, sums, own, copies, gain, *scratch)
    for patch in range(4):
        mine[patch] = mine[patch] + tokens[place * 4 + patch]
    for index in range(8):
        value = jnp.where(place == index // 4, mine[index % 4], parts[index % 4])
        if index < 2:
            value = value + placed[index]
        flat[pl.ds(index, FRAMES, stride=8), :] = value
    rest = jnp.broadcast_to(folded[...][None], (FRAMES, PART // 2, LANES))
    message[...] = jnp.concatenate([flat[0:TOKENS].reshape(FRAMES, 8, LANES), rest], axis=1).astype(BF)


def outer_odd(halo, taps, sums, own, tokens, copies, gain, parts, placed, folded):
    return pl.pallas_call(
        outer_odd_kernel,
        out_shape=jax.ShapeDtypeStruct((FRAMES, MESSAGE, LANES), BF),
        in_specs=[VMEM] * 10,
        out_specs=VMEM,
        scratch_shapes=outer_scratch() + [pltpu.VMEM((TOKENS + SPARE, LANES), F32)],
        compiler_params=pltpu.CompilerParams(vmem_limit_bytes=24 * MIB),
        cost_estimate=pl.CostEstimate(flops=800_000_000, bytes_accessed=4 * MIB, transcendentals=MIB // 4),
        name="outer_odd",
    )(halo, taps, sums, own, tokens, copies, gain, parts, placed, folded)


def fold_kernel(after, listed, columns, patch, embed, scale, folded, placed, gram, added, table, rows, counts, sem):
    del after
    load = pltpu.make_async_copy(listed, counts, sem)
    load.start()
    table[0:64, :] = patch[...]
    table[64:80, :] = jnp.concatenate(
        [embed[...].astype(F32), jnp.zeros((16 - MAXF, HID), F32)], axis=0
    ).astype(BF)
    high, low = split(table[...].astype(F32) * scale[...])
    rows[0:64, :] = high[:64]
    rows[64:128, :] = low[:64]
    rows[128:144, :] = high[64:]
    rows[144:160, :] = low[64:]
    product = nt(rows[...], columns[...])
    product = jnp.concatenate([product, jnp.zeros((160, LANES - PART), F32)], axis=1)
    both = (product[:64] + product[64:128]).T
    both = jnp.concatenate([both, both], axis=1)
    lane = lax.broadcasted_iota(jnp.int32, (PART // 2, LANES), 1)
    folded[...] = jnp.where(lane < 64, both[: PART // 2], both[PART // 2 : PART])
    offsets = pltpu.roll(product[128:144] + product[144:160], 64, 1)
    product = nt(table[...], table[...])
    matrix = product[:64, :64]
    pieces = []
    for _ in range(3):
        pieces.append(matrix.astype(BF).astype(F32))
        matrix = matrix - pieces[-1]
    pieces = jnp.concatenate([*pieces, jnp.zeros((64, 64), F32)], axis=1)
    gram[...] = jnp.concatenate([pieces, jnp.zeros((64, 256), F32)], axis=0).astype(BF)
    own = lax.axis_index("cp")
    load.wait()
    start, begin = 0, 0
    frame = lax.broadcasted_iota(jnp.int32, (FRAMES, 1), 0)
    begins = jnp.zeros((FRAMES, 1), jnp.int32)
    for clip in range(CLIPS):
        begin = jnp.where(start <= own, start, begin)
        begins = jnp.where(frame >= start, start, begins)
        start = start + counts[clip]
    position = jnp.zeros((FRAMES, LANES), F32)
    for offset in range(MAXF):
        position = position + jnp.where(frame - begins == offset, offsets[offset : offset + 1, :], 0.0)
    high, low = split(position)
    placed[0] = high.astype(F32)
    placed[1] = low.astype(F32)
    line = lax.broadcasted_iota(jnp.int32, (16, 80), 0)
    position = jnp.sum(jnp.where(line == own - begin, product[64:], 0.0), axis=0, keepdims=True)
    lane = lax.broadcasted_iota(jnp.int32, (1, 80), 1)
    square = jnp.sum(jnp.where(lane == 64 + own - begin, position, 0.0), axis=1, keepdims=True)
    added[0:1, :] = jnp.concatenate([2.0 * position[:, :64], jnp.zeros((1, 64), F32)], axis=1)
    added[1:2, :] = jnp.broadcast_to(square, (1, LANES))


def fold(after, counts, columns, patch, embed, scale):
    return pl.pallas_call(
        fold_kernel,
        out_shape=(
            jax.ShapeDtypeStruct((PART // 2, LANES), F32),
            jax.ShapeDtypeStruct((2, FRAMES, LANES), F32),
            jax.ShapeDtypeStruct((LANES, 256), BF),
            jax.ShapeDtypeStruct((2, LANES), F32),
        ),
        in_specs=[VMEM, HBM] + [VMEM] * 4,
        out_specs=(VMEM,) * 4,
        scratch_shapes=[
            pltpu.VMEM((80, HID), BF),
            pltpu.VMEM((160, HID), BF),
            pltpu.SMEM((CLIPS,), jnp.int32),
            pltpu.SemaphoreType.DMA,
        ],
        compiler_params=pltpu.CompilerParams(vmem_limit_bytes=8 * MIB),
        cost_estimate=pl.CostEstimate(flops=1_000_000_000, bytes_accessed=MIB, transcendentals=0),
        name="fold",
    )(after, in_hbm(counts), columns, patch, embed, scale)


GROUP = 4


def project_kernel(arrived, gram, added, spread, out, flat, columns, shift, held, sems):
    got = arrived[...].astype(F32)
    rows = got[:, 0:8].reshape(TOKENS, LANES)
    flat[0:TOKENS] = rows
    lane = lax.broadcasted_iota(jnp.int32, (TOKENS, LANES), 1)
    token = jnp.where(lane < 64, rows, 0.0)
    token = token + pltpu.roll(token, 64, 1)
    query = token.astype(BF)
    product = dot(query, gram[...])
    total = (product[:, :LANES] + product[:, LANES:] + added[0:1, :]) * token
    total = jnp.sum(total, axis=-1, keepdims=True) + added[1:2, 0:1]
    scale = lax.rsqrt(jnp.maximum(total, 0.0) * (1.0 / HID) + EPSILON)
    rest = got[:, 8:MESSAGE]
    lane = lax.broadcasted_iota(jnp.int32, rest.shape, 2)
    low, high = jnp.where(lane < 64, rest, 0.0), jnp.where(lane < 64, 0.0, rest)
    columns[...] = jnp.concatenate([low, high], axis=1).reshape(HID, LANES).astype(BF)
    lane = lax.broadcasted_iota(jnp.int32, (FRAMES, LANES), 1)
    piece = jnp.where(
        lane < 64, pltpu.roll(flat[pl.ds(0, FRAMES, stride=8), :], 64, 1), flat[pl.ds(1, FRAMES, stride=8), :]
    )
    laid = dot(piece.astype(BF), spread[...])
    lane = lax.broadcasted_iota(jnp.int32, (8, 8 * PART), 1)
    line = lax.broadcasted_iota(jnp.int32, (8, 8 * PART), 0) * PART
    mask = (lane >= line) & (lane < line + PART)
    for block in range(8):
        shift[:, block * 8 * PART : (block + 1) * 8 * PART] = jnp.sum(
            jnp.where(mask, laid[block * 8 : (block + 1) * 8], 0.0), axis=0, keepdims=True
        )
    copies = []
    for group in range(HEADS // GROUP):
        at = slice(group * GROUP * HEAD_DIM, (group + 1) * GROUP * HEAD_DIM)
        value = ((nt(query, columns[at, :]) + shift[:, at]) * scale).astype(BF)
        for head in range(GROUP):
            held[group * GROUP + head] = value[:, head * HEAD_DIM : (head + 1) * HEAD_DIM]
        heads = pl.ds(group * GROUP, GROUP)
        copies.append(pltpu.make_async_copy(held.at[heads], out.at[heads], sems.at[group]))
        copies[-1].start()
    for copy in copies:
        copy.wait()


def project(arrived, gram, added, spread):
    return pl.pallas_call(
        project_kernel,
        out_shape=jax.ShapeDtypeStruct((HEADS, TOKENS, HEAD_DIM), BF),
        in_specs=[VMEM] * 4,
        out_specs=HBM,
        scratch_shapes=[
            pltpu.VMEM((TOKENS + SPARE, LANES), F32),
            pltpu.VMEM((HID, LANES), BF),
            pltpu.VMEM((1, HID), F32),
            pltpu.VMEM((HEADS, TOKENS, HEAD_DIM), BF),
            pltpu.SemaphoreType.DMA((HEADS // GROUP,)),
        ],
        compiler_params=pltpu.CompilerParams(vmem_limit_bytes=24 * MIB),
        cost_estimate=pl.CostEstimate(flops=800_000_000, bytes_accessed=5 * MIB, transcendentals=0),
        name="project",
    )(arrived, gram, added, spread)


def spread_table():
    table = np.zeros((LANES, 8 * PART), np.float32)
    lane = np.arange(8 * PART)
    table[lane % PART, lane] = 1.0
    table[64 + lane % PART, lane] = 1.0
    return table


def local(
    frame_rows,
    frame_counts,
    conv_weight,
    norm_gain,
    latent_proj,
    patch_weight,
    frame_embed,
    query_gain,
    query_weight,
):
    devices = lax.axis_size("cp")
    pairs = [[(i, i + 1) for i in range(begin, devices - 1, 2)] for begin in (1, 0)]
    swaps = [pair + [(j, i) for i, j in pair] for pair in pairs]
    odd_rows, even_rows, stage = fetch(frame_counts, frame_rows)
    even_pair = lax.ppermute(even_rows, "cp", swaps[1])
    odd_pair = lax.ppermute(odd_rows, "cp", swaps[0])
    sums, own, tokens, taps, copies, gain = inner(
        stage, conv_weight, latent_proj.T, norm_gain[None, :]
    )
    folded, placed, gram, added = fold(
        gain, frame_counts, query_weight.T, patch_weight, frame_embed, query_gain[None, :]
    )
    parts = outer_even(even_pair, taps, sums, own, tokens, copies, gain)
    message = outer_odd(odd_pair, taps, sums, own, tokens, copies, gain, parts, placed, folded)
    arrived = lax.all_to_all(message, "cp", split_axis=0, concat_axis=0, tiled=True)
    return project(arrived, gram, added, jnp.asarray(spread_table(), BF))


def solution(mesh):
    return jax.shard_map(
        local,
        mesh=mesh,
        in_specs=(P("dp", "cp", None, None), P("dp"), P(), P(), P(), P(), P(), P(), P(None, "cp")),
        out_specs=P(None, ("dp", "cp"), None),
        check_vma=False,
    )
```

```python
import functools

import jax
import jax.numpy as jnp
import numpy as np
from jax import lax
from jax.experimental import pallas as pl
from jax.experimental.pallas import tpu as pltpu
from jax.sharding import PartitionSpec as P

LAT = 16
HID = 3072
HEAD_DIM = 128
HEADS = HID // HEAD_DIM
MAXF = 6
C = 512
WIDTH = 8
STRIP = 4
FRAMES = 64
CLIPS = 16
PART = HID // FRAMES
TOKENS = 512
SPARE = 64
LANES = 128
MESSAGE = 32
EPSILON = 1e-06
BF = jnp.bfloat16
F32 = jnp.float32
VMEM = pl.BlockSpec(memory_space=pltpu.VMEM)
SMEM = pl.BlockSpec(memory_space=pltpu.SMEM)
HBM = pl.BlockSpec(memory_space=pltpu.HBM)
MIB = 1 << 20


def in_hbm(value):
    return pltpu.with_memory_space_constraint(value, pltpu.HBM)


def nt(left, right):
    return lax.dot_general(left, right, (((1,), (1,)), ((), ())), preferred_element_type=F32)


def dot(left, right):
    return jnp.dot(left, right, preferred_element_type=F32)


def split(value):
    high = value.astype(BF)
    return high, (value - high.astype(F32)).astype(BF)


def each_clip(counts, body):
    start = 0
    for clip in range(CLIPS):
        body(clip, start, counts[clip])
        start = start + counts[clip]


def is_odd():
    return lax.rem(lax.axis_index("cp"), 2)


def fetch_kernel(counts, frames, odd_rows, even_rows, stage, sem):
    def clip(at, start, count):
        slots, places = pl.ds(at * MAXF, count), pl.ds(start, count)
        for row in (0, 2):
            rows = pl.ds(row, 2)
            pltpu.make_async_copy(frames.at[slots, rows], stage.at[places, rows], sem).start()

    each_clip(counts, clip)
    pltpu.make_async_copy(stage, stage, sem).wait()
    row = is_odd() * (STRIP - 1)
    odd_rows[...] = stage[:, row]
    even_rows[...] = stage[:, STRIP - 1 - row]


def fetch(counts, frames):
    return pl.pallas_call(
        fetch_kernel,
        out_shape=(
            pltpu.VMEM((FRAMES, WIDTH, C), BF),
            pltpu.VMEM((FRAMES, WIDTH, C), BF),
            pltpu.VMEM((FRAMES, STRIP, WIDTH, C), BF),
        ),
        in_specs=[SMEM, HBM],
        out_specs=(VMEM,) * 3,
        scratch_shapes=[pltpu.SemaphoreType.DMA],
        cost_estimate=pl.CostEstimate(flops=0, bytes_accessed=4 * MIB, transcendentals=0),
        name="fetch",
    )(in_hbm(counts), in_hbm(frames))


def latent_of(summed, frame, gain, proj):
    half = 0.5 * summed
    residual = frame.astype(F32) + (half + half * jnp.tanh(half))
    mean = jnp.mean(residual * residual, axis=-1, keepdims=True)
    return dot((residual * gain).astype(BF), proj) * lax.rsqrt(mean + EPSILON)


def in_patch(latent, below):
    lane = lax.broadcasted_iota(jnp.int32, (FRAMES, LANES), 1) // LAT
    tokens = []
    for patch in range(WIDTH // 2):
        total = jnp.zeros((FRAMES, LANES), F32)
        for side in range(2):
            column = 2 * patch + side
            block = latent[column * FRAMES : (column + 1) * FRAMES]
            total = total + jnp.where(lane == below * 2 + side, block, 0.0)
        tokens.append(total)
    return tokens


def spread_proj(proj, copies):
    four = jnp.concatenate([proj[...].astype(F32)] * 4 + [jnp.zeros((LANES - 4 * LAT, C), F32)], axis=0)
    copies[...] = four.T.astype(BF)


def by_column(row, wide, cols, lane):
    row = row.astype(F32).reshape(FRAMES * WIDTH, C)
    for piece in range(C // LANES):
        wide[piece, 0 : FRAMES * WIDTH] = row[:, piece * LANES : (piece + 1) * LANES]
    for column in range(WIDTH):
        blocks = [wide[piece, pl.ds(column, FRAMES, stride=WIDTH), :] for piece in range(C // LANES)]
        block = jnp.concatenate(blocks, axis=1).astype(BF)
        cols[column * FRAMES : (column + 1) * FRAMES, lane : lane + C] = block


def inner_kernel(
    stage,
    weight,
    proj,
    gain,
    sums,
    own,
    tokens,
    taps,
    copies,
    norm,
    wide,
    cols,
    total,
    projs,
    small_sems,
    sems,
):
    small = [
        pltpu.make_async_copy(source, target, small_sems.at[place])
        for place, (source, target) in enumerate(((proj, projs), (gain, norm)))
    ]
    order = (1, 0, 2)
    loads = {}
    for side in order:
        for row in (1, 2, 0):
            loads[side, row] = pltpu.make_async_copy(
                weight.at[row, side], taps.at[side, pl.ds(row * C, C)], sems.at[side, row]
            )
            loads[side, row].start()
    for copy in small:
        copy.start()
    for row in range(STRIP):
        by_column(stage[:, row], wide.at[row], cols, row * C)
    for place, row in enumerate((0, STRIP - 1)):
        own[place] = cols[:, row * C : (row + 1) * C]
    count = FRAMES * WIDTH
    for side in order:
        begin, end = max(0, side - 1) * FRAMES, count - max(0, 1 - side) * FRAMES
        shift = (1 - side) * FRAMES
        for row in range(STRIP):
            low, high = max(row - 1, 0), min(row + 2, STRIP)
            for tap in ((1, 2), (0,), (), ())[row]:
                loads[side, tap].wait()
            skip = low - (row - 1)
            part = dot(
                cols[begin:end, low * C : high * C],
                taps[side, skip * C : (skip + high - low) * C, :],
            )
            target = sums.at[row // 2] if row in (0, STRIP - 1) else total.at[row - 1]
            if side == 1:
                target[...] = part
            else:
                target[begin + shift : end + shift, :] += part
    for copy in small:
        copy.wait()
    spread_proj(projs, copies)
    for row in (1, 2):
        latent = latent_of(total[row - 1], cols[:, row * C : (row + 1) * C], norm[...], copies[...])
        for patch_index, value in enumerate(in_patch(latent, row % 2)):
            tokens[(row // 2) * 4 + patch_index] = value


def inner(stage, *operands):
    return pl.pallas_call(
        inner_kernel,
        out_shape=(
            jax.ShapeDtypeStruct((2, FRAMES * WIDTH, C), F32),
            jax.ShapeDtypeStruct((2, FRAMES * WIDTH, C), BF),
            jax.ShapeDtypeStruct((8, FRAMES, LANES), F32),
            jax.ShapeDtypeStruct((3, 3 * C, C), BF),
            jax.ShapeDtypeStruct((C, LANES), BF),
            jax.ShapeDtypeStruct((1, C), F32),
        ),
        in_specs=[VMEM] + [HBM] * 3,
        out_specs=(VMEM,) * 6,
        scratch_shapes=[
            pltpu.VMEM((STRIP, C // LANES, FRAMES * WIDTH + SPARE, LANES), F32),
            pltpu.VMEM((FRAMES * WIDTH, STRIP * C), BF),
            pltpu.VMEM((2, FRAMES * WIDTH, C), F32),
            pltpu.VMEM((LAT, C), BF),
            pltpu.SemaphoreType.DMA((2,)),
            pltpu.SemaphoreType.DMA((3, 3)),
        ],
        compiler_params=pltpu.CompilerParams(vmem_limit_bytes=32 * MIB),
        cost_estimate=pl.CostEstimate(flops=8_000_000_000, bytes_accessed=9 * MIB, transcendentals=MIB // 2),
        name="inner",
    )(stage, *map(in_hbm, operands))


def edge_row(place, halo, taps, sums, own, copies, gain, wide, cols, total):
    count = FRAMES * WIDTH
    tap = pl.multiple_of(place * 2 * C, C)
    by_column(halo[...], wide, cols, 0)
    total[...] = sums[place]
    for side in (0, 2, 1):
        begin, end = max(0, side - 1) * FRAMES, count - max(0, 1 - side) * FRAMES
        shift = (1 - side) * FRAMES
        total[begin + shift : end + shift, :] += dot(cols[begin:end], taps[side, pl.ds(tap, C), :])
    latent = latent_of(total[...], own[place], gain[...], copies[...])
    return in_patch(latent, place)


def outer_scratch():
    return [
        pltpu.VMEM((C // LANES, FRAMES * WIDTH + SPARE, LANES), F32),
        pltpu.VMEM((FRAMES * WIDTH, C), BF),
        pltpu.VMEM((FRAMES * WIDTH, C), F32),
    ]


def outer_even_kernel(halo, taps, sums, own, tokens, copies, gain, parts, *scratch):
    place = 1 - is_odd()
    for patch, value in enumerate(edge_row(place, halo, taps, sums, own, copies, gain, *scratch)):
        parts[patch] = tokens[place * 4 + patch] + value


def outer_even(halo, taps, sums, own, tokens, copies, gain):
    return pl.pallas_call(
        outer_even_kernel,
        out_shape=jax.ShapeDtypeStruct((4, FRAMES, LANES), F32),
        in_specs=[VMEM] * 7,
        out_specs=VMEM,
        scratch_shapes=outer_scratch(),
        compiler_params=pltpu.CompilerParams(vmem_limit_bytes=24 * MIB),
        cost_estimate=pl.CostEstimate(flops=800_000_000, bytes_accessed=4 * MIB, transcendentals=MIB // 4),
        name="outer_even",
    )(halo, taps, sums, own, tokens, copies, gain)


def outer_odd_kernel(halo, taps, sums, own, tokens, copies, gain, parts, placed, folded, message, *scratch):
    *scratch, flat = scratch
    place = is_odd()
    mine = edge_row(place, halo, taps, sums, own, copies, gain, *scratch)
    for patch in range(4):
        mine[patch] = mine[patch] + tokens[place * 4 + patch]
    for index in range(8):
        value = jnp.where(place == index // 4, mine[index % 4], parts[index % 4])
        if index < 2:
            value = value + placed[index]
        flat[pl.ds(index, FRAMES, stride=8), :] = value
    rest = jnp.broadcast_to(folded[...][None], (FRAMES, PART // 2, LANES))
    message[...] = jnp.concatenate([flat[0:TOKENS].reshape(FRAMES, 8, LANES), rest], axis=1).astype(BF)


def outer_odd(halo, taps, sums, own, tokens, copies, gain, parts, placed, folded):
    return pl.pallas_call(
        outer_odd_kernel,
        out_shape=jax.ShapeDtypeStruct((FRAMES, MESSAGE, LANES), BF),
        in_specs=[VMEM] * 10,
        out_specs=VMEM,
        scratch_shapes=outer_scratch() + [pltpu.VMEM((TOKENS + SPARE, LANES), F32)],
        compiler_params=pltpu.CompilerParams(vmem_limit_bytes=24 * MIB),
        cost_estimate=pl.CostEstimate(flops=800_000_000, bytes_accessed=4 * MIB, transcendentals=MIB // 4),
        name="outer_odd",
    )(halo, taps, sums, own, tokens, copies, gain, parts, placed, folded)


def fold_kernel(after, listed, columns, patch, embed, scale, folded, placed, gram, added, table, rows, counts, sem):
    del after
    load = pltpu.make_async_copy(listed, counts, sem)
    load.start()
    table[0:64, :] = patch[...]
    table[64:80, :] = jnp.concatenate(
        [embed[...].astype(F32), jnp.zeros((16 - MAXF, HID), F32)], axis=0
    ).astype(BF)
    high, low = split(table[...].astype(F32) * scale[...])
    rows[0:64, :] = high[:64]
    rows[64:128, :] = low[:64]
    rows[128:144, :] = high[64:]
    rows[144:160, :] = low[64:]
    product = nt(rows[...], columns[...])
    product = jnp.concatenate([product, jnp.zeros((160, LANES - PART), F32)], axis=1)
    both = (product[:64] + product[64:128]).T
    both = jnp.concatenate([both, both], axis=1)
    lane = lax.broadcasted_iota(jnp.int32, (PART // 2, LANES), 1)
    folded[...] = jnp.where(lane < 64, both[: PART // 2], both[PART // 2 : PART])
    offsets = pltpu.roll(product[128:144] + product[144:160], 64, 1)
    product = nt(table[...], table[...])
    matrix = product[:64, :64]
    pieces = []
    for _ in range(3):
        pieces.append(matrix.astype(BF).astype(F32))
        matrix = matrix - pieces[-1]
    pieces = jnp.concatenate([*pieces, jnp.zeros((64, 64), F32)], axis=1)
    gram[...] = jnp.concatenate([pieces, jnp.zeros((64, 256), F32)], axis=0).astype(BF)
    own = lax.axis_index("cp")
    load.wait()
    start, begin = 0, 0
    frame = lax.broadcasted_iota(jnp.int32, (FRAMES, 1), 0)
    begins = jnp.zeros((FRAMES, 1), jnp.int32)
    for clip in range(CLIPS):
        begin = jnp.where(start <= own, start, begin)
        begins = jnp.where(frame >= start, start, begins)
        start = start + counts[clip]
    position = jnp.zeros((FRAMES, LANES), F32)
    for offset in range(MAXF):
        position = position + jnp.where(frame - begins == offset, offsets[offset : offset + 1, :], 0.0)
    high, low = split(position)
    placed[0] = high.astype(F32)
    placed[1] = low.astype(F32)
    line = lax.broadcasted_iota(jnp.int32, (16, 80), 0)
    position = jnp.sum(jnp.where(line == own - begin, product[64:], 0.0), axis=0, keepdims=True)
    lane = lax.broadcasted_iota(jnp.int32, (1, 80), 1)
    square = jnp.sum(jnp.where(lane == 64 + own - begin, position, 0.0), axis=1, keepdims=True)
    added[0:1, :] = jnp.concatenate([2.0 * position[:, :64], jnp.zeros((1, 64), F32)], axis=1)
    added[1:2, :] = jnp.broadcast_to(square, (1, LANES))


def fold(after, counts, columns, patch, embed, scale):
    return pl.pallas_call(
        fold_kernel,
        out_shape=(
            jax.ShapeDtypeStruct((PART // 2, LANES), F32),
            jax.ShapeDtypeStruct((2, FRAMES, LANES), F32),
            jax.ShapeDtypeStruct((LANES, 256), BF),
            jax.ShapeDtypeStruct((2, LANES), F32),
        ),
        in_specs=[VMEM, HBM] + [VMEM] * 4,
        out_specs=(VMEM,) * 4,
        scratch_shapes=[
            pltpu.VMEM((80, HID), BF),
            pltpu.VMEM((160, HID), BF),
            pltpu.SMEM((CLIPS,), jnp.int32),
            pltpu.SemaphoreType.DMA,
        ],
        compiler_params=pltpu.CompilerParams(vmem_limit_bytes=8 * MIB),
        cost_estimate=pl.CostEstimate(flops=1_000_000_000, bytes_accessed=MIB, transcendentals=0),
        name="fold",
    )(after, in_hbm(counts), columns, patch, embed, scale)


GROUP = 4


def project_kernel(arrived, gram, added, spread, out, flat, columns, shift, held, sems):
    got = arrived[...].astype(F32)
    rows = got[:, 0:8].reshape(TOKENS, LANES)
    flat[0:TOKENS] = rows
    lane = lax.broadcasted_iota(jnp.int32, (TOKENS, LANES), 1)
    token = jnp.where(lane < 64, rows, 0.0)
    token = token + pltpu.roll(token, 64, 1)
    query = token.astype(BF)
    product = dot(query, gram[...])
    total = (product[:, :LANES] + product[:, LANES:] + added[0:1, :]) * token
    total = jnp.sum(total, axis=-1, keepdims=True) + added[1:2, 0:1]
    scale = lax.rsqrt(jnp.maximum(total, 0.0) * (1.0 / HID) + EPSILON)
    rest = got[:, 8:MESSAGE]
    lane = lax.broadcasted_iota(jnp.int32, rest.shape, 2)
    low, high = jnp.where(lane < 64, rest, 0.0), jnp.where(lane < 64, 0.0, rest)
    columns[...] = jnp.concatenate([low, high], axis=1).reshape(HID, LANES).astype(BF)
    lane = lax.broadcasted_iota(jnp.int32, (FRAMES, LANES), 1)
    piece = jnp.where(
        lane < 64, pltpu.roll(flat[pl.ds(0, FRAMES, stride=8), :], 64, 1), flat[pl.ds(1, FRAMES, stride=8), :]
    )
    laid = dot(piece.astype(BF), spread[...])
    lane = lax.broadcasted_iota(jnp.int32, (8, 8 * PART), 1)
    line = lax.broadcasted_iota(jnp.int32, (8, 8 * PART), 0) * PART
    mask = (lane >= line) & (lane < line + PART)
    for block in range(8):
        shift[:, block * 8 * PART : (block + 1) * 8 * PART] = jnp.sum(
            jnp.where(mask, laid[block * 8 : (block + 1) * 8], 0.0), axis=0, keepdims=True
        )
    copies = []
    for group in range(HEADS // GROUP):
        at = slice(group * GROUP * HEAD_DIM, (group + 1) * GROUP * HEAD_DIM)
        value = ((nt(query, columns[at, :]) + shift[:, at]) * scale).astype(BF)
        for head in range(GROUP):
            held[group * GROUP + head] = value[:, head * HEAD_DIM : (head + 1) * HEAD_DIM]
        heads = pl.ds(group * GROUP, GROUP)
        copies.append(pltpu.make_async_copy(held.at[heads], out.at[heads], sems.at[group]))
        copies[-1].start()
    for copy in copies:
        copy.wait()


def project(arrived, gram, added, spread):
    return pl.pallas_call(
        project_kernel,
        out_shape=jax.ShapeDtypeStruct((HEADS, TOKENS, HEAD_DIM), BF),
        in_specs=[VMEM] * 4,
        out_specs=HBM,
        scratch_shapes=[
            pltpu.VMEM((TOKENS + SPARE, LANES), F32),
            pltpu.VMEM((HID, LANES), BF),
            pltpu.VMEM((1, HID), F32),
            pltpu.VMEM((HEADS, TOKENS, HEAD_DIM), BF),
            pltpu.SemaphoreType.DMA((HEADS // GROUP,)),
        ],
        compiler_params=pltpu.CompilerParams(vmem_limit_bytes=24 * MIB),
        cost_estimate=pl.CostEstimate(flops=800_000_000, bytes_accessed=5 * MIB, transcendentals=0),
        name="project",
    )(arrived, gram, added, spread)


def spread_table():
    table = np.zeros((LANES, 8 * PART), np.float32)
    lane = np.arange(8 * PART)
    table[lane % PART, lane] = 1.0
    table[64 + lane % PART, lane] = 1.0
    return table


def local(
    frame_rows,
    frame_counts,
    conv_weight,
    norm_gain,
    latent_proj,
    patch_weight,
    frame_embed,
    query_gain,
    query_weight,
):
    devices = lax.axis_size("cp")
    pairs = [[(i, i + 1) for i in range(begin, devices - 1, 2)] for begin in (1, 0)]
    swaps = [pair + [(j, i) for i, j in pair] for pair in pairs]
    odd_rows, even_rows, stage = fetch(frame_counts, frame_rows)
    even_pair = lax.ppermute(even_rows, "cp", swaps[1])
    odd_pair = lax.ppermute(odd_rows, "cp", swaps[0])
    sums, own, tokens, taps, copies, gain = inner(
        stage, conv_weight, latent_proj.T, norm_gain[None, :]
    )
    folded, placed, gram, added = fold(
        gain, frame_counts, query_weight.T, patch_weight, frame_embed, query_gain[None, :]
    )
    parts = outer_even(even_pair, taps, sums, own, tokens, copies, gain)
    message = outer_odd(odd_pair, taps, sums, own, tokens, copies, gain, parts, placed, folded)
    arrived = lax.all_to_all(message, "cp", split_axis=0, concat_axis=0, tiled=True)
    return project(arrived, gram, added, jnp.asarray(spread_table(), BF))


def solution(mesh):
    return jax.shard_map(
        local,
        mesh=mesh,
        in_specs=(P("dp", "cp", None, None), P("dp"), P(), P(), P(), P(), P(), P(), P(None, "cp")),
        out_specs=P(None, ("dp", "cp"), None),
        check_vma=False,
    )
```

```python
import functools

import jax
import jax.numpy as jnp
import numpy as np
from jax import lax
from jax.experimental import pallas as pl
from jax.experimental.pallas import tpu as pltpu
from jax.sharding import PartitionSpec as P

LAT = 16
HID = 3072
HEAD_DIM = 128
HEADS = HID // HEAD_DIM
MAXF = 6
C = 512
WIDTH = 8
STRIP = 4
FRAMES = 64
CLIPS = 16
PART = HID // FRAMES
TOKENS = 512
SPARE = 64
LANES = 128
MESSAGE = 32
EPSILON = 1e-06
BF = jnp.bfloat16
F32 = jnp.float32
VMEM = pl.BlockSpec(memory_space=pltpu.VMEM)
SMEM = pl.BlockSpec(memory_space=pltpu.SMEM)
HBM = pl.BlockSpec(memory_space=pltpu.HBM)
MIB = 1 << 20


def in_hbm(value):
    return pltpu.with_memory_space_constraint(value, pltpu.HBM)


def nt(left, right):
    return lax.dot_general(left, right, (((1,), (1,)), ((), ())), preferred_element_type=F32)


def dot(left, right):
    return jnp.dot(left, right, preferred_element_type=F32)


def split(value):
    high = value.astype(BF)
    return high, (value - high.astype(F32)).astype(BF)


def each_clip(counts, body):
    start = 0
    for clip in range(CLIPS):
        body(clip, start, counts[clip])
        start = start + counts[clip]


def is_odd():
    return lax.rem(lax.axis_index("cp"), 2)


def fetch_kernel(counts, frames, odd_rows, even_rows, stage, sem):
    def clip(at, start, count):
        pltpu.make_async_copy(
            frames.at[pl.ds(at * MAXF, count)], stage.at[pl.ds(start, count)], sem
        ).start()

    each_clip(counts, clip)
    pltpu.make_async_copy(stage, stage, sem).wait()
    row = is_odd() * (STRIP - 1)
    odd_rows[...] = stage[:, row]
    even_rows[...] = stage[:, STRIP - 1 - row]


def fetch(counts, frames):
    return pl.pallas_call(
        fetch_kernel,
        out_shape=(
            pltpu.VMEM((FRAMES, WIDTH, C), BF),
            pltpu.VMEM((FRAMES, WIDTH, C), BF),
            pltpu.VMEM((FRAMES, STRIP, WIDTH, C), BF),
        ),
        in_specs=[SMEM, HBM],
        out_specs=(VMEM,) * 3,
        scratch_shapes=[pltpu.SemaphoreType.DMA],
        cost_estimate=pl.CostEstimate(flops=0, bytes_accessed=4 * MIB, transcendentals=0),
        name="fetch",
    )(in_hbm(counts), in_hbm(frames))


def latent_of(summed, frame, gain, proj):
    half = 0.5 * summed
    residual = frame.astype(F32) + (half + half * jnp.tanh(half))
    mean = jnp.mean(residual * residual, axis=-1, keepdims=True)
    return dot((residual * gain).astype(BF), proj) * lax.rsqrt(mean + EPSILON)


def in_patch(latent, below):
    lane = lax.broadcasted_iota(jnp.int32, (FRAMES, LANES), 1) // LAT
    tokens = []
    for patch in range(WIDTH // 2):
        total = jnp.zeros((FRAMES, LANES), F32)
        for side in range(2):
            column = 2 * patch + side
            block = latent[column * FRAMES : (column + 1) * FRAMES]
            total = total + jnp.where(lane == below * 2 + side, block, 0.0)
        tokens.append(total)
    return tokens


def spread_proj(proj, copies):
    four = jnp.concatenate([proj[...].astype(F32)] * 4 + [jnp.zeros((LANES - 4 * LAT, C), F32)], axis=0)
    copies[...] = four.T.astype(BF)


def by_column(row, wide, cols, lane):
    row = row.astype(F32).reshape(FRAMES * WIDTH, C)
    for piece in range(C // LANES):
        wide[piece, 0 : FRAMES * WIDTH] = row[:, piece * LANES : (piece + 1) * LANES]
    for column in range(WIDTH):
        blocks = [wide[piece, pl.ds(column, FRAMES, stride=WIDTH), :] for piece in range(C // LANES)]
        block = jnp.concatenate(blocks, axis=1).astype(BF)
        cols[column * FRAMES : (column + 1) * FRAMES, lane : lane + C] = block


def inner_kernel(
    stage,
    weight,
    proj,
    gain,
    sums,
    own,
    tokens,
    taps,
    copies,
    norm,
    wide,
    cols,
    total,
    projs,
    small_sems,
    sems,
):
    small = [
        pltpu.make_async_copy(source, target, small_sems.at[place])
        for place, (source, target) in enumerate(((proj, projs), (gain, norm)))
    ]
    order = (1, 0, 2)
    loads = {}
    for side in order:
        for row in (1, 2, 0):
            loads[side, row] = pltpu.make_async_copy(
                weight.at[row, side], taps.at[side, pl.ds(row * C, C)], sems.at[side, row]
            )
            loads[side, row].start()
    for copy in small:
        copy.start()
    for row in range(STRIP):
        by_column(stage[:, row], wide.at[row], cols, row * C)
    for place, row in enumerate((0, STRIP - 1)):
        own[place] = cols[:, row * C : (row + 1) * C]
    count = FRAMES * WIDTH
    for side in order:
        begin, end = max(0, side - 1) * FRAMES, count - max(0, 1 - side) * FRAMES
        shift = (1 - side) * FRAMES
        for row in range(STRIP):
            low, high = max(row - 1, 0), min(row + 2, STRIP)
            for tap in ((1, 2), (0,), (), ())[row]:
                loads[side, tap].wait()
            skip = low - (row - 1)
            part = dot(
                cols[begin:end, low * C : high * C],
                taps[side, skip * C : (skip + high - low) * C, :],
            )
            target = sums.at[row // 2] if row in (0, STRIP - 1) else total.at[row - 1]
            if side == 1:
                target[...] = part
            else:
                target[begin + shift : end + shift, :] += part
    for copy in small:
        copy.wait()
    spread_proj(projs, copies)
    for row in (1, 2):
        latent = latent_of(total[row - 1], cols[:, row * C : (row + 1) * C], norm[...], copies[...])
        for patch_index, value in enumerate(in_patch(latent, row % 2)):
            tokens[(row // 2) * 4 + patch_index] = value


def inner(stage, *operands):
    return pl.pallas_call(
        inner_kernel,
        out_shape=(
            jax.ShapeDtypeStruct((2, FRAMES * WIDTH, C), F32),
            jax.ShapeDtypeStruct((2, FRAMES * WIDTH, C), BF),
            jax.ShapeDtypeStruct((8, FRAMES, LANES), F32),
            jax.ShapeDtypeStruct((3, 3 * C, C), BF),
            jax.ShapeDtypeStruct((C, LANES), BF),
            jax.ShapeDtypeStruct((1, C), F32),
        ),
        in_specs=[VMEM] + [HBM] * 3,
        out_specs=(VMEM,) * 6,
        scratch_shapes=[
            pltpu.VMEM((STRIP, C // LANES, FRAMES * WIDTH + SPARE, LANES), F32),
            pltpu.VMEM((FRAMES * WIDTH, STRIP * C), BF),
            pltpu.VMEM((2, FRAMES * WIDTH, C), F32),
            pltpu.VMEM((LAT, C), BF),
            pltpu.SemaphoreType.DMA((2,)),
            pltpu.SemaphoreType.DMA((3, 3)),
        ],
        compiler_params=pltpu.CompilerParams(vmem_limit_bytes=32 * MIB),
        cost_estimate=pl.CostEstimate(flops=8_000_000_000, bytes_accessed=9 * MIB, transcendentals=MIB // 2),
        name="inner",
    )(stage, *map(in_hbm, operands))


def edge_row(place, halo, taps, sums, own, copies, gain, wide, cols, total):
    count = FRAMES * WIDTH
    tap = pl.multiple_of(place * 2 * C, C)
    by_column(halo[...], wide, cols, 0)
    total[...] = sums[place]
    for side in (0, 2, 1):
        begin, end = max(0, side - 1) * FRAMES, count - max(0, 1 - side) * FRAMES
        shift = (1 - side) * FRAMES
        total[begin + shift : end + shift, :] += dot(cols[begin:end], taps[side, pl.ds(tap, C), :])
    latent = latent_of(total[...], own[place], gain[...], copies[...])
    return in_patch(latent, place)


def outer_scratch():
    return [
        pltpu.VMEM((C // LANES, FRAMES * WIDTH + SPARE, LANES), F32),
        pltpu.VMEM((FRAMES * WIDTH, C), BF),
        pltpu.VMEM((FRAMES * WIDTH, C), F32),
    ]


def outer_even_kernel(halo, taps, sums, own, tokens, copies, gain, placed, parts, *scratch):
    place = 1 - is_odd()
    mine = edge_row(place, halo, taps, sums, own, copies, gain, *scratch)
    for index in range(8):
        value = tokens[index] + jnp.where(place == index // 4, mine[index % 4], 0.0)
        parts[index] = value + placed[index] if index < 2 else value


def outer_even(halo, taps, sums, own, tokens, copies, gain, placed):
    return pl.pallas_call(
        outer_even_kernel,
        out_shape=jax.ShapeDtypeStruct((8, FRAMES, LANES), F32),
        in_specs=[VMEM] * 8,
        out_specs=VMEM,
        scratch_shapes=outer_scratch(),
        compiler_params=pltpu.CompilerParams(vmem_limit_bytes=24 * MIB),
        cost_estimate=pl.CostEstimate(flops=800_000_000, bytes_accessed=4 * MIB, transcendentals=MIB // 4),
        name="outer_even",
    )(halo, taps, sums, own, tokens, copies, gain, placed)


def outer_odd_kernel(halo, taps, sums, own, copies, gain, parts, folded, message, *scratch):
    *scratch, flat = scratch
    place = is_odd()
    mine = edge_row(place, halo, taps, sums, own, copies, gain, *scratch)
    for index in range(8):
        value = parts[index] + jnp.where(place == index // 4, mine[index % 4], 0.0)
        flat[pl.ds(index, FRAMES, stride=8), :] = value
    rest = jnp.broadcast_to(folded[...][None], (FRAMES, PART // 2, LANES))
    message[...] = jnp.concatenate([flat[0:TOKENS].reshape(FRAMES, 8, LANES), rest], axis=1).astype(BF)


def outer_odd(halo, taps, sums, own, copies, gain, parts, folded):
    return pl.pallas_call(
        outer_odd_kernel,
        out_shape=jax.ShapeDtypeStruct((FRAMES, MESSAGE, LANES), BF),
        in_specs=[VMEM] * 8,
        out_specs=VMEM,
        scratch_shapes=outer_scratch() + [pltpu.VMEM((TOKENS + SPARE, LANES), F32)],
        compiler_params=pltpu.CompilerParams(vmem_limit_bytes=24 * MIB),
        cost_estimate=pl.CostEstimate(flops=800_000_000, bytes_accessed=4 * MIB, transcendentals=MIB // 4),
        name="outer_odd",
    )(halo, taps, sums, own, copies, gain, parts, folded)


def fold_kernel(after, listed, columns, patch, embed, scale, folded, placed, gram, added, table, rows, counts, sem):
    del after
    load = pltpu.make_async_copy(listed, counts, sem)
    load.start()
    table[0:64, :] = patch[...]
    table[64:80, :] = jnp.concatenate(
        [embed[...].astype(F32), jnp.zeros((16 - MAXF, HID), F32)], axis=0
    ).astype(BF)
    high, low = split(table[...].astype(F32) * scale[...])
    rows[0:64, :] = high[:64]
    rows[64:128, :] = low[:64]
    rows[128:144, :] = high[64:]
    rows[144:160, :] = low[64:]
    product = nt(rows[...], columns[...])
    product = jnp.concatenate([product, jnp.zeros((160, LANES - PART), F32)], axis=1)
    both = (product[:64] + product[64:128]).T
    both = jnp.concatenate([both, both], axis=1)
    lane = lax.broadcasted_iota(jnp.int32, (PART // 2, LANES), 1)
    folded[...] = jnp.where(lane < 64, both[: PART // 2], both[PART // 2 : PART])
    offsets = pltpu.roll(product[128:144] + product[144:160], 64, 1)
    product = nt(table[...], table[...])
    matrix = product[:64, :64]
    pieces = []
    for _ in range(3):
        pieces.append(matrix.astype(BF).astype(F32))
        matrix = matrix - pieces[-1]
    pieces = jnp.concatenate([*pieces, jnp.zeros((64, 64), F32)], axis=1)
    gram[...] = jnp.concatenate([pieces, jnp.zeros((64, 256), F32)], axis=0).astype(BF)
    own = lax.axis_index("cp")
    load.wait()
    start, begin = 0, 0
    frame = lax.broadcasted_iota(jnp.int32, (FRAMES, 1), 0)
    begins = jnp.zeros((FRAMES, 1), jnp.int32)
    for clip in range(CLIPS):
        begin = jnp.where(start <= own, start, begin)
        begins = jnp.where(frame >= start, start, begins)
        start = start + counts[clip]
    position = jnp.zeros((FRAMES, LANES), F32)
    for offset in range(MAXF):
        position = position + jnp.where(frame - begins == offset, offsets[offset : offset + 1, :], 0.0)
    high, low = split(position)
    placed[0] = high.astype(F32)
    placed[1] = low.astype(F32)
    line = lax.broadcasted_iota(jnp.int32, (16, 80), 0)
    position = jnp.sum(jnp.where(line == own - begin, product[64:], 0.0), axis=0, keepdims=True)
    lane = lax.broadcasted_iota(jnp.int32, (1, 80), 1)
    square = jnp.sum(jnp.where(lane == 64 + own - begin, position, 0.0), axis=1, keepdims=True)
    added[0:1, :] = jnp.concatenate([2.0 * position[:, :64], jnp.zeros((1, 64), F32)], axis=1)
    added[1:2, :] = jnp.broadcast_to(square, (1, LANES))


def fold(after, counts, columns, patch, embed, scale):
    return pl.pallas_call(
        fold_kernel,
        out_shape=(
            jax.ShapeDtypeStruct((PART // 2, LANES), F32),
            jax.ShapeDtypeStruct((2, FRAMES, LANES), F32),
            jax.ShapeDtypeStruct((LANES, 256), BF),
            jax.ShapeDtypeStruct((2, LANES), F32),
        ),
        in_specs=[VMEM, HBM] + [VMEM] * 4,
        out_specs=(VMEM,) * 4,
        scratch_shapes=[
            pltpu.VMEM((80, HID), BF),
            pltpu.VMEM((160, HID), BF),
            pltpu.SMEM((CLIPS,), jnp.int32),
            pltpu.SemaphoreType.DMA,
        ],
        compiler_params=pltpu.CompilerParams(vmem_limit_bytes=8 * MIB),
        cost_estimate=pl.CostEstimate(flops=1_000_000_000, bytes_accessed=MIB, transcendentals=0),
        name="fold",
    )(after, in_hbm(counts), columns, patch, embed, scale)


GROUP = 4


def project_kernel(arrived, gram, added, spread, out, flat, columns, shift, held, sems):
    got = arrived[...].astype(F32)
    rows = got[:, 0:8].reshape(TOKENS, LANES)
    flat[0:TOKENS] = rows
    lane = lax.broadcasted_iota(jnp.int32, (TOKENS, LANES), 1)
    token = jnp.where(lane < 64, rows, 0.0)
    token = token + pltpu.roll(token, 64, 1)
    query = token.astype(BF)
    product = dot(query, gram[...])
    total = (product[:, :LANES] + product[:, LANES:] + added[0:1, :]) * token
    total = jnp.sum(total, axis=-1, keepdims=True) + added[1:2, 0:1]
    scale = lax.rsqrt(jnp.maximum(total, 0.0) * (1.0 / HID) + EPSILON)
    rest = got[:, 8:MESSAGE]
    lane = lax.broadcasted_iota(jnp.int32, rest.shape, 2)
    low, high = jnp.where(lane < 64, rest, 0.0), jnp.where(lane < 64, 0.0, rest)
    columns[...] = jnp.concatenate([low, high], axis=1).reshape(HID, LANES).astype(BF)
    lane = lax.broadcasted_iota(jnp.int32, (FRAMES, LANES), 1)
    piece = jnp.where(
        lane < 64, pltpu.roll(flat[pl.ds(0, FRAMES, stride=8), :], 64, 1), flat[pl.ds(1, FRAMES, stride=8), :]
    )
    laid = dot(piece.astype(BF), spread[...])
    lane = lax.broadcasted_iota(jnp.int32, (8, 8 * PART), 1)
    line = lax.broadcasted_iota(jnp.int32, (8, 8 * PART), 0) * PART
    mask = (lane >= line) & (lane < line + PART)
    for block in range(8):
        shift[:, block * 8 * PART : (block + 1) * 8 * PART] = jnp.sum(
            jnp.where(mask, laid[block * 8 : (block + 1) * 8], 0.0), axis=0, keepdims=True
        )
    copies = []
    for group in range(HEADS // GROUP):
        at = slice(group * GROUP * HEAD_DIM, (group + 1) * GROUP * HEAD_DIM)
        value = ((nt(query, columns[at, :]) + shift[:, at]) * scale).astype(BF)
        for head in range(GROUP):
            held[group * GROUP + head] = value[:, head * HEAD_DIM : (head + 1) * HEAD_DIM]
        heads = pl.ds(group * GROUP, GROUP)
        copies.append(pltpu.make_async_copy(held.at[heads], out.at[heads], sems.at[group]))
        copies[-1].start()
    for copy in copies:
        copy.wait()


def project(arrived, gram, added, spread):
    return pl.pallas_call(
        project_kernel,
        out_shape=jax.ShapeDtypeStruct((HEADS, TOKENS, HEAD_DIM), BF),
        in_specs=[VMEM] * 4,
        out_specs=HBM,
        scratch_shapes=[
            pltpu.VMEM((TOKENS + SPARE, LANES), F32),
            pltpu.VMEM((HID, LANES), BF),
            pltpu.VMEM((1, HID), F32),
            pltpu.VMEM((HEADS, TOKENS, HEAD_DIM), BF),
            pltpu.SemaphoreType.DMA((HEADS // GROUP,)),
        ],
        compiler_params=pltpu.CompilerParams(vmem_limit_bytes=24 * MIB),
        cost_estimate=pl.CostEstimate(flops=800_000_000, bytes_accessed=5 * MIB, transcendentals=0),
        name="project",
    )(arrived, gram, added, spread)


def spread_table():
    table = np.zeros((LANES, 8 * PART), np.float32)
    lane = np.arange(8 * PART)
    table[lane % PART, lane] = 1.0
    table[64 + lane % PART, lane] = 1.0
    return table


def local(
    frame_rows,
    frame_counts,
    conv_weight,
    norm_gain,
    latent_proj,
    patch_weight,
    frame_embed,
    query_gain,
    query_weight,
):
    devices = lax.axis_size("cp")
    pairs = [[(i, i + 1) for i in range(begin, devices - 1, 2)] for begin in (1, 0)]
    swaps = [pair + [(j, i) for i, j in pair] for pair in pairs]
    odd_rows, even_rows, stage = fetch(frame_counts, frame_rows)
    even_pair = lax.ppermute(even_rows, "cp", swaps[1])
    odd_pair = lax.ppermute(odd_rows, "cp", swaps[0])
    sums, own, tokens, taps, copies, gain = inner(
        stage, conv_weight, latent_proj.T, norm_gain[None, :]
    )
    folded, placed, gram, added = fold(
        gain, frame_counts, query_weight.T, patch_weight, frame_embed, query_gain[None, :]
    )
    parts = outer_even(even_pair, taps, sums, own, tokens, copies, gain, placed)
    message = outer_odd(odd_pair, taps, sums, own, copies, gain, parts, folded)
    arrived = lax.all_to_all(message, "cp", split_axis=0, concat_axis=0, tiled=True)
    return project(arrived, gram, added, jnp.asarray(spread_table(), BF))


def solution(mesh):
    return jax.shard_map(
        local,
        mesh=mesh,
        in_specs=(P("dp", "cp", None, None), P("dp"), P(), P(), P(), P(), P(), P(), P(None, "cp")),
        out_specs=P(None, ("dp", "cp"), None),
        check_vma=False,
    )
```
